512 devices in a mesh: row: 32 (over x, y_lo, core), col: 16 (over y_hi, z).
Axes of the slice: x: 4, y: 8 (y_hi: 2, y_lo: 4; y = y_hi * 4 + y_lo), z: 8, core: 2. Of those that a mesh axis runs over, the one named last changes fastest.
Arguments:
- tokens: bfloat16 [1024, 6144], P('row', 'col'), may hold values from -6 to 6
- grad_out: bfloat16 [1024, 6144], P('row', 'col'), may hold values from -6 to 6
- gate_pre: bfloat16 [1024, 24576], P('col', 'row'), may hold values from -8 to 8
- up_pre: bfloat16 [1024, 24576], P('col', 'row'), may hold values from -6 to 6
- w_gate: bfloat16 [6144, 24576], P('col', 'row'), may hold values from -0.078125 to 0.078125
- w_up: bfloat16 [6144, 24576], P('col', 'row'), may hold values from -0.078125 to 0.078125
- w_down: bfloat16 [24576, 6144], P('row', 'col'), may hold values from -0.0390625 to 0.0390625
Outputs:
- grad_tokens: bfloat16 [1024, 6144], P('row', 'col')
- grad_gate: bfloat16 [6144, 24576], P('col', 'row')
- grad_up: bfloat16 [6144, 24576], P('col', 'row')
- grad_down: bfloat16 [24576, 6144], P('row', 'col')
The draws below stay inside these ranges and needn't reach their ends.
All inputs are finite; a program needn't handle non-finite values.
Results may differ from the reference program's by a relative error of at most 0.0049.
Values may be sent and summed in bfloat16 or wider, within the bound.
A program may use at most 64 MiB of HBM per device.

```python
import jax
import jax.numpy as jnp
from jax import lax

D = 6144
FF = 24576
TOKENS = 1024


def steps_of(stream_key, dims, cuts, smallest, high):
    def one(axis_at, parts):
        heights = jax.random.uniform(jax.random.fold_in(jax.random.fold_in(stream_key, 6), axis_at), (parts,), jnp.float32, smallest / len(cuts), high / len(cuts))
        return jnp.repeat(jnp.exp(heights), dims[axis_at] // parts).reshape((-1,) + (1,) * (len(dims) - axis_at - 1))

    loudness = one(*cuts[0])
    for cut in cuts[1:]:
        loudness = loudness * one(*cut)
    return loudness


def centred(own_key, shape, spread, most, shards=(), held_as=jnp.bfloat16):
    level = steps_of(own_key, shape, shards, -0.22, 0.18) if shards else 1.0
    array = jax.random.normal(own_key, shape, jnp.float32) * spread * level
    return jnp.minimum(jnp.maximum(array, -most), most).astype(held_as)


def setup_inputs(seed: int = 0) -> dict:
    splits = jax.random.split(jax.random.key(seed), 8)
    return {
        "tokens": centred(splits[0], (TOKENS, D), 1.0, 6.0, ((0, 32), (1, 16))),
        "grad_out": centred(splits[1], (TOKENS, D), 1.0, 6.0, ((0, 32), (1, 16))),
        "gate_pre": centred(splits[2], (TOKENS, FF), 1.5, 8.0, ((0, 16), (1, 32))),
        "up_pre": centred(splits[3], (TOKENS, FF), 1.0, 6.0, ((0, 16), (1, 32))),
        "w_gate": centred(splits[4], (D, FF), D ** -0.5, 0.078125, ((0, 16), (1, 32))),
        "w_up": centred(splits[5], (D, FF), D ** -0.5, 0.078125, ((0, 16), (1, 32))),
        "w_down": centred(splits[6], (FF, D), FF ** -0.5, 0.0390625, ((0, 32), (1, 16))),
    }


def swiglu_backward(grad_hidden, gate_pre, up_pre):
    gate_value = gate_pre.astype(jnp.float32)
    up_value = up_pre.astype(jnp.float32)
    sigmoid_gate = jax.nn.sigmoid(gate_value)
    silu_gate = gate_value * sigmoid_gate
    hidden = (silu_gate * up_value).astype(jnp.bfloat16)
    grad_up = (grad_hidden * silu_gate).astype(jnp.bfloat16)
    grad_gate = (grad_hidden * up_value * sigmoid_gate * (1.0 + gate_value * (1.0 - sigmoid_gate))).astype(jnp.bfloat16)
    return hidden, grad_gate, grad_up


def contract(left_side, right_side, left_dim, right_dim):
    return lax.dot_general(left_side, right_side, (((left_dim,), (right_dim,)), ((), ())), preferred_element_type=jnp.float32)


def reference(tokens, grad_out, gate_pre, up_pre, w_gate, w_up, w_down):
    grad_hidden = contract(grad_out, w_down, 1, 1)
    hidden, gate_grad, up_grad = swiglu_backward(grad_hidden, gate_pre, up_pre)
    grad_down = contract(hidden, grad_out, 0, 0).astype(jnp.bfloat16)
    grad_gate = contract(tokens, gate_grad, 0, 0).astype(jnp.bfloat16)
    grad_up = contract(tokens, up_grad, 0, 0).astype(jnp.bfloat16)
    grad_tokens = (contract(gate_grad, w_gate, 1, 1) + contract(up_grad, w_up, 1, 1)).astype(jnp.bfloat16)
    return (grad_tokens, grad_gate, grad_up, grad_down)
```

```python
import functools

import jax
import jax.numpy as jnp
from jax import lax
from jax.experimental import pallas as pl
from jax.experimental.pallas import tpu as pltpu
from jax.sharding import PartitionSpec as P

MESH = pl.DeviceIdType.MESH
F32 = jnp.float32
BF16 = jnp.bfloat16
NX, NY, NC = 4, 4, 2
NH, NZ = 2, 8
ROWS = 16
COPIES = 110


def dot(left, right, left_dim, right_dim):
    return lax.dot_general(
        left, right, (((left_dim,), (right_dim,)), ((), ())), preferred_element_type=F32
    )


def kernel(
    tok_ref, go_ref, gate_ref, up_ref, wg_ref, wu_ref, wd_ref,
    out_gt, out_gg, out_gu, out_gd,
    tok_all, go_all, acts, wg, wu, wd, part, rs_send, rs_recv, swap_send, swap_recv,
    grad_h, silu, slope, hidden, gate_grad, up_grad, tok_t, pair_sum, core_send, core_recv,
    x_send, x_recv, x_own, y_send, y_recv, st_gg, st_gu, st_gd,
    send, recv, core_send_sem, core_recv_sem, x_send_sem, x_recv_sem, here,
):
    row, col = lax.axis_index("row"), lax.axis_index("col")
    x, yl, core = row // (NY * NC), (row // NC) % NY, row % NC
    yh, z = col // NZ, col % NZ
    tb, half = acts.shape[3], acts.shape[3] // 2

    def at_row(px, py, pc):
        return (px * (NY * NC) + py * NC + pc, col)

    def at_col(ph, pz):
        return (row, ph * NZ + pz)

    xs = [at_row((x + d) % NX, yl, core) for d in range(1, NX)]
    ys = [at_row(x, (yl + d) % NY, core) for d in range(1, NY)]
    sibling = at_row(x, yl, 1 - core)
    ahead, behind = at_col(yh, (z + 1) % NZ), at_col(yh, (z + NZ - 1) % NZ)
    across = at_col(1 - yh, z)

    sent = []

    def push(src, dst, to):
        n = len(sent)
        copy = pltpu.make_async_remote_copy(
            src_ref=src, dst_ref=dst, send_sem=send.at[n], recv_sem=recv.at[n],
            device_id=to, device_id_type=MESH,
        )
        copy.start()
        sent.append(copy)
        return copy

    def landed(copies):
        for copy in copies:
            copy.wait_recv()

    mine = x * NY + yl
    loads = [
        (go_ref, go_all.at[mine, core]), (tok_ref, tok_all.at[mine, core]),
        (gate_ref, acts.at[0, yh, z]), (up_ref, acts.at[1, yh, z]),
        (wd_ref, wd), (wg_ref, wg), (wu_ref, wu),
    ]
    loads = [pltpu.make_async_copy(s, d, here.at[i]) for i, (s, d) in enumerate(loads)]
    for load in loads:
        load.start()

    barrier = pltpu.get_barrier_semaphore()
    partners = xs + ys + [sibling, ahead, behind, across]
    for to in partners:
        pl.semaphore_signal(barrier, inc=1, device_id=to, device_id_type=MESH)
    pl.semaphore_wait(barrier, len(partners))

    def ring_send(block, step, first=None):
        copies = []
        for k in range(2):
            for way, to in ((1, ahead), (-1, behind)):
                at = (z + (NZ - way * (step - 1))) % NZ
                src = block(k, at) if first is None else first[k]
                dst = block(k, at)
                if step == NZ // 2:
                    rows = pl.ds(0 if way == 1 else half, half)
                    src, dst = src.at[rows], dst.at[rows]
                copies.append(push(src, dst, to))
        return copies

    def ring_pass(block, step, before):
        copies = []
        for k in range(2):
            for w, (way, to) in enumerate(((1, ahead), (-1, behind))):
                before[2 * k + w].wait_recv()
                at = (z + (NZ - way * (step - 1))) % NZ
                ref = block(k, at)
                if step == NZ // 2:
                    ref = ref.at[pl.ds(0 if way == 1 else half, half)]
                copies.append(push(ref, ref, to))
        return copies

    def own_act(k, at):
        return acts.at[k, yh, at]

    def other_act(k, at):
        return acts.at[k, 1 - yh, at]

    def grad_block(k, at):
        return grad_h.at[k, at]

    def pair_loop(m, step):
        if m in (0, NZ // 2):
            step(m)
        else:
            pl.loop(0, 2)(lambda i: step(m + (NZ - 2 * m) * i))

    def activate(h, m):
        def step(o):
            at = (z + o) % NZ

            @pl.loop(0, tb // ROWS)
            def _(i):
                rows = pl.ds(pl.multiple_of(i * ROWS, ROWS), ROWS)
                g = acts[0, h, at, rows].astype(F32)
                u = acts[1, h, at, rows].astype(F32)
                s = jax.nn.sigmoid(g)
                gs = g * s
                silu[h, at, rows] = gs
                slope[h, at, rows] = u * s * (1.0 + g * (1.0 - s))
                hidden[h, at, rows] = (gs * u).astype(BF16)

        pair_loop(m, step)

    def share(m):
        def step(o):
            at = (z + o) % NZ
            rows = jnp.concatenate(
                [go_all[h * NZ + at].reshape(tb, -1) for h in range(NH)], axis=0
            )
            sums = dot(rows, wd[...], 1, 1)
            for h in range(NH):
                part[h, at] = sums[h * tb : (h + 1) * tb]

        pair_loop(m, step)

    def reduce_step(step, before):
        copies = []
        for h in range(NH):
            for w, (way, to) in enumerate(((1, ahead), (-1, behind))):
                at = (z + (NZ + way * (NZ // 2 + 1 - step))) % NZ
                out = rs_send.at[h, w, step - 1]
                rows = pl.ds(0 if way == 1 else half, half)
                if step == 1:
                    out[rows] = part[h, at, rows].astype(BF16)
                    copies.append(push(out.at[rows], rs_recv.at[h, w, 0, rows], to))
                    continue
                before[2 * h + w].wait_recv()
                if step == 2:
                    rest = pl.ds(half if way == 1 else 0, half)
                    out[rows] = (part[h, at, rows] + rs_recv[h, w, 0, rows].astype(F32)).astype(BF16)
                    out[rest] = part[h, at, rest].astype(BF16)
                else:
                    out[...] = (part[h, at] + rs_recv[h, w, step - 2].astype(F32)).astype(BF16)
                copies.append(push(out, rs_recv.at[h, w, step - 1], to))
        return copies

    def spread(own, copies_of, source):
        return [push(source, own, to) for to in copies_of]

    act1 = ring_send(own_act, 1, first=(gate_ref, up_ref))
    go_y = spread(go_all.at[mine, core], ys, go_ref)
    tok_y = spread(tok_all.at[mine, core], ys, tok_ref)

    def x_line(ref):
        return ref.at[pl.ds(x * NY, NY), core]

    loads[0].wait()
    landed(go_y)
    go_x = spread(x_line(go_all), xs, x_line(go_all))
    act1 = ring_pass(own_act, 2, act1)
    loads[1].wait()
    landed(tok_y)
    tok_x = spread(x_line(tok_all), xs, x_line(tok_all))
    act_y = [push(ref, acts.at[k, yh, z], across) for k, ref in enumerate((gate_ref, up_ref))]
    act1 = ring_pass(own_act, 3, act1)
    landed(go_x)
    go_c = push(go_all.at[:, core], go_all.at[:, core], sibling)
    act1 = ring_pass(own_act, 4, act1)
    loads[4].wait()
    go_c.wait_recv()

    share(4)
    sums = reduce_step(1, None)
    share(3)
    landed(tok_x)
    tok_c = push(tok_all.at[:, core], tok_all.at[:, core], sibling)
    sums = reduce_step(2, sums)
    share(2)
    loads[2].wait()
    loads[3].wait()
    activate(yh, 0)
    activate(yh, 1)
    sums = reduce_step(3, sums)
    share(1)
    share(0)
    activate(yh, 2)
    sums = reduce_step(4, sums)
    landed(act1)
    landed(act_y)
    act2 = ring_send(other_act, 1)
    activate(yh, 3)
    activate(yh, 4)

    swaps = []
    for h in range(NH):
        landed(sums[2 * h : 2 * h + 2])
        total = part[h, z] + rs_recv[h, 0, 3].astype(F32) + rs_recv[h, 1, 3].astype(F32)
        part[h, z] = total
        swap_send[h] = total.astype(BF16)
        swaps.append(push(swap_send.at[h], swap_recv.at[h], across))
    tok_c.wait_recv()
    tok_t[...] = tok_all[...].reshape(-1, tok_all.shape[3]).T
    act2 = ring_pass(other_act, 2, act2)
    activate(1 - yh, 0)
    for h in range(NH):
        swaps[h].wait_recv()
        grad_h[h, z] = (part[h, z] + swap_recv[h].astype(F32)).astype(BF16)
    grads = ring_send(grad_block, 1)
    act2 = ring_pass(other_act, 3, act2)
    activate(1 - yh, 1)
    loads[5].wait()
    loads[6].wait()

    def gradients(m):
        def step(o):
            at = (z + o) % NZ
            for h in range(NH):

                @pl.loop(0, tb // ROWS)
                def _(i):
                    rows = pl.ds(pl.multiple_of(i * ROWS, ROWS), ROWS)
                    gh = grad_h[h, at, rows].astype(F32)
                    gate_grad[h, at, rows] = (gh * slope[h, at, rows]).astype(BF16)
                    up_grad[h, at, rows] = (gh * silu[h, at, rows]).astype(BF16)

            sums = dot(gate_grad[:, at].reshape(NH * tb, -1), wg[...], 1, 1)
            sums += dot(up_grad[:, at].reshape(NH * tb, -1), wu[...], 1, 1)
            pair_sum[o] = sums.reshape(pair_sum.shape[1:])
            core_send[o] = pair_sum[o, :, 1 - core]
            core_copy(o).start()

        pair_loop(m, step)

    def core_copy(o):
        return pltpu.make_async_remote_copy(
            src_ref=core_send.at[o], dst_ref=core_recv.at[o], send_sem=core_send_sem.at[o],
            recv_sem=core_recv_sem.at[o], device_id=sibling, device_id_type=MESH,
        )

    def x_copy(o, h, to_x, to_y):
        return pltpu.make_async_remote_copy(
            src_ref=x_send.at[o, h], dst_ref=x_recv.at[x, to_y], send_sem=x_send_sem.at[o, h],
            recv_sem=x_recv_sem.at[to_y, x], device_id=at_row(to_x, yl, core), device_id_type=MESH,
        )

    def target(o, h):
        at = h * NZ + (z + o) % NZ
        return at // NY, at % NY

    def outward(m):
        def step(o):
            core_copy(o).wait_recv()
            for h in range(NH):
                to_x, to_y = target(o, h)
                x_send[o, h] = pair_sum[o, h, core] + core_recv[o, h]

                @pl.when(to_x == x)
                def _():
                    x_own[to_y] = x_send[o, h]

                @pl.when(to_x != x)
                def _():
                    x_copy(o, h, to_x, to_y).start()

        pair_loop(m, step)

    grads = ring_pass(grad_block, 2, grads)
    gradients(0)
    act2 = ring_pass(other_act, 4, act2)
    activate(1 - yh, 2)
    gradients(1)
    grads = ring_pass(grad_block, 3, grads)
    activate(1 - yh, 3)
    outward(0)
    outward(1)
    gradients(2)
    landed(act2)
    activate(1 - yh, 4)
    grads = ring_pass(grad_block, 4, grads)
    outward(2)
    gradients(3)
    go_flat = go_all[...].reshape(-1, go_all.shape[3])
    width = 256
    for n in range(hidden.shape[3] // width):
        cols = pl.ds(n * width, width)
        st_gd[cols] = dot(hidden[..., cols].reshape(-1, width), go_flat, 0, 0).astype(BF16)
    stores = [pltpu.make_async_copy(st_gd, out_gd, here.at[7])]
    stores[0].start()
    outward(3)
    landed(grads)
    gradients(4)
    for i, (grad, stage, out) in enumerate(((gate_grad, st_gg, out_gg), (up_grad, st_gu, out_gu))):
        for n in range(grad.shape[3] // width):
            cols = pl.ds(n * width, width)
            if i == 0 and n == 1:
                outward(4)
            stage[:, cols] = dot(tok_t[...], grad[..., cols].reshape(-1, width), 1, 0).astype(BF16)
        stores.append(pltpu.make_async_copy(stage, out, here.at[8 + i]))
        stores[-1].start()

    def line_sum(to_y):
        total = x_own[to_y]
        for d in range(1, NX):
            src = (x + d) % NX
            pltpu.make_async_remote_copy(
                src_ref=x_send.at[0, 0], dst_ref=x_recv.at[src, to_y], send_sem=x_send_sem.at[0, 0],
                recv_sem=x_recv_sem.at[to_y, src], device_id=sibling, device_id_type=MESH,
            ).wait_recv()
            total = total + x_recv[src, to_y]
        return total

    last = []
    for d in range(1, NY):
        y_send[d - 1] = line_sum((yl + d) % NY)
        last.append(push(y_send.at[d - 1], y_recv.at[d - 1], ys[d - 1]))
    total = line_sum(yl)
    for d in range(1, NY):
        last[d - 1].wait_recv()
        total = total + y_recv[d - 1]
    out_gt[...] = total.astype(BF16)

    for copy in sent:
        copy.wait_send()

    @pl.loop(0, NZ)
    def _(o):
        core_copy(o).wait_send()
        for h in range(NH):
            to_x, to_y = target(o, h)

            @pl.when(to_x != x)
            def _():
                x_copy(o, h, to_x, to_y).wait_send()

    for store in stores:
        store.wait()


def on_device(tokens, grad_out, gate_pre, up_pre, w_gate, w_up, w_down):
    th, dd = tokens.shape
    tb, ff = gate_pre.shape
    nrow, ncol = NX * NY, NH * NZ
    anywhere = pl.BlockSpec(memory_space=pl.ANY)
    vmem = pltpu.VMEM
    dma = pltpu.SemaphoreType.DMA
    out = [
        jax.ShapeDtypeStruct(tokens.shape, BF16),
        jax.ShapeDtypeStruct(w_gate.shape, BF16),
        jax.ShapeDtypeStruct(w_up.shape, BF16),
        jax.ShapeDtypeStruct(w_down.shape, BF16),
    ]
    every = (NH, NZ, tb, ff)
    scratch = [
        vmem((nrow, NC, th, dd), BF16),
        vmem((nrow, NC, th, dd), BF16),
        vmem((2,) + every, BF16),
        vmem((dd, ff), BF16),
        vmem((dd, ff), BF16),
        vmem((ff, dd), BF16),
        vmem(every, F32),
        vmem((NH, 2, 4, tb, ff), BF16),
        vmem((NH, 2, 4, tb, ff), BF16),
        vmem((NH, tb, ff), BF16),
        vmem((NH, tb, ff), BF16),
        vmem(every, BF16),
        vmem(every, F32),
        vmem(every, F32),
        vmem(every, BF16),
        vmem(every, BF16),
        vmem(every, BF16),
        vmem((dd, ncol * tb), BF16),
        vmem((NZ, NH, NC, th, dd), F32),
        vmem((NZ, NH, th, dd), F32),
        vmem((NZ, NH, th, dd), F32),
        vmem((NZ, NH, th, dd), F32),
        vmem((NX, NY, th, dd), F32),
        vmem((NY, th, dd), F32),
        vmem((NY - 1, th, dd), F32),
        vmem((NY - 1, th, dd), F32),
        vmem((dd, ff), BF16),
        vmem((dd, ff), BF16),
        vmem((ff, dd), BF16),
        dma((COPIES,)),
        dma((COPIES,)),
        dma((NZ,)),
        dma((NZ,)),
        dma((NZ, NH)),
        dma((NY, NX)),
        dma((10,)),
    ]
    return tuple(
        pl.pallas_call(
            kernel,
            out_shape=out,
            in_specs=[anywhere] * 7,
            out_specs=[pl.BlockSpec(memory_space=vmem)] + [anywhere] * 3,
            scratch_shapes=scratch,
            compiler_params=pltpu.CompilerParams(
                collective_id=0, has_side_effects=True, vmem_limit_bytes=56 * 2**20
            ),
            cost_estimate=pl.CostEstimate(
                flops=12 * nrow * NC * th * dd * ff, bytes_accessed=8 * dd * ff * 2, transcendentals=ncol * tb * ff
            ),
        )(tokens, grad_out, gate_pre, up_pre, w_gate, w_up, w_down)
    )


def solution(mesh):
    return jax.shard_map(
        on_device,
        mesh=mesh,
        in_specs=(
            P("row", "col"),
            P("row", "col"),
            P("col", "row"),
            P("col", "row"),
            P("col", "row"),
            P("col", "row"),
            P("row", "col"),
        ),
        out_specs=(P("row", "col"), P("col", "row"), P("col", "row"), P("row", "col")),
        check_vma=False,
    )
```

```python
import functools

import jax
import jax.numpy as jnp
from jax import lax
from jax.experimental import pallas as pl
from jax.experimental.pallas import tpu as pltpu
from jax.sharding import PartitionSpec as P

MESH = pl.DeviceIdType.MESH
F32 = jnp.float32
BF16 = jnp.bfloat16
NX, NY, NC = 4, 4, 2
NH, NZ = 2, 8
ROWS = 32
COPIES = 94


def dot(left, right, left_dim, right_dim):
    return lax.dot_general(
        left, right, (((left_dim,), (right_dim,)), ((), ())), preferred_element_type=F32
    )


def kernel(
    tok_ref, go_ref, gate_ref, up_ref, wg_ref, wu_ref, wd_ref,
    out_gt, out_gg, out_gu, out_gd,
    tok_all, go_all, acts, wg, wu, wd, part, rs_send, rs_recv, swap_send, swap_recv,
    grad_h, silu, slope, hidden, gate_grad, up_grad, tok_t, pair_sum, core_send, core_recv,
    x_send, x_recv, x_own, y_send, y_recv, st_gg, st_gu, st_gd,
    send, recv, core_send_sem, core_recv_sem, x_send_sem, x_recv_sem, y_send_sem, y_recv_sem, here,
):
    row, col = lax.axis_index("row"), lax.axis_index("col")
    x, yl, core = row // (NY * NC), (row // NC) % NY, row % NC
    yh, z = col // NZ, col % NZ
    tb, half = acts.shape[3], acts.shape[3] // 2

    def at_row(px, py, pc):
        return (px * (NY * NC) + py * NC + pc, col)

    def at_col(ph, pz):
        return (row, ph * NZ + pz)

    xs = [at_row((x + d) % NX, yl, core) for d in range(1, NX)]
    ys = [at_row(x, (yl + d) % NY, core) for d in range(1, NY)]
    sibling = at_row(x, yl, 1 - core)
    ahead, behind = at_col(yh, (z + 1) % NZ), at_col(yh, (z + NZ - 1) % NZ)
    across = at_col(1 - yh, z)

    sent = []

    def push(src, dst, to):
        n = len(sent)
        copy = pltpu.make_async_remote_copy(
            src_ref=src, dst_ref=dst, send_sem=send.at[n], recv_sem=recv.at[n],
            device_id=to, device_id_type=MESH,
        )
        copy.start()
        sent.append(copy)
        return copy

    def landed(copies):
        for copy in copies:
            copy.wait_recv()

    mine = x * NY + yl
    loads = [
        (go_ref, go_all.at[mine, core]), (tok_ref, tok_all.at[mine, core]),
        (gate_ref, acts.at[0, yh, z]), (up_ref, acts.at[1, yh, z]),
        (wd_ref, wd), (wg_ref, wg), (wu_ref, wu),
    ]
    loads = [pltpu.make_async_copy(s, d, here.at[i]) for i, (s, d) in enumerate(loads)]
    for load in loads:
        load.start()

    barrier = pltpu.get_barrier_semaphore()
    partners = xs + ys + [sibling, ahead, behind, across]
    for to in partners:
        pl.semaphore_signal(barrier, inc=1, device_id=to, device_id_type=MESH)
    pl.semaphore_wait(barrier, len(partners))

    def ring_send(block, k, step, first=None):
        copies = []
        for way, to in ((1, ahead), (-1, behind)):
            at = (z + (NZ - way * (step - 1))) % NZ
            ref = block(k, at)
            if step == NZ // 2:
                ref = ref.at[pl.ds(0 if way == 1 else half, half)]
            copies.append(push(ref if first is None else first, ref, to))
        return copies

    def ring_pass(block, k, step, before):
        landed(before)
        return ring_send(block, k, step)

    def both_pass(block, step, before):
        return [ring_pass(block, k, step, before[k]) for k in range(2)]

    def own_act(k, at):
        return acts.at[k, yh, at]

    def other_act(k, at):
        return acts.at[k, 1 - yh, at]

    def grad_block(k, at):
        return grad_h.at[k, at]

    def pair_loop(m, step):
        if m in (0, NZ // 2):
            step(m)
        else:
            pl.loop(0, 2)(lambda i: step(m + (NZ - 2 * m) * i))

    def activate(h, m):
        def step(o):
            at = (z + o) % NZ

            @pl.loop(0, tb // ROWS)
            def _(i):
                rows = pl.ds(pl.multiple_of(i * ROWS, ROWS), ROWS)
                g = acts[0, h, at, rows].astype(F32)
                u = acts[1, h, at, rows].astype(F32)
                s = jax.nn.sigmoid(g)
                gs = g * s
                silu[h, at, rows] = gs
                slope[h, at, rows] = u * s * (1.0 + g * (1.0 - s))
                hidden[h, at, rows] = (gs * u).astype(BF16)

        pair_loop(m, step)

    def share(m):
        def step(o):
            at = (z + o) % NZ
            rows = jnp.concatenate(
                [go_all[h * NZ + at].reshape(tb, -1) for h in range(NH)], axis=0
            )
            sums = dot(rows, wd[...], 1, 1)
            for h in range(NH):
                part[h, at] = sums[h * tb : (h + 1) * tb]

        pair_loop(m, step)

    def reduce_step(step, before):
        copies = []
        for h in range(NH):
            for w, (way, to) in enumerate(((1, ahead), (-1, behind))):
                at = (z + (NZ + way * (NZ // 2 + 1 - step))) % NZ
                out = rs_send.at[h, w, step - 1]
                rows = pl.ds(0 if way == 1 else half, half)
                if step == 1:
                    out[rows] = part[h, at, rows].astype(BF16)
                    copies.append(push(out.at[rows], rs_recv.at[h, w, 0, rows], to))
                    continue
                before[2 * h + w].wait_recv()
                if step == 2:
                    rest = pl.ds(half if way == 1 else 0, half)
                    out[rows] = (part[h, at, rows] + rs_recv[h, w, 0, rows].astype(F32)).astype(BF16)
                    out[rest] = part[h, at, rest].astype(BF16)
                else:
                    out[...] = (part[h, at] + rs_recv[h, w, step - 2].astype(F32)).astype(BF16)
                copies.append(push(out, rs_recv.at[h, w, step - 1], to))
        return copies

    def spread(own, copies_of, source):
        return [push(source, own, to) for to in copies_of]

    def x_line(ref, px):
        return ref.at[pl.ds(px * NY, NY), core]

    go_own = go_all.at[mine, core]
    go_y = spread(go_own, ys, go_ref)
    go_x = [spread(go_own, xs, go_ref)]
    act1 = [ring_send(own_act, k, 1, first=ref) for k, ref in enumerate((gate_ref, up_ref))]
    tok_y = spread(tok_all.at[mine, core], ys, tok_ref)
    for d in range(1, NY):
        go_y[d - 1].wait_recv()
        block = go_all.at[x * NY + (yl + NY - d) % NY, core]
        go_x.append(spread(block, xs, block))
    act_y = [push(ref, acts.at[k, yh, z], across) for k, ref in enumerate((gate_ref, up_ref))]
    loads[0].wait()
    go_c = [push(x_line(go_all, x), x_line(go_all, x), sibling)]
    loads[2].wait()
    loads[3].wait()
    activate(yh, 0)
    act1 = both_pass(own_act, 2, act1)
    activate(yh, 1)
    loads[1].wait()
    landed(tok_y)
    for d in (1, 3, 2):
        landed([copies[d - 1] for copies in go_x])
        line = x_line(go_all, (x + NX - d) % NX)
        go_c.append(push(line, line, sibling))
    tok_x = spread(x_line(tok_all, x), xs, x_line(tok_all, x))
    act1 = both_pass(own_act, 3, act1)
    loads[4].wait()
    landed(go_c)

    share(4)
    sums = reduce_step(1, None)
    share(3)
    act1 = both_pass(own_act, 4, act1)
    sums = reduce_step(2, sums)
    share(2)
    landed(tok_x)
    tok_c = push(tok_all.at[:, core], tok_all.at[:, core], sibling)
    activate(yh, 2)
    sums = reduce_step(3, sums)
    share(1)
    share(0)
    sums = reduce_step(4, sums)
    landed(act_y)
    act2 = [ring_send(other_act, k, 1) for k in range(2)]
    for copies in act1:
        landed(copies)
    activate(yh, 3)

    swaps = []
    for h in range(NH):
        landed(sums[2 * h : 2 * h + 2])
        total = part[h, z] + rs_recv[h, 0, 3].astype(F32) + rs_recv[h, 1, 3].astype(F32)
        part[h, z] = total
        swap_send[h] = total.astype(BF16)
        swaps.append(push(swap_send.at[h], swap_recv.at[h], across))
    activate(yh, 4)
    activate(1 - yh, 0)
    act2 = both_pass(other_act, 2, act2)
    tok_c.wait_recv()
    tok_t[...] = tok_all[...].reshape(-1, tok_all.shape[3]).T
    activate(1 - yh, 1)
    act2 = both_pass(other_act, 3, act2)
    activate(1 - yh, 2)
    loads[5].wait()
    loads[6].wait()

    def grad_start(h):
        swaps[h].wait_recv()
        grad_h[h, z] = (part[h, z] + swap_recv[h].astype(F32)).astype(BF16)
        return ring_send(grad_block, h, 1)

    def gradients(m):
        offsets = (m,) if m in (0, NZ // 2) else (m, NZ - m)
        places = [(z + o) % NZ for o in offsets]
        for at in places:
            for h in range(NH):

                @pl.loop(0, tb // ROWS)
                def _(i):
                    rows = pl.ds(pl.multiple_of(i * ROWS, ROWS), ROWS)
                    gh = grad_h[h, at, rows].astype(F32)
                    gate_grad[h, at, rows] = (gh * slope[h, at, rows]).astype(BF16)
                    up_grad[h, at, rows] = (gh * silu[h, at, rows]).astype(BF16)

        def tall(ref):
            return jnp.concatenate([ref[:, at].reshape(NH * tb, -1) for at in places], axis=0)

        sums = dot(tall(gate_grad), wg[...], 1, 1) + dot(tall(up_grad), wu[...], 1, 1)
        for n, o in enumerate(offsets):
            pair_sum[o] = sums[n * NH * tb : (n + 1) * NH * tb].reshape(pair_sum.shape[1:])
            core_send[o] = pair_sum[o, :, 1 - core]
            core_copy(o).start()

    def core_copy(o):
        return pltpu.make_async_remote_copy(
            src_ref=core_send.at[o], dst_ref=core_recv.at[o], send_sem=core_send_sem.at[o],
            recv_sem=core_recv_sem.at[o], device_id=sibling, device_id_type=MESH,
        )

    def x_copy(o, h, to_x, to_y):
        return pltpu.make_async_remote_copy(
            src_ref=x_send.at[o, h], dst_ref=x_recv.at[x, to_y], send_sem=x_send_sem.at[o, h],
            recv_sem=x_recv_sem.at[to_y, x], device_id=at_row(to_x, yl, core), device_id_type=MESH,
        )

    def target(o, h):
        at = h * NZ + (z + o) % NZ
        return at // NY, at % NY

    def outward(m):
        def step(o):
            core_copy(o).wait_recv()
            for h in range(NH):
                to_x, to_y = target(o, h)
                x_send[o, h] = pair_sum[o, h, core] + core_recv[o, h]

                @pl.when(to_x == x)
                def _():
                    x_own[to_y] = x_send[o, h]

                @pl.when(to_x != x)
                def _():
                    x_copy(o, h, to_x, to_y).start()

        pair_loop(m, step)

    def line_sum(to_y):
        total = x_own[to_y]
        for d in range(1, NX):
            src = (x + d) % NX
            pltpu.make_async_remote_copy(
                src_ref=x_send.at[0, 0], dst_ref=x_recv.at[src, to_y], send_sem=x_send_sem.at[0, 0],
                recv_sem=x_recv_sem.at[to_y, src], device_id=sibling, device_id_type=MESH,
            ).wait_recv()
            total = total + x_recv[src, to_y]
        return total

    def y_copy(e, src, to_y):
        return pltpu.make_async_remote_copy(
            src_ref=y_send.at[e], dst_ref=y_recv.at[src], send_sem=y_send_sem.at[e],
            recv_sem=y_recv_sem.at[src], device_id=at_row(x, to_y, core), device_id_type=MESH,
        )

    late = z % NY

    def y_start(e):
        to_y = (late + e) % NY
        y_send[e] = line_sum(to_y)

        @pl.when(to_y != yl)
        def _():
            y_copy(e, yl, to_y).start()

    grads = [grad_start(0)]
    act2 = both_pass(other_act, 4, act2)
    activate(1 - yh, 3)
    grads.append(grad_start(1))
    gradients(0)
    grads = both_pass(grad_block, 2, grads)
    for copies in act2:
        landed(copies)
    activate(1 - yh, 4)
    gradients(1)
    outward(0)
    grads = both_pass(grad_block, 3, grads)
    gradients(2)
    outward(1)
    grads = both_pass(grad_block, 4, grads)
    gradients(3)
    outward(2)
    go_flat = go_all[...].reshape(-1, go_all.shape[3])
    width = 256
    for n in range(hidden.shape[3] // width):
        cols = pl.ds(n * width, width)
        st_gd[cols] = dot(hidden[..., cols].reshape(-1, width), go_flat, 0, 0).astype(BF16)
    stores = [pltpu.make_async_copy(st_gd, out_gd, here.at[7])]
    stores[0].start()
    outward(3)
    for copies in grads:
        landed(copies)
    gradients(4)
    for e in (2, 1, 3):
        y_start(e)
    outward(4)
    for i, (grad, stage, out) in enumerate(((gate_grad, st_gg, out_gg), (up_grad, st_gu, out_gu))):
        for n in range(grad.shape[3] // width):
            cols = pl.ds(n * width, width)
            if i == 1 and n == 0:
                y_start(0)
            stage[:, cols] = dot(tok_t[...], grad[..., cols].reshape(-1, width), 1, 0).astype(BF16)
        stores.append(pltpu.make_async_copy(stage, out, here.at[8 + i]))
        stores[-1].start()

    total = y_send[(yl + NY - late) % NY]
    for d in range(1, NY):
        src = (yl + d) % NY
        y_copy(0, src, yl).wait_recv()
        total = total + y_recv[src]
    out_gt[...] = total.astype(BF16)

    for copy in sent:
        copy.wait_send()

    @pl.loop(0, NZ)
    def _(o):
        core_copy(o).wait_send()
        for h in range(NH):
            to_x, to_y = target(o, h)

            @pl.when(to_x != x)
            def _():
                x_copy(o, h, to_x, to_y).wait_send()

    for e in range(NY):
        to_y = (late + e) % NY

        @pl.when(to_y != yl)
        def _():
            y_copy(e, yl, to_y).wait_send()

    for store in stores:
        store.wait()


def copy_kernel(*refs):
    sources, results, sems = refs[:4], refs[4:8], refs[8]
    copies = [pltpu.make_async_copy(s, r, sems.at[i]) for i, (s, r) in enumerate(zip(sources, results))]
    for copy in copies:
        copy.start()
    for copy in copies:
        copy.wait()


def on_device(tokens, grad_out, gate_pre, up_pre, w_gate, w_up, w_down):
    th, dd = tokens.shape
    tb, ff = gate_pre.shape
    nrow, ncol = NX * NY, NH * NZ
    anywhere = pl.BlockSpec(memory_space=pl.ANY)
    vmem = pltpu.VMEM
    dma = pltpu.SemaphoreType.DMA
    out = [
        jax.ShapeDtypeStruct(tokens.shape, BF16),
        jax.ShapeDtypeStruct(w_gate.shape, BF16),
        jax.ShapeDtypeStruct(w_up.shape, BF16),
        jax.ShapeDtypeStruct(w_down.shape, BF16),
    ]
    every = (NH, NZ, tb, ff)
    scratch = [
        vmem((nrow, NC, th, dd), BF16),
        vmem((nrow, NC, th, dd), BF16),
        vmem((2,) + every, BF16),
        vmem((dd, ff), BF16),
        vmem((dd, ff), BF16),
        vmem((ff, dd), BF16),
        vmem(every, F32),
        vmem((NH, 2, 4, tb, ff), BF16),
        vmem((NH, 2, 4, tb, ff), BF16),
        vmem((NH, tb, ff), BF16),
        vmem((NH, tb, ff), BF16),
        vmem(every, BF16),
        vmem(every, F32),
        vmem(every, F32),
        vmem(every, BF16),
        vmem(every, BF16),
        vmem(every, BF16),
        vmem((dd, ncol * tb), BF16),
        vmem((NZ, NH, NC, th, dd), F32),
        vmem((NZ, NH, th, dd), F32),
        vmem((NZ, NH, th, dd), F32),
        vmem((NZ, NH, th, dd), F32),
        vmem((NX, NY, th, dd), F32),
        vmem((NY, th, dd), F32),
        vmem((NY, th, dd), F32),
        vmem((NY, th, dd), F32),
        vmem((dd, ff), BF16),
        vmem((dd, ff), BF16),
        vmem((ff, dd), BF16),
        dma((COPIES,)),
        dma((COPIES,)),
        dma((NZ,)),
        dma((NZ,)),
        dma((NZ, NH)),
        dma((NY, NX)),
        dma((NY,)),
        dma((NY,)),
        dma((10,)),
    ]
    results = (
        pl.pallas_call(
            kernel,
            out_shape=out,
            in_specs=[anywhere] * 7,
            out_specs=[pl.BlockSpec(memory_space=vmem)] + [anywhere] * 3,
            scratch_shapes=scratch,
            compiler_params=pltpu.CompilerParams(
                collective_id=0, has_side_effects=True, vmem_limit_bytes=56 * 2**20
            ),
            cost_estimate=pl.CostEstimate(
                flops=12 * nrow * NC * th * dd * ff, bytes_accessed=8 * dd * ff * 2, transcendentals=ncol * tb * ff
            ),
        )(tokens, grad_out, gate_pre, up_pre, w_gate, w_up, w_down)
    )
    return tuple(
        pl.pallas_call(
            copy_kernel,
            out_shape=out,
            in_specs=[anywhere] * 4,
            out_specs=[anywhere] * 4,
            scratch_shapes=[dma((4,))],
            compiler_params=pltpu.CompilerParams(vmem_limit_bytes=60 * 2**20),
        )(*results)
    )


def solution(mesh):
    return jax.shard_map(
        on_device,
        mesh=mesh,
        in_specs=(
            P("row", "col"),
            P("row", "col"),
            P("col", "row"),
            P("col", "row"),
            P("col", "row"),
            P("col", "row"),
            P("row", "col"),
        ),
        out_specs=(P("row", "col"), P("col", "row"), P("col", "row"), P("row", "col")),
        check_vma=False,
    )
```

```python
import functools

import jax
import jax.numpy as jnp
from jax import lax
from jax.experimental import pallas as pl
from jax.experimental.pallas import tpu as pltpu
from jax.sharding import PartitionSpec as P

MESH = pl.DeviceIdType.MESH
F32 = jnp.float32
BF16 = jnp.bfloat16
NX, NY, NC = 4, 4, 2
NH, NZ = 2, 8
ROWS = 32
COPIES = 94


def dot(left, right, left_dim, right_dim):
    return lax.dot_general(
        left, right, (((left_dim,), (right_dim,)), ((), ())), preferred_element_type=F32
    )


def kernel(
    tok_ref, go_ref, gate_ref, up_ref, wg_ref, wu_ref, wd_ref,
    out_gt, out_gg, out_gu, out_gd,
    tok_all, go_all, acts, wg, wu, wd, part, rs_send, rs_recv, swap_send, swap_recv,
    grad_h, silu, slope, hidden, gate_grad, up_grad, tok_t, pair_sum, core_send, core_recv,
    x_send, x_recv, x_own, y_send, y_recv, st_gg, st_gu, st_gd,
    send, recv, core_send_sem, core_recv_sem, x_send_sem, x_recv_sem, y_send_sem, y_recv_sem, here,
):
    row, col = lax.axis_index("row"), lax.axis_index("col")
    x, yl, core = row // (NY * NC), (row // NC) % NY, row % NC
    yh, z = col // NZ, col % NZ
    tb, half = acts.shape[3], acts.shape[3] // 2

    def at_row(px, py, pc):
        return (px * (NY * NC) + py * NC + pc, col)

    def at_col(ph, pz):
        return (row, ph * NZ + pz)

    xs = [at_row((x + d) % NX, yl, core) for d in range(1, NX)]
    ys = [at_row(x, (yl + d) % NY, core) for d in range(1, NY)]
    sibling = at_row(x, yl, 1 - core)
    ahead, behind = at_col(yh, (z + 1) % NZ), at_col(yh, (z + NZ - 1) % NZ)
    across = at_col(1 - yh, z)

    sent = []

    def push(src, dst, to):
        n = len(sent)
        copy = pltpu.make_async_remote_copy(
            src_ref=src, dst_ref=dst, send_sem=send.at[n], recv_sem=recv.at[n],
            device_id=to, device_id_type=MESH,
        )
        copy.start()
        sent.append(copy)
        return copy

    def landed(copies):
        for copy in copies:
            copy.wait_recv()

    mine = x * NY + yl
    loads = [
        (go_ref, go_all.at[mine, core]), (tok_ref, tok_all.at[mine, core]),
        (gate_ref, acts.at[0, yh, z]), (up_ref, acts.at[1, yh, z]),
        (wd_ref, wd), (wg_ref, wg), (wu_ref, wu),
    ]
    loads = [pltpu.make_async_copy(s, d, here.at[i]) for i, (s, d) in enumerate(loads)]
    for load in loads:
        load.start()

    barrier = pltpu.get_barrier_semaphore()
    partners = xs + ys + [sibling, ahead, behind, across]
    for to in partners:
        pl.semaphore_signal(barrier, inc=1, device_id=to, device_id_type=MESH)
    pl.semaphore_wait(barrier, len(partners))

    def ring_send(block, k, step, first=None):
        copies = []
        for way, to in ((1, ahead), (-1, behind)):
            at = (z + (NZ - way * (step - 1))) % NZ
            ref = block(k, at)
            if step == NZ // 2:
                ref = ref.at[pl.ds(0 if way == 1 else half, half)]
            copies.append(push(ref if first is None else first, ref, to))
        return copies

    def ring_pass(block, k, step, before):
        landed(before)
        return ring_send(block, k, step)

    def both_pass(block, step, before):
        return [ring_pass(block, k, step, before[k]) for k in range(2)]

    def own_act(k, at):
        return acts.at[k, yh, at]

    def other_act(k, at):
        return acts.at[k, 1 - yh, at]

    def grad_block(k, at):
        return grad_h.at[k, at]

    def pair_loop(m, step):
        if m in (0, NZ // 2):
            step(m)
        else:
            pl.loop(0, 2)(lambda i: step(m + (NZ - 2 * m) * i))

    def activate(h, m):
        def step(o):
            at = (z + o) % NZ

            @pl.loop(0, tb // ROWS)
            def _(i):
                rows = pl.ds(pl.multiple_of(i * ROWS, ROWS), ROWS)
                g = acts[0, h, at, rows].astype(F32)
                u = acts[1, h, at, rows].astype(F32)
                s = jax.nn.sigmoid(g)
                gs = g * s
                silu[h, at, rows] = gs
                slope[h, at, rows] = u * s * (1.0 + g * (1.0 - s))
                hidden[h, at, rows] = (gs * u).astype(BF16)

        pair_loop(m, step)

    def share(m):
        def step(o):
            at = (z + o) % NZ
            rows = jnp.concatenate(
                [go_all[h * NZ + at].reshape(tb, -1) for h in range(NH)], axis=0
            )
            sums = dot(rows, wd[...], 1, 1)
            for h in range(NH):
                part[h, at] = sums[h * tb : (h + 1) * tb]

        pair_loop(m, step)

    def reduce_step(step, before):
        copies = []
        for h in range(NH):
            for w, (way, to) in enumerate(((1, ahead), (-1, behind))):
                at = (z + (NZ + way * (NZ // 2 + 1 - step))) % NZ
                out = rs_send.at[h, w, step - 1]
                rows = pl.ds(0 if way == 1 else half, half)
                if step == 1:
                    out[rows] = part[h, at, rows].astype(BF16)
                    copies.append(push(out.at[rows], rs_recv.at[h, w, 0, rows], to))
                    continue
                before[2 * h + w].wait_recv()
                if step == 2:
                    rest = pl.ds(half if way == 1 else 0, half)
                    out[rows] = (part[h, at, rows] + rs_recv[h, w, 0, rows].astype(F32)).astype(BF16)
                    out[rest] = part[h, at, rest].astype(BF16)
                else:
                    out[...] = (part[h, at] + rs_recv[h, w, step - 2].astype(F32)).astype(BF16)
                copies.append(push(out, rs_recv.at[h, w, step - 1], to))
        return copies

    def spread(own, copies_of, source):
        return [push(source, own, to) for to in copies_of]

    def x_line(ref, px):
        return ref.at[pl.ds(px * NY, NY), core]

    go_own = go_all.at[mine, core]
    go_y = spread(go_own, ys, go_ref)
    go_x = [spread(go_own, xs, go_ref)]
    act1 = [ring_send(own_act, k, 1, first=ref) for k, ref in enumerate((gate_ref, up_ref))]
    tok_y = spread(tok_all.at[mine, core], ys, tok_ref)
    for d in range(1, NY):
        go_y[d - 1].wait_recv()
        block = go_all.at[x * NY + (yl + NY - d) % NY, core]
        go_x.append(spread(block, xs, block))
    act_y = [push(ref, acts.at[k, yh, z], across) for k, ref in enumerate((gate_ref, up_ref))]
    loads[0].wait()
    go_c = [push(x_line(go_all, x), x_line(go_all, x), sibling)]
    loads[2].wait()
    loads[3].wait()
    activate(yh, 0)
    act1 = both_pass(own_act, 2, act1)
    activate(yh, 1)
    loads[1].wait()
    landed(tok_y)
    for d in (1, 3, 2):
        landed([copies[d - 1] for copies in go_x])
        line = x_line(go_all, (x + NX - d) % NX)
        go_c.append(push(line, line, sibling))
    tok_x = spread(x_line(tok_all, x), xs, x_line(tok_all, x))
    act1 = both_pass(own_act, 3, act1)
    loads[4].wait()
    landed(go_c)

    share(4)
    sums = reduce_step(1, None)
    share(3)
    act1 = both_pass(own_act, 4, act1)
    sums = reduce_step(2, sums)
    share(2)
    landed(tok_x)
    tok_c = push(tok_all.at[:, core], tok_all.at[:, core], sibling)
    activate(yh, 2)
    sums = reduce_step(3, sums)
    share(1)
    share(0)
    sums = reduce_step(4, sums)
    landed(act_y)
    act2 = [ring_send(other_act, k, 1) for k in range(2)]
    for copies in act1:
        landed(copies)
    activate(yh, 3)

    swaps = []
    for h in range(NH):
        landed(sums[2 * h : 2 * h + 2])
        total = part[h, z] + rs_recv[h, 0, 3].astype(F32) + rs_recv[h, 1, 3].astype(F32)
        part[h, z] = total
        swap_send[h] = total.astype(BF16)
        swaps.append(push(swap_send.at[h], swap_recv.at[h], across))
    activate(yh, 4)
    activate(1 - yh, 0)
    act2 = both_pass(other_act, 2, act2)
    tok_c.wait_recv()
    tok_t[...] = tok_all[...].reshape(-1, tok_all.shape[3]).T
    activate(1 - yh, 1)
    act2 = both_pass(other_act, 3, act2)
    activate(1 - yh, 2)
    loads[5].wait()
    loads[6].wait()

    def grad_start(h):
        swaps[h].wait_recv()
        grad_h[h, z] = (part[h, z] + swap_recv[h].astype(F32)).astype(BF16)
        return ring_send(grad_block, h, 1)

    def gradients(m):
        offsets = (m,) if m in (0, NZ // 2) else (m, NZ - m)
        places = [(z + o) % NZ for o in offsets]
        for at in places:
            for h in range(NH):

                @pl.loop(0, tb // ROWS)
                def _(i):
                    rows = pl.ds(pl.multiple_of(i * ROWS, ROWS), ROWS)
                    gh = grad_h[h, at, rows].astype(F32)
                    gate_grad[h, at, rows] = (gh * slope[h, at, rows]).astype(BF16)
                    up_grad[h, at, rows] = (gh * silu[h, at, rows]).astype(BF16)

        def tall(ref):
            return jnp.concatenate([ref[:, at].reshape(NH * tb, -1) for at in places], axis=0)

        sums = dot(tall(gate_grad), wg[...], 1, 1) + dot(tall(up_grad), wu[...], 1, 1)
        for n, o in enumerate(offsets):
            pair_sum[o] = sums[n * NH * tb : (n + 1) * NH * tb].reshape(pair_sum.shape[1:])
            core_send[o] = pair_sum[o, :, 1 - core]
            core_copy(o).start()

    def core_copy(o):
        return pltpu.make_async_remote_copy(
            src_ref=core_send.at[o], dst_ref=core_recv.at[o], send_sem=core_send_sem.at[o],
            recv_sem=core_recv_sem.at[o], device_id=sibling, device_id_type=MESH,
        )

    def x_copy(o, h, to_x, to_y):
        return pltpu.make_async_remote_copy(
            src_ref=x_send.at[o, h], dst_ref=x_recv.at[x, to_y], send_sem=x_send_sem.at[o, h],
            recv_sem=x_recv_sem.at[to_y, x], device_id=at_row(to_x, yl, core), device_id_type=MESH,
        )

    def target(o, h):
        at = h * NZ + (z + o) % NZ
        return at // NY, at % NY

    def outward(m):
        def step(o):
            core_copy(o).wait_recv()
            for h in range(NH):
                to_x, to_y = target(o, h)
                x_send[o, h] = pair_sum[o, h, core] + core_recv[o, h]

                @pl.when(to_x == x)
                def _():
                    x_own[to_y] = x_send[o, h]

                @pl.when(to_x != x)
                def _():
                    x_copy(o, h, to_x, to_y).start()

        pair_loop(m, step)

    def line_sum(to_y):
        total = x_own[to_y]
        for d in range(1, NX):
            src = (x + d) % NX
            pltpu.make_async_remote_copy(
                src_ref=x_send.at[0, 0], dst_ref=x_recv.at[src, to_y], send_sem=x_send_sem.at[0, 0],
                recv_sem=x_recv_sem.at[to_y, src], device_id=sibling, device_id_type=MESH,
            ).wait_recv()
            total = total + x_recv[src, to_y]
        return total

    def y_copy(e, src, to_y):
        return pltpu.make_async_remote_copy(
            src_ref=y_send.at[e], dst_ref=y_recv.at[src], send_sem=y_send_sem.at[e],
            recv_sem=y_recv_sem.at[src], device_id=at_row(x, to_y, core), device_id_type=MESH,
        )

    late = z % NY

    def y_start(e):
        to_y = (late + e) % NY
        y_send[e] = line_sum(to_y)

        @pl.when(to_y != yl)
        def _():
            y_copy(e, yl, to_y).start()

    grads = [grad_start(0)]
    act2 = both_pass(other_act, 4, act2)
    activate(1 - yh, 3)
    grads.append(grad_start(1))
    gradients(0)
    grads = both_pass(grad_block, 2, grads)
    for copies in act2:
        landed(copies)
    activate(1 - yh, 4)
    gradients(1)
    outward(0)
    grads = both_pass(grad_block, 3, grads)
    gradients(2)
    outward(1)
    grads = both_pass(grad_block, 4, grads)
    gradients(3)
    outward(2)
    go_flat = go_all[...].reshape(-1, go_all.shape[3])
    width = 256
    for n in range(hidden.shape[3] // width):
        cols = pl.ds(n * width, width)
        st_gd[cols] = dot(hidden[..., cols].reshape(-1, width), go_flat, 0, 0).astype(BF16)
    stores = [pltpu.make_async_copy(st_gd, out_gd, here.at[7])]
    stores[0].start()
    outward(3)
    for copies in grads:
        landed(copies)
    gradients(4)
    for i, (grad, stage, out) in enumerate(((gate_grad, st_gg, out_gg), (up_grad, st_gu, out_gu))):
        for n in range(grad.shape[3] // width):
            cols = pl.ds(n * width, width)
            if i == 0 and n == 1:
                outward(4)
                for e in (2, 1, 3):
                    y_start(e)
            if i == 1 and n == 1:
                y_start(0)
            stage[:, cols] = dot(tok_t[...], grad[..., cols].reshape(-1, width), 1, 0).astype(BF16)
        stores.append(pltpu.make_async_copy(stage, out, here.at[8 + i]))
        stores[-1].start()

    total = y_send[(yl + NY - late) % NY]
    for d in range(1, NY):
        src = (yl + d) % NY
        y_copy(0, src, yl).wait_recv()
        total = total + y_recv[src]
    out_gt[...] = total.astype(BF16)

    for copy in sent:
        copy.wait_send()

    @pl.loop(0, NZ)
    def _(o):
        core_copy(o).wait_send()
        for h in range(NH):
            to_x, to_y = target(o, h)

            @pl.when(to_x != x)
            def _():
                x_copy(o, h, to_x, to_y).wait_send()

    for e in range(NY):
        to_y = (late + e) % NY

        @pl.when(to_y != yl)
        def _():
            y_copy(e, yl, to_y).wait_send()

    for store in stores:
        store.wait()


def copy_kernel(*refs):
    sources, results, held, sems = refs[:4], refs[4:8], refs[8:12], refs[12]
    reads = [pltpu.make_async_copy(s, h, sems.at[0, i]) for i, (s, h) in enumerate(zip(sources, held))]
    writes = [pltpu.make_async_copy(h, r, sems.at[1, i]) for i, (h, r) in enumerate(zip(held, results))]
    for read in reads:
        read.start()
    for read, write in zip(reads, writes):
        read.wait()
        write.start()
    for write in writes:
        write.wait()


def on_device(tokens, grad_out, gate_pre, up_pre, w_gate, w_up, w_down):
    th, dd = tokens.shape
    tb, ff = gate_pre.shape
    nrow, ncol = NX * NY, NH * NZ
    anywhere = pl.BlockSpec(memory_space=pl.ANY)
    vmem = pltpu.VMEM
    dma = pltpu.SemaphoreType.DMA
    out = [
        jax.ShapeDtypeStruct(tokens.shape, BF16),
        jax.ShapeDtypeStruct(w_gate.shape, BF16),
        jax.ShapeDtypeStruct(w_up.shape, BF16),
        jax.ShapeDtypeStruct(w_down.shape, BF16),
    ]
    every = (NH, NZ, tb, ff)
    scratch = [
        vmem((nrow, NC, th, dd), BF16),
        vmem((nrow, NC, th, dd), BF16),
        vmem((2,) + every, BF16),
        vmem((dd, ff), BF16),
        vmem((dd, ff), BF16),
        vmem((ff, dd), BF16),
        vmem(every, F32),
        vmem((NH, 2, 4, tb, ff), BF16),
        vmem((NH, 2, 4, tb, ff), BF16),
        vmem((NH, tb, ff), BF16),
        vmem((NH, tb, ff), BF16),
        vmem(every, BF16),
        vmem(every, F32),
        vmem(every, F32),
        vmem(every, BF16),
        vmem(every, BF16),
        vmem(every, BF16),
        vmem((dd, ncol * tb), BF16),
        vmem((NZ, NH, NC, th, dd), F32),
        vmem((NZ, NH, th, dd), F32),
        vmem((NZ, NH, th, dd), F32),
        vmem((NZ, NH, th, dd), F32),
        vmem((NX, NY, th, dd), F32),
        vmem((NY, th, dd), F32),
        vmem((NY, th, dd), F32),
        vmem((NY, th, dd), F32),
        vmem((dd, ff), BF16),
        vmem((dd, ff), BF16),
        vmem((ff, dd), BF16),
        dma((COPIES,)),
        dma((COPIES,)),
        dma((NZ,)),
        dma((NZ,)),
        dma((NZ, NH)),
        dma((NY, NX)),
        dma((NY,)),
        dma((NY,)),
        dma((10,)),
    ]
    results = (
        pl.pallas_call(
            kernel,
            out_shape=out,
            in_specs=[anywhere] * 7,
            out_specs=[pl.BlockSpec(memory_space=vmem)] + [anywhere] * 3,
            scratch_shapes=scratch,
            compiler_params=pltpu.CompilerParams(
                collective_id=0, has_side_effects=True, vmem_limit_bytes=56 * 2**20
            ),
            cost_estimate=pl.CostEstimate(
                flops=12 * nrow * NC * th * dd * ff, bytes_accessed=8 * dd * ff * 2, transcendentals=ncol * tb * ff
            ),
        )(tokens, grad_out, gate_pre, up_pre, w_gate, w_up, w_down)
    )
    return tuple(
        pl.pallas_call(
            copy_kernel,
            out_shape=out,
            in_specs=[anywhere] * 4,
            out_specs=[anywhere] * 4,
            scratch_shapes=[vmem(o.shape, o.dtype) for o in out] + [dma((2, 4))],
            compiler_params=pltpu.CompilerParams(vmem_limit_bytes=60 * 2**20),
        )(*results)
    )


def solution(mesh):
    return jax.shard_map(
        on_device,
        mesh=mesh,
        in_specs=(
            P("row", "col"),
            P("row", "col"),
            P("col", "row"),
            P("col", "row"),
            P("col", "row"),
            P("col", "row"),
            P("row", "col"),
        ),
        out_specs=(P("row", "col"), P("col", "row"), P("col", "row"), P("row", "col")),
        check_vma=False,
    )
```

```python
import functools

import jax
import jax.numpy as jnp
from jax import lax
from jax.experimental import pallas as pl
from jax.experimental.pallas import tpu as pltpu
from jax.sharding import PartitionSpec as P

MESH = pl.DeviceIdType.MESH
F32 = jnp.float32
BF16 = jnp.bfloat16
NX, NY, NC = 4, 4, 2
NH, NZ = 2, 8
ROWS = 32
COPIES = 100


def dot(left, right, left_dim, right_dim):
    return lax.dot_general(
        left, right, (((left_dim,), (right_dim,)), ((), ())), preferred_element_type=F32
    )


def kernel(
    tok_ref, go_ref, gate_ref, up_ref, wg_ref, wu_ref, wd_ref,
    out_gt, out_gg, out_gu, out_gd,
    tok_all, go_all, acts, wg, wu, wd, part, rs_send, rs_recv, swap_send, swap_stop, swap_recv,
    grad_h, silu, slope, hidden, gate_grad, up_grad, tok_t, pair_sum, core_send, core_recv,
    x_send, x_recv, x_own, y_send, y_recv, st_gg, st_gu, st_gd,
    send, recv, core_send_sem, core_recv_sem, x_send_sem, x_recv_sem, y_send_sem, y_recv_sem, here,
):
    row, col = lax.axis_index("row"), lax.axis_index("col")
    x, yl, core = row // (NY * NC), (row // NC) % NY, row % NC
    yh, z = col // NZ, col % NZ
    tb, half = acts.shape[3], acts.shape[3] // 2

    def at_row(px, py, pc):
        return (px * (NY * NC) + py * NC + pc, col)

    def at_col(ph, pz):
        return (row, ph * NZ + pz)

    xs = [at_row((x + d) % NX, yl, core) for d in range(1, NX)]
    ys = [at_row(x, (yl + d) % NY, core) for d in range(1, NY)]
    sibling = at_row(x, yl, 1 - core)
    ahead, behind = at_col(yh, (z + 1) % NZ), at_col(yh, (z + NZ - 1) % NZ)
    across = at_col(1 - yh, z)

    def two_along(turn):
        return (at_row(x, (yl + 2) % NY, core)[0], ((yh + turn) % NH) * NZ + z)

    turn = (yl + 2) // NY
    two_up, two_down = two_along(turn), two_along(1 - turn)
    diagonal = two_along(1)

    sent = []

    def push(src, dst, to):
        n = len(sent)
        copy = pltpu.make_async_remote_copy(
            src_ref=src, dst_ref=dst, send_sem=send.at[n], recv_sem=recv.at[n],
            device_id=to, device_id_type=MESH,
        )
        copy.start()
        sent.append(copy)
        return copy

    def landed(copies):
        for copy in copies:
            copy.wait_recv()

    mine = x * NY + yl
    loads = [
        (go_ref, go_all.at[mine, core]), (tok_ref, tok_all.at[mine, core]),
        (gate_ref, acts.at[0, yh, z]), (up_ref, acts.at[1, yh, z]),
        (wd_ref, wd), (wg_ref, wg), (wu_ref, wu),
    ]
    loads = [pltpu.make_async_copy(s, d, here.at[i]) for i, (s, d) in enumerate(loads)]
    for load in loads:
        load.start()

    barrier = pltpu.get_barrier_semaphore()
    partners = xs + ys + [sibling, ahead, behind, across, diagonal]
    for to in partners:
        pl.semaphore_signal(barrier, inc=1, device_id=to, device_id_type=MESH)
    pl.semaphore_wait(barrier, len(partners))

    def ring_send(block, k, step, first=None):
        copies = []
        for way, to in ((1, ahead), (-1, behind)):
            at = (z + (NZ - way * (step - 1))) % NZ
            ref = block(k, at)
            if step == NZ // 2:
                ref = ref.at[pl.ds(0 if way == 1 else half, half)]
            copies.append(push(ref if first is None else first, ref, to))
        return copies

    def ring_pass(block, k, step, before):
        landed(before)
        return ring_send(block, k, step)

    def both_pass(block, step, before):
        return [ring_pass(block, k, step, before[k]) for k in range(2)]

    def own_act(k, at):
        return acts.at[k, yh, at]

    def other_act(k, at):
        return acts.at[k, 1 - yh, at]

    def grad_block(k, at):
        return grad_h.at[k, at]

    def pair_loop(m, step):
        if m in (0, NZ // 2):
            step(m)
        else:
            pl.loop(0, 2)(lambda i: step(m + (NZ - 2 * m) * i))

    def activate(h, m):
        def step(o):
            at = (z + o) % NZ

            @pl.loop(0, tb // ROWS)
            def _(i):
                rows = pl.ds(pl.multiple_of(i * ROWS, ROWS), ROWS)
                g = acts[0, h, at, rows].astype(F32)
                u = acts[1, h, at, rows].astype(F32)
                s = jax.nn.sigmoid(g)
                gs = g * s
                silu[h, at, rows] = gs
                slope[h, at, rows] = u * s * (1.0 + g * (1.0 - s))
                hidden[h, at, rows] = (gs * u).astype(BF16)

        pair_loop(m, step)

    def share(m):
        def step(o):
            at = (z + o) % NZ
            rows = jnp.concatenate(
                [go_all[h * NZ + at].reshape(tb, -1) for h in range(NH)], axis=0
            )
            sums = dot(rows, wd[...], 1, 1)
            for h in range(NH):
                part[h, at] = sums[h * tb : (h + 1) * tb]

        pair_loop(m, step)

    def reduce_step(step, before):
        copies = []
        for h in range(NH):
            for w, (way, to) in enumerate(((1, ahead), (-1, behind))):
                at = (z + (NZ + way * (NZ // 2 + 1 - step))) % NZ
                out = rs_send.at[h, w, step - 1]
                rows = pl.ds(0 if way == 1 else half, half)
                if step == 1:
                    out[rows] = part[h, at, rows].astype(BF16)
                    copies.append(push(out.at[rows], rs_recv.at[h, w, 0, rows], to))
                    continue
                before[2 * h + w].wait_recv()
                if step == 2:
                    rest = pl.ds(half if way == 1 else 0, half)
                    out[rows] = (part[h, at, rows] + rs_recv[h, w, 0, rows].astype(F32)).astype(BF16)
                    out[rest] = part[h, at, rest].astype(BF16)
                else:
                    out[...] = (part[h, at] + rs_recv[h, w, step - 2].astype(F32)).astype(BF16)
                copies.append(push(out, rs_recv.at[h, w, step - 1], to))
        return copies

    def spread(own, copies_of, source):
        return [push(source, own, to) for to in copies_of]

    def x_line(ref, px):
        return ref.at[pl.ds(px * NY, NY), core]

    go_own = go_all.at[mine, core]
    go_y = spread(go_own, ys, go_ref)
    go_x = [spread(go_own, xs, go_ref)]
    act1 = [ring_send(own_act, k, 1, first=ref) for k, ref in enumerate((gate_ref, up_ref))]
    tok_y = spread(tok_all.at[mine, core], ys, tok_ref)
    for d in range(1, NY):
        go_y[d - 1].wait_recv()
        block = go_all.at[x * NY + (yl + NY - d) % NY, core]
        go_x.append(spread(block, xs, block))
    act_y = [push(ref, acts.at[k, yh, z], across) for k, ref in enumerate((gate_ref, up_ref))]
    loads[0].wait()
    go_c = [push(x_line(go_all, x), x_line(go_all, x), sibling)]
    loads[2].wait()
    loads[3].wait()
    activate(yh, 0)
    act1 = both_pass(own_act, 2, act1)
    activate(yh, 1)
    loads[1].wait()
    landed(tok_y)
    act1 = both_pass(own_act, 3, act1)
    for d in (1, 3, 2):
        landed([copies[d - 1] for copies in go_x])
        line = x_line(go_all, (x + NX - d) % NX)
        go_c.append(push(line, line, sibling))
    tok_x = spread(x_line(tok_all, x), xs, x_line(tok_all, x))
    loads[4].wait()
    landed(go_c)

    share(4)
    sums = reduce_step(1, None)
    act1 = both_pass(own_act, 4, act1)
    share(3)
    sums = reduce_step(2, sums)
    share(2)
    landed(tok_x)
    tok_c = push(tok_all.at[:, core], tok_all.at[:, core], sibling)
    activate(yh, 2)
    sums = reduce_step(3, sums)
    share(1)
    share(0)
    sums = reduce_step(4, sums)
    landed(act_y)
    act2 = [ring_send(other_act, k, 1) for k in range(2)]
    for copies in act1:
        landed(copies)
    activate(yh, 3)

    def swap_send_on(h, src, dst):
        copies = []
        for part_at, to in enumerate((two_up, two_down)):
            rows = pl.ds(part_at * half, half)
            copies.append(push(src.at[h, rows], dst.at[h, rows], to))
        return copies

    def swap_pass(h):
        copies = []
        for part_at, to in enumerate((two_up, two_down)):
            swaps[h][part_at].wait_recv()
            rows = pl.ds(part_at * half, half)
            copies.append(push(swap_stop.at[h, rows], swap_recv.at[h, rows], to))
        swaps[h] = copies

    swaps = []
    for h in range(NH):
        landed(sums[2 * h : 2 * h + 2])
        total = part[h, z] + rs_recv[h, 0, 3].astype(F32) + rs_recv[h, 1, 3].astype(F32)
        part[h, z] = total
        swap_send[h] = total.astype(BF16)
        swaps.append(swap_send_on(h, swap_send, swap_stop))
    activate(yh, 4)
    activate(1 - yh, 0)
    swap_pass(0)
    act2 = both_pass(other_act, 2, act2)
    swap_pass(1)
    tok_c.wait_recv()
    tok_t[...] = tok_all[...].reshape(-1, tok_all.shape[3]).T
    activate(1 - yh, 1)
    loads[5].wait()
    loads[6].wait()

    def grad_start(h):
        landed(swaps[h])
        grad_h[h, z] = (part[h, z] + swap_recv[h].astype(F32)).astype(BF16)
        return ring_send(grad_block, h, 1)

    def gradients(m):
        offsets = (m,) if m in (0, NZ // 2) else (m, NZ - m)
        places = [(z + o) % NZ for o in offsets]
        for at in places:
            for h in range(NH):

                @pl.loop(0, tb // ROWS)
                def _(i):
                    rows = pl.ds(pl.multiple_of(i * ROWS, ROWS), ROWS)
                    gh = grad_h[h, at, rows].astype(F32)
                    gate_grad[h, at, rows] = (gh * slope[h, at, rows]).astype(BF16)
                    up_grad[h, at, rows] = (gh * silu[h, at, rows]).astype(BF16)

        def tall(ref):
            return jnp.concatenate([ref[:, at].reshape(NH * tb, -1) for at in places], axis=0)

        sums = dot(tall(gate_grad), wg[...], 1, 1) + dot(tall(up_grad), wu[...], 1, 1)
        for n, o in enumerate(offsets):
            pair_sum[o] = sums[n * NH * tb : (n + 1) * NH * tb].reshape(pair_sum.shape[1:])
            core_send[o] = pair_sum[o, :, 1 - core]
            core_copy(o).start()

    def core_copy(o):
        return pltpu.make_async_remote_copy(
            src_ref=core_send.at[o], dst_ref=core_recv.at[o], send_sem=core_send_sem.at[o],
            recv_sem=core_recv_sem.at[o], device_id=sibling, device_id_type=MESH,
        )

    def x_copy(o, h, to_x, to_y):
        return pltpu.make_async_remote_copy(
            src_ref=x_send.at[o, h], dst_ref=x_recv.at[x, to_y], send_sem=x_send_sem.at[o, h],
            recv_sem=x_recv_sem.at[to_y, x], device_id=at_row(to_x, yl, core), device_id_type=MESH,
        )

    def target(o, h):
        at = h * NZ + (z + o) % NZ
        return at // NY, at % NY

    def outward(m):
        def step(o):
            core_copy(o).wait_recv()
            for h in range(NH):
                to_x, to_y = target(o, h)
                x_send[o, h] = pair_sum[o, h, core] + core_recv[o, h]

                @pl.when(to_x == x)
                def _():
                    x_own[to_y] = x_send[o, h]

                @pl.when(to_x != x)
                def _():
                    x_copy(o, h, to_x, to_y).start()

        pair_loop(m, step)

    def line_sum(to_y):
        total = x_own[to_y]
        for d in range(1, NX):
            src = (x + d) % NX
            pltpu.make_async_remote_copy(
                src_ref=x_send.at[0, 0], dst_ref=x_recv.at[src, to_y], send_sem=x_send_sem.at[0, 0],
                recv_sem=x_recv_sem.at[to_y, src], device_id=sibling, device_id_type=MESH,
            ).wait_recv()
            total = total + x_recv[src, to_y]
        return total

    def y_copy(e, src, to_y):
        return pltpu.make_async_remote_copy(
            src_ref=y_send.at[e], dst_ref=y_recv.at[src], send_sem=y_send_sem.at[e],
            recv_sem=y_recv_sem.at[src], device_id=at_row(x, to_y, core), device_id_type=MESH,
        )

    late = z % NY

    def y_start(e):
        to_y = (late + e) % NY
        y_send[e] = line_sum(to_y)

        @pl.when(to_y != yl)
        def _():
            y_copy(e, yl, to_y).start()

    grads = [grad_start(0)]
    act2 = both_pass(other_act, 3, act2)
    grads.append(grad_start(1))
    activate(1 - yh, 2)
    act2 = both_pass(other_act, 4, act2)
    activate(1 - yh, 3)
    gradients(0)
    grads = both_pass(grad_block, 2, grads)
    for copies in act2:
        landed(copies)
    activate(1 - yh, 4)
    gradients(1)
    outward(0)
    grads = both_pass(grad_block, 3, grads)
    gradients(2)
    outward(1)
    grads = both_pass(grad_block, 4, grads)
    gradients(3)
    outward(2)
    go_flat = go_all[...].reshape(-1, go_all.shape[3])
    width = 256
    for n in range(hidden.shape[3] // width):
        cols = pl.ds(n * width, width)
        st_gd[cols] = dot(hidden[..., cols].reshape(-1, width), go_flat, 0, 0).astype(BF16)
    stores = [pltpu.make_async_copy(st_gd, out_gd, here.at[7])]
    stores[0].start()
    outward(3)
    for copies in grads:
        landed(copies)
    gradients(4)
    for i, (grad, stage, out) in enumerate(((gate_grad, st_gg, out_gg), (up_grad, st_gu, out_gu))):
        for n in range(grad.shape[3] // width):
            cols = pl.ds(n * width, width)
            if i == 0 and n == 1:
                outward(4)
                for e in (2, 1, 3):
                    y_start(e)
            if i == 1 and n == 1:
                y_start(0)
            stage[:, cols] = dot(tok_t[...], grad[..., cols].reshape(-1, width), 1, 0).astype(BF16)
        stores.append(pltpu.make_async_copy(stage, out, here.at[8 + i]))
        stores[-1].start()

    total = y_send[(yl + NY - late) % NY]
    for d in range(1, NY):
        src = (yl + d) % NY
        y_copy(0, src, yl).wait_recv()
        total = total + y_recv[src]
    out_gt[...] = total.astype(BF16)

    for copy in sent:
        copy.wait_send()

    @pl.loop(0, NZ)
    def _(o):
        core_copy(o).wait_send()
        for h in range(NH):
            to_x, to_y = target(o, h)

            @pl.when(to_x != x)
            def _():
                x_copy(o, h, to_x, to_y).wait_send()

    for e in range(NY):
        to_y = (late + e) % NY

        @pl.when(to_y != yl)
        def _():
            y_copy(e, yl, to_y).wait_send()

    for store in stores:
        store.wait()


def copy_kernel(*refs):
    sources, results, held, sems = refs[:4], refs[4:8], refs[8:12], refs[12]
    reads = [pltpu.make_async_copy(s, h, sems.at[0, i]) for i, (s, h) in enumerate(zip(sources, held))]
    writes = [pltpu.make_async_copy(h, r, sems.at[1, i]) for i, (h, r) in enumerate(zip(held, results))]
    for read in reads:
        read.start()
    for read, write in zip(reads, writes):
        read.wait()
        write.start()
    for write in writes:
        write.wait()


def on_device(tokens, grad_out, gate_pre, up_pre, w_gate, w_up, w_down):
    th, dd = tokens.shape
    tb, ff = gate_pre.shape
    nrow, ncol = NX * NY, NH * NZ
    anywhere = pl.BlockSpec(memory_space=pl.ANY)
    vmem = pltpu.VMEM
    dma = pltpu.SemaphoreType.DMA
    out = [
        jax.ShapeDtypeStruct(tokens.shape, BF16),
        jax.ShapeDtypeStruct(w_gate.shape, BF16),
        jax.ShapeDtypeStruct(w_up.shape, BF16),
        jax.ShapeDtypeStruct(w_down.shape, BF16),
    ]
    every = (NH, NZ, tb, ff)
    scratch = [
        vmem((nrow, NC, th, dd), BF16),
        vmem((nrow, NC, th, dd), BF16),
        vmem((2,) + every, BF16),
        vmem((dd, ff), BF16),
        vmem((dd, ff), BF16),
        vmem((ff, dd), BF16),
        vmem(every, F32),
        vmem((NH, 2, 4, tb, ff), BF16),
        vmem((NH, 2, 4, tb, ff), BF16),
        vmem((NH, tb, ff), BF16),
        vmem((NH, tb, ff), BF16),
        vmem((NH, tb, ff), BF16),
        vmem(every, BF16),
        vmem(every, F32),
        vmem(every, F32),
        vmem(every, BF16),
        vmem(every, BF16),
        vmem(every, BF16),
        vmem((dd, ncol * tb), BF16),
        vmem((NZ, NH, NC, th, dd), F32),
        vmem((NZ, NH, th, dd), F32),
        vmem((NZ, NH, th, dd), F32),
        vmem((NZ, NH, th, dd), F32),
        vmem((NX, NY, th, dd), F32),
        vmem((NY, th, dd), F32),
        vmem((NY, th, dd), F32),
        vmem((NY, th, dd), F32),
        vmem((dd, ff), BF16),
        vmem((dd, ff), BF16),
        vmem((ff, dd), BF16),
        dma((COPIES,)),
        dma((COPIES,)),
        dma((NZ,)),
        dma((NZ,)),
        dma((NZ, NH)),
        dma((NY, NX)),
        dma((NY,)),
        dma((NY,)),
        dma((10,)),
    ]
    results = (
        pl.pallas_call(
            kernel,
            out_shape=out,
            in_specs=[anywhere] * 7,
            out_specs=[pl.BlockSpec(memory_space=vmem)] + [anywhere] * 3,
            scratch_shapes=scratch,
            compiler_params=pltpu.CompilerParams(
                collective_id=0, has_side_effects=True, vmem_limit_bytes=56 * 2**20
            ),
            cost_estimate=pl.CostEstimate(
                flops=12 * nrow * NC * th * dd * ff, bytes_accessed=8 * dd * ff * 2, transcendentals=ncol * tb * ff
            ),
        )(tokens, grad_out, gate_pre, up_pre, w_gate, w_up, w_down)
    )
    return tuple(
        pl.pallas_call(
            copy_kernel,
            out_shape=out,
            in_specs=[anywhere] * 4,
            out_specs=[anywhere] * 4,
            scratch_shapes=[vmem(o.shape, o.dtype) for o in out] + [dma((2, 4))],
            compiler_params=pltpu.CompilerParams(vmem_limit_bytes=60 * 2**20),
        )(*results)
    )


def solution(mesh):
    return jax.shard_map(
        on_device,
        mesh=mesh,
        in_specs=(
            P("row", "col"),
            P("row", "col"),
            P("col", "row"),
            P("col", "row"),
            P("col", "row"),
            P("col", "row"),
            P("row", "col"),
        ),
        out_specs=(P("row", "col"), P("col", "row"), P("col", "row"), P("row", "col")),
        check_vma=False,
    )
```

```python
import functools

import jax
import jax.numpy as jnp
from jax import lax
from jax.experimental import pallas as pl
from jax.experimental.pallas import tpu as pltpu
from jax.sharding import PartitionSpec as P

MESH = pl.DeviceIdType.MESH
F32 = jnp.float32
BF16 = jnp.bfloat16
NX, NY, NC = 4, 4, 2
NH, NZ = 2, 8
ROWS = 32
COPIES = 92


def dot(left, right, left_dim, right_dim):
    return lax.dot_general(
        left, right, (((left_dim,), (right_dim,)), ((), ())), preferred_element_type=F32
    )


def kernel(
    tok_ref, go_ref, gate_ref, up_ref, wg_ref, wu_ref, wd_ref,
    out_gt, out_gg, out_gu, out_gd,
    tok_all, go_all, acts, wg, wu, wd, part, rs_send, rs_recv, swap_send, swap_recv,
    grad_h, silu, slope, hidden, gate_grad, up_grad, tok_t, pair_sum, core_send, core_recv,
    x_send, x_recv, x_own, y_send, y_recv, st_gg, st_gu, st_gd,
    send, recv, core_send_sem, core_recv_sem, x_send_sem, x_recv_sem, y_send_sem, y_recv_sem, here,
):
    row, col = lax.axis_index("row"), lax.axis_index("col")
    x, yl, core = row // (NY * NC), (row // NC) % NY, row % NC
    yh, z = col // NZ, col % NZ
    tb, half = acts.shape[3], acts.shape[3] // 2

    def at_row(px, py, pc):
        return (px * (NY * NC) + py * NC + pc, col)

    def at_col(ph, pz):
        return (row, ph * NZ + pz)

    xs = [at_row((x + d) % NX, yl, core) for d in range(1, NX)]
    ys = [at_row(x, (yl + d) % NY, core) for d in range(1, NY)]
    sibling = at_row(x, yl, 1 - core)
    ahead, behind = at_col(yh, (z + 1) % NZ), at_col(yh, (z + NZ - 1) % NZ)
    across = at_col(1 - yh, z)

    sent = []

    def push(src, dst, to):
        n = len(sent)
        copy = pltpu.make_async_remote_copy(
            src_ref=src, dst_ref=dst, send_sem=send.at[n], recv_sem=recv.at[n],
            device_id=to, device_id_type=MESH,
        )
        copy.start()
        sent.append(copy)
        return copy

    def landed(copies):
        for copy in copies:
            copy.wait_recv()

    mine = x * NY + yl
    loads = [
        (go_ref, go_all.at[mine, core]), (tok_ref, tok_all.at[mine, core]),
        (gate_ref, acts.at[0, yh, z]), (up_ref, acts.at[1, yh, z]),
        (wd_ref, wd), (wg_ref, wg), (wu_ref, wu),
    ]
    loads = [pltpu.make_async_copy(s, d, here.at[i]) for i, (s, d) in enumerate(loads)]
    for load in loads:
        load.start()

    barrier = pltpu.get_barrier_semaphore()
    partners = xs + ys + [sibling, ahead, behind, across]
    for to in partners:
        pl.semaphore_signal(barrier, inc=1, device_id=to, device_id_type=MESH)
    pl.semaphore_wait(barrier, len(partners))

    def ring_send(block, k, step, first=None):
        copies = []
        for way, to in ((1, ahead), (-1, behind)):
            at = (z + (NZ - way * (step - 1))) % NZ
            ref = block(k, at)
            if step == NZ // 2:
                ref = ref.at[pl.ds(0 if way == 1 else half, half)]
            copies.append(push(ref if first is None else first, ref, to))
        return copies

    def ring_pass(block, k, step, before):
        landed(before)
        return ring_send(block, k, step)

    def both_pass(block, step, before):
        return [ring_pass(block, k, step, before[k]) for k in range(2)]

    def own_act(k, at):
        return acts.at[k, yh, at]

    def other_act(k, at):
        return acts.at[k, 1 - yh, at]

    def grad_block(k, at):
        return grad_h.at[k, at]

    def pair_loop(m, step):
        if m in (0, NZ // 2):
            step(m)
        else:
            pl.loop(0, 2)(lambda i: step(m + (NZ - 2 * m) * i))

    def activate(h, m):
        def step(o):
            at = (z + o) % NZ

            @pl.loop(0, tb // ROWS)
            def _(i):
                rows = pl.ds(pl.multiple_of(i * ROWS, ROWS), ROWS)
                g = acts[0, h, at, rows].astype(F32)
                u = acts[1, h, at, rows].astype(F32)
                s = jax.nn.sigmoid(g)
                gs = g * s
                silu[h, at, rows] = gs
                slope[h, at, rows] = u * s * (1.0 + g * (1.0 - s))
                hidden[h, at, rows] = (gs * u).astype(BF16)

        pair_loop(m, step)

    def share(m):
        def step(o):
            at = (z + o) % NZ
            rows = jnp.concatenate(
                [go_all[h * NZ + at].reshape(tb, -1) for h in range(NH)], axis=0
            )
            sums = dot(rows, wd[...], 1, 1)
            for h in range(NH):
                part[h, at] = sums[h * tb : (h + 1) * tb]

        pair_loop(m, step)

    def reduce_step(step, before):
        copies = []
        for h in range(NH):
            for w, (way, to) in enumerate(((1, ahead), (-1, behind))):
                at = (z + (NZ + way * (NZ // 2 + 1 - step))) % NZ
                out = rs_send.at[h, w, step - 1]
                rows = pl.ds(0 if way == 1 else half, half)
                if step == 1:
                    out[rows] = part[h, at, rows].astype(BF16)
                    copies.append(push(out.at[rows], rs_recv.at[h, w, 0, rows], to))
                    continue
                before[2 * h + w].wait_recv()
                if step == 2:
                    rest = pl.ds(half if way == 1 else 0, half)
                    out[rows] = (part[h, at, rows] + rs_recv[h, w, 0, rows].astype(F32)).astype(BF16)
                    out[rest] = part[h, at, rest].astype(BF16)
                else:
                    out[...] = (part[h, at] + rs_recv[h, w, step - 2].astype(F32)).astype(BF16)
                copies.append(push(out, rs_recv.at[h, w, step - 1], to))
        return copies

    def spread(own, copies_of, source):
        return [push(source, own, to) for to in copies_of]

    def x_line(ref, px):
        return ref.at[pl.ds(px * NY, NY), core]

    go_own = go_all.at[mine, core]
    go_y = spread(go_own, ys, go_ref)
    go_x = [spread(go_own, xs, go_ref)]
    act1 = [ring_send(own_act, k, 1, first=ref) for k, ref in enumerate((gate_ref, up_ref))]
    tok_y = spread(tok_all.at[mine, core], ys, tok_ref)
    for d in range(1, NY):
        go_y[d - 1].wait_recv()
        block = go_all.at[x * NY + (yl + NY - d) % NY, core]
        go_x.append(spread(block, xs, block))
    act_y = [push(ref, acts.at[k, yh, z], across) for k, ref in enumerate((gate_ref, up_ref))]
    loads[0].wait()
    go_c = [push(x_line(go_all, x), x_line(go_all, x), sibling)]
    loads[2].wait()
    loads[3].wait()
    activate(yh, 0)
    act1 = both_pass(own_act, 2, act1)

    def across_send(*offsets):
        refs = [own_act(k, (z + o) % NZ) for k in range(2) for o in offsets]
        return [push(ref, ref, across) for ref in refs]

    act_near = across_send(1, NZ - 1)
    activate(yh, 1)
    loads[1].wait()
    landed(tok_y)
    act1 = both_pass(own_act, 3, act1)
    for d in (1, 3, 2):
        landed([copies[d - 1] for copies in go_x])
        line = x_line(go_all, (x + NX - d) % NX)
        go_c.append(push(line, line, sibling))
    tok_x = spread(x_line(tok_all, x), xs, x_line(tok_all, x))
    loads[4].wait()
    landed(go_c)

    share(4)
    sums = reduce_step(1, None)
    share(3)
    sums = reduce_step(2, sums)
    share(2)
    landed(tok_x)
    tok_c = push(tok_all.at[:, core], tok_all.at[:, core], sibling)
    activate(yh, 2)
    sums = reduce_step(3, sums)
    share(1)
    share(0)
    sums = reduce_step(4, sums)
    act1 = both_pass(own_act, 4, act1)
    activate(yh, 3)

    swaps = []
    for h in range(NH):
        landed(sums[2 * h : 2 * h + 2])
        total = part[h, z] + rs_recv[h, 0, 3].astype(F32) + rs_recv[h, 1, 3].astype(F32)
        part[h, z] = total
        swap_send[h] = total.astype(BF16)
        swaps.append(push(swap_send.at[h], swap_recv.at[h], across))
    landed(act_y)
    landed(act_near)
    act2 = [ring_send(other_act, k, 2) for k in range(2)]
    for copies in act1:
        landed(copies)
    act_far = across_send(NZ // 2)
    activate(yh, 4)
    activate(1 - yh, 0)
    tok_c.wait_recv()
    tok_t[...] = tok_all[...].reshape(-1, tok_all.shape[3]).T
    act2 = both_pass(other_act, 3, act2)
    activate(1 - yh, 1)
    loads[5].wait()
    loads[6].wait()

    def grad_start(h):
        swaps[h].wait_recv()
        grad_h[h, z] = (part[h, z] + swap_recv[h].astype(F32)).astype(BF16)
        return ring_send(grad_block, h, 1)

    def gradients(m):
        offsets = (m,) if m in (0, NZ // 2) else (m, NZ - m)
        places = [(z + o) % NZ for o in offsets]
        for at in places:
            for h in range(NH):

                @pl.loop(0, tb // ROWS)
                def _(i):
                    rows = pl.ds(pl.multiple_of(i * ROWS, ROWS), ROWS)
                    gh = grad_h[h, at, rows].astype(F32)
                    gate_grad[h, at, rows] = (gh * slope[h, at, rows]).astype(BF16)
                    up_grad[h, at, rows] = (gh * silu[h, at, rows]).astype(BF16)

        def tall(ref):
            return jnp.concatenate([ref[:, at].reshape(NH * tb, -1) for at in places], axis=0)

        sums = dot(tall(gate_grad), wg[...], 1, 1) + dot(tall(up_grad), wu[...], 1, 1)
        for n, o in enumerate(offsets):
            pair_sum[o] = sums[n * NH * tb : (n + 1) * NH * tb].reshape(pair_sum.shape[1:])
            core_send[o] = pair_sum[o, :, 1 - core]
            core_copy(o).start()

    def core_copy(o):
        return pltpu.make_async_remote_copy(
            src_ref=core_send.at[o], dst_ref=core_recv.at[o], send_sem=core_send_sem.at[o],
            recv_sem=core_recv_sem.at[o], device_id=sibling, device_id_type=MESH,
        )

    def x_copy(o, h, to_x, to_y):
        return pltpu.make_async_remote_copy(
            src_ref=x_send.at[o, h], dst_ref=x_recv.at[x, to_y], send_sem=x_send_sem.at[o, h],
            recv_sem=x_recv_sem.at[to_y, x], device_id=at_row(to_x, yl, core), device_id_type=MESH,
        )

    def target(o, h):
        at = h * NZ + (z + o) % NZ
        return at // NY, at % NY

    def outward(m):
        def step(o):
            core_copy(o).wait_recv()
            for h in range(NH):
                to_x, to_y = target(o, h)
                x_send[o, h] = pair_sum[o, h, core] + core_recv[o, h]

                @pl.when(to_x == x)
                def _():
                    x_own[to_y] = x_send[o, h]

                @pl.when(to_x != x)
                def _():
                    x_copy(o, h, to_x, to_y).start()

        pair_loop(m, step)

    def line_sum(to_y):
        total = x_own[to_y]
        for d in range(1, NX):
            src = (x + d) % NX
            pltpu.make_async_remote_copy(
                src_ref=x_send.at[0, 0], dst_ref=x_recv.at[src, to_y], send_sem=x_send_sem.at[0, 0],
                recv_sem=x_recv_sem.at[to_y, src], device_id=sibling, device_id_type=MESH,
            ).wait_recv()
            total = total + x_recv[src, to_y]
        return total

    def y_copy(e, src, to_y):
        return pltpu.make_async_remote_copy(
            src_ref=y_send.at[e], dst_ref=y_recv.at[src], send_sem=y_send_sem.at[e],
            recv_sem=y_recv_sem.at[src], device_id=at_row(x, to_y, core), device_id_type=MESH,
        )

    late = z % NY

    def y_start(e):
        to_y = (late + e) % NY
        y_send[e] = line_sum(to_y)

        @pl.when(to_y != yl)
        def _():
            y_copy(e, yl, to_y).start()

    grads = [grad_start(0)]
    grads.append(grad_start(1))
    activate(1 - yh, 2)
    for copies in act2:
        landed(copies)
    activate(1 - yh, 3)
    gradients(0)
    grads = both_pass(grad_block, 2, grads)
    gradients(1)
    outward(0)
    grads = both_pass(grad_block, 3, grads)
    landed(act_far)
    activate(1 - yh, 4)
    gradients(2)
    outward(1)
    grads = both_pass(grad_block, 4, grads)
    gradients(3)
    outward(2)
    go_flat = go_all[...].reshape(-1, go_all.shape[3])
    width = 256
    for n in range(hidden.shape[3] // width):
        cols = pl.ds(n * width, width)
        st_gd[cols] = dot(hidden[..., cols].reshape(-1, width), go_flat, 0, 0).astype(BF16)
    stores = [pltpu.make_async_copy(st_gd, out_gd, here.at[7])]
    stores[0].start()
    outward(3)
    for copies in grads:
        landed(copies)
    gradients(4)
    for i, (grad, stage, out) in enumerate(((gate_grad, st_gg, out_gg), (up_grad, st_gu, out_gu))):
        for n in range(grad.shape[3] // width):
            cols = pl.ds(n * width, width)
            if i == 0 and n == 1:
                outward(4)
                for e in (2, 1, 3):
                    y_start(e)
            if i == 1 and n == 1:
                y_start(0)
            stage[:, cols] = dot(tok_t[...], grad[..., cols].reshape(-1, width), 1, 0).astype(BF16)
        stores.append(pltpu.make_async_copy(stage, out, here.at[8 + i]))
        stores[-1].start()

    total = y_send[(yl + NY - late) % NY]
    for d in range(1, NY):
        src = (yl + d) % NY
        y_copy(0, src, yl).wait_recv()
        total = total + y_recv[src]
    out_gt[...] = total.astype(BF16)

    for copy in sent:
        copy.wait_send()

    @pl.loop(0, NZ)
    def _(o):
        core_copy(o).wait_send()
        for h in range(NH):
            to_x, to_y = target(o, h)

            @pl.when(to_x != x)
            def _():
                x_copy(o, h, to_x, to_y).wait_send()

    for e in range(NY):
        to_y = (late + e) % NY

        @pl.when(to_y != yl)
        def _():
            y_copy(e, yl, to_y).wait_send()

    for store in stores:
        store.wait()


def copy_kernel(*refs):
    sources, results, held, sems = refs[:4], refs[4:8], refs[8:12], refs[12]
    reads = [pltpu.make_async_copy(s, h, sems.at[0, i]) for i, (s, h) in enumerate(zip(sources, held))]
    writes = [pltpu.make_async_copy(h, r, sems.at[1, i]) for i, (h, r) in enumerate(zip(held, results))]
    for read in reads:
        read.start()
    for read, write in zip(reads, writes):
        read.wait()
        write.start()
    for write in writes:
        write.wait()


def on_device(tokens, grad_out, gate_pre, up_pre, w_gate, w_up, w_down):
    th, dd = tokens.shape
    tb, ff = gate_pre.shape
    nrow, ncol = NX * NY, NH * NZ
    anywhere = pl.BlockSpec(memory_space=pl.ANY)
    vmem = pltpu.VMEM
    dma = pltpu.SemaphoreType.DMA
    out = [
        jax.ShapeDtypeStruct(tokens.shape, BF16),
        jax.ShapeDtypeStruct(w_gate.shape, BF16),
        jax.ShapeDtypeStruct(w_up.shape, BF16),
        jax.ShapeDtypeStruct(w_down.shape, BF16),
    ]
    every = (NH, NZ, tb, ff)
    scratch = [
        vmem((nrow, NC, th, dd), BF16),
        vmem((nrow, NC, th, dd), BF16),
        vmem((2,) + every, BF16),
        vmem((dd, ff), BF16),
        vmem((dd, ff), BF16),
        vmem((ff, dd), BF16),
        vmem(every, F32),
        vmem((NH, 2, 4, tb, ff), BF16),
        vmem((NH, 2, 4, tb, ff), BF16),
        vmem((NH, tb, ff), BF16),
        vmem((NH, tb, ff), BF16),
        vmem(every, BF16),
        vmem(every, F32),
        vmem(every, F32),
        vmem(every, BF16),
        vmem(every, BF16),
        vmem(every, BF16),
        vmem((dd, ncol * tb), BF16),
        vmem((NZ, NH, NC, th, dd), F32),
        vmem((NZ, NH, th, dd), F32),
        vmem((NZ, NH, th, dd), F32),
        vmem((NZ, NH, th, dd), F32),
        vmem((NX, NY, th, dd), F32),
        vmem((NY, th, dd), F32),
        vmem((NY, th, dd), F32),
        vmem((NY, th, dd), F32),
        vmem((dd, ff), BF16),
        vmem((dd, ff), BF16),
        vmem((ff, dd), BF16),
        dma((COPIES,)),
        dma((COPIES,)),
        dma((NZ,)),
        dma((NZ,)),
        dma((NZ, NH)),
        dma((NY, NX)),
        dma((NY,)),
        dma((NY,)),
        dma((10,)),
    ]
    results = (
        pl.pallas_call(
            kernel,
            out_shape=out,
            in_specs=[anywhere] * 7,
            out_specs=[pl.BlockSpec(memory_space=vmem)] + [anywhere] * 3,
            scratch_shapes=scratch,
            compiler_params=pltpu.CompilerParams(
                collective_id=0, has_side_effects=True, vmem_limit_bytes=56 * 2**20
            ),
            cost_estimate=pl.CostEstimate(
                flops=12 * nrow * NC * th * dd * ff, bytes_accessed=8 * dd * ff * 2, transcendentals=ncol * tb * ff
            ),
        )(tokens, grad_out, gate_pre, up_pre, w_gate, w_up, w_down)
    )
    return tuple(
        pl.pallas_call(
            copy_kernel,
            out_shape=out,
            in_specs=[anywhere] * 4,
            out_specs=[anywhere] * 4,
            scratch_shapes=[vmem(o.shape, o.dtype) for o in out] + [dma((2, 4))],
            compiler_params=pltpu.CompilerParams(vmem_limit_bytes=60 * 2**20),
        )(*results)
    )


def solution(mesh):
    return jax.shard_map(
        on_device,
        mesh=mesh,
        in_specs=(
            P("row", "col"),
            P("row", "col"),
            P("col", "row"),
            P("col", "row"),
            P("col", "row"),
            P("col", "row"),
            P("row", "col"),
        ),
        out_specs=(P("row", "col"), P("col", "row"), P("col", "row"), P("row", "col")),
        check_vma=False,
    )
```

```python
import functools

import jax
import jax.numpy as jnp
from jax import lax
from jax.experimental import pallas as pl
from jax.experimental.pallas import tpu as pltpu
from jax.sharding import PartitionSpec as P

MESH = pl.DeviceIdType.MESH
F32 = jnp.float32
BF16 = jnp.bfloat16
NX, NY, NC = 4, 4, 2
NH, NZ = 2, 8
ROWS = 32
COPIES = 82
ORDER = (
    ("a", 1, 0, 1), ("a", 1, 1, 1), ("goy",), ("toky",), ("gox",), ("a", 1, 0, 2), ("a", 1, 1, 2), ("tokx",),
    ("acty",), ("a", 1, 0, 3), ("a", 1, 1, 3), ("goc",), ("a", 1, 0, 4), ("a", 1, 1, 4), ("S", 4),
    ("r", 0, 1), ("r", 1, 1), ("S", 3), ("tokc",), ("r", 0, 2), ("r", 1, 2), ("S", 2), ("A", 1, 0),
    ("A", 1, 1), ("r", 0, 3), ("r", 1, 3), ("S", 1), ("S", 0), ("A", 1, 2), ("r", 0, 4), ("r", 1, 4),
    ("a", 2, 0, 1), ("a", 2, 1, 1), ("A", 1, 3), ("A", 1, 4), ("w", 0), ("w", 1), ("T",), ("a", 2, 0, 2),
    ("a", 2, 1, 2), ("A", 2, 0), ("g", 0, 1), ("g", 1, 1), ("a", 2, 0, 3), ("a", 2, 1, 3), ("A", 2, 1),
    ("g", 0, 2), ("g", 1, 2), ("G", 0), ("a", 2, 0, 4), ("a", 2, 1, 4), ("A", 2, 2), ("G", 1), ("g", 0, 3),
    ("g", 1, 3), ("A", 2, 3), ("O", 0), ("O", 1), ("G", 2), ("A", 2, 4), ("g", 0, 4), ("g", 1, 4), ("O", 2),
    ("G", 3), ("D",), ("O", 3), ("G", 4),
)


def dot(left, right, left_dim, right_dim):
    return lax.dot_general(
        left, right, (((left_dim,), (right_dim,)), ((), ())), preferred_element_type=F32
    )


def kernel(
    tok_ref, go_ref, gate_ref, up_ref, wg_ref, wu_ref, wd_ref,
    out_gt, out_gg, out_gu, out_gd,
    tok_all, go_all, acts, wg, wu, wd, part, rs_send, rs_recv, swap_send, swap_recv,
    grad_h, silu, slope, hidden, gate_grad, up_grad, tok_t, pair_sum, core_send, core_recv,
    x_send, x_recv, x_late_send, x_late_recv, x_own, y_send, y_recv, y_late_send, y_late_recv, st_gg, st_gu, st_gd,
    send, recv, core_send_sem, core_recv_sem, x_send_sem, x_recv_sem, y_send_sem, y_recv_sem, here,
):
    row, col = lax.axis_index("row"), lax.axis_index("col")
    x, yl, core = row // (NY * NC), (row // NC) % NY, row % NC
    yh, z = col // NZ, col % NZ
    tb, half = acts.shape[3], acts.shape[3] // 2

    def at_row(px, py, pc):
        return (px * (NY * NC) + py * NC + pc, col)

    def at_col(ph, pz):
        return (row, ph * NZ + pz)

    xs = [at_row((x + d) % NX, yl, core) for d in range(1, NX)]
    ys = [at_row(x, (yl + d) % NY, core) for d in range(1, NY)]
    sibling = at_row(x, yl, 1 - core)
    ahead, behind = at_col(yh, (z + 1) % NZ), at_col(yh, (z + NZ - 1) % NZ)
    across = at_col(1 - yh, z)

    sent = []
    coming = {}

    def push(src, dst, to):
        n = len(sent)
        copy = pltpu.make_async_remote_copy(
            src_ref=src, dst_ref=dst, send_sem=send.at[n], recv_sem=recv.at[n],
            device_id=to, device_id_type=MESH,
        )
        copy.start()
        sent.append(copy)
        return copy

    def arrive(*key):
        for copy in coming[key]:
            copy.wait_recv()
        coming[key] = ()

    def loaded(*which):
        for i in which:
            if loads[i] is not None:
                loads[i].wait()
                loads[i] = None

    mine = x * NY + yl
    loads = [
        (go_ref, go_all.at[mine, core]), (tok_ref, tok_all.at[mine, core]),
        (gate_ref, acts.at[0, yh, z]), (up_ref, acts.at[1, yh, z]),
        (wd_ref, wd), (wg_ref, wg), (wu_ref, wu),
    ]
    loads = [pltpu.make_async_copy(s, d, here.at[i]) for i, (s, d) in enumerate(loads)]
    for load in loads:
        load.start()

    barrier = pltpu.get_barrier_semaphore()
    partners = xs + ys + [sibling, ahead, behind, across]
    for to in partners:
        pl.semaphore_signal(barrier, inc=1, device_id=to, device_id_type=MESH)
    pl.semaphore_wait(barrier, len(partners))

    def ring_send(block, k, step, first=None):
        copies = []
        for way, to in ((1, ahead), (-1, behind)):
            at = (z + (NZ - way * (step - 1))) % NZ
            ref = block(k, at)
            if step == NZ // 2:
                ref = ref.at[pl.ds(0 if way == 1 else half, half)]
            copies.append(push(ref if first is None else first, ref, to))
        return copies

    def own_act(k, at):
        return acts.at[k, yh, at]

    def other_act(k, at):
        return acts.at[k, 1 - yh, at]

    def grad_block(k, at):
        return grad_h.at[k, at]

    def pair_loop(m, step):
        if m in (0, NZ // 2):
            step(m)
        else:
            pl.loop(0, 2)(lambda i: step(m + (NZ - 2 * m) * i))

    def activate(ring, m):
        h = yh if ring == 1 else 1 - yh
        if m == 0 and ring == 1:
            loaded(2, 3)
        elif m == 0:
            arrive("act_y")
        else:
            arrive("act", ring, 0, m)
            arrive("act", ring, 1, m)

        def step(o):
            at = (z + o) % NZ

            @pl.loop(0, tb // ROWS)
            def _(i):
                rows = pl.ds(pl.multiple_of(i * ROWS, ROWS), ROWS)
                g = acts[0, h, at, rows].astype(F32)
                u = acts[1, h, at, rows].astype(F32)
                s = jax.nn.sigmoid(g)
                gs = g * s
                silu[h, at, rows] = gs
                slope[h, at, rows] = u * s * (1.0 + g * (1.0 - s))
                hidden[h, at, rows] = (gs * u).astype(BF16)

        pair_loop(m, step)

    def share(m):
        arrive("go_core")
        loaded(4)

        def step(o):
            at = (z + o) % NZ
            rows = jnp.concatenate(
                [go_all[h * NZ + at].reshape(tb, -1) for h in range(NH)], axis=0
            )
            sums = dot(rows, wd[...], 1, 1)
            for h in range(NH):
                part[h, at] = sums[h * tb : (h + 1) * tb]

        pair_loop(m, step)

    def reduce_step(h, step):
        copies = []
        for w, (way, to) in enumerate(((1, ahead), (-1, behind))):
            at = (z + (NZ + way * (NZ // 2 + 1 - step))) % NZ
            out = rs_send.at[h, w, step - 1]
            rows = pl.ds(0 if way == 1 else half, half)
            if step == 1:
                out[rows] = part[h, at, rows].astype(BF16)
                copies.append(push(out.at[rows], rs_recv.at[h, w, 0, rows], to))
                continue
            coming["sums", h, step - 1][w].wait_recv()
            if step == 2:
                rest = pl.ds(half if way == 1 else 0, half)
                out[rows] = (part[h, at, rows] + rs_recv[h, w, 0, rows].astype(F32)).astype(BF16)
                out[rest] = part[h, at, rest].astype(BF16)
            else:
                out[...] = (part[h, at] + rs_recv[h, w, step - 2].astype(F32)).astype(BF16)
            copies.append(push(out, rs_recv.at[h, w, step - 1], to))
        coming["sums", h, step] = copies

    def spread(own, copies_of, source):
        return [push(source, own, to) for to in copies_of]

    def x_line(ref):
        return ref.at[pl.ds(x * NY, NY), core]

    def go_along_y():
        coming[("go_y",)] = spread(go_all.at[mine, core], ys, go_ref)

    def go_along_x():
        loaded(0)
        arrive("go_y")
        coming[("go_x",)] = spread(x_line(go_all), xs, x_line(go_all))

    def go_to_core():
        arrive("go_x")
        coming[("go_core",)] = [push(go_all.at[:, core], go_all.at[:, core], sibling)]

    def tok_along_y():
        coming[("tok_y",)] = spread(tok_all.at[mine, core], ys, tok_ref)

    def tok_along_x():
        loaded(1)
        arrive("tok_y")
        coming[("tok_x",)] = spread(x_line(tok_all), xs, x_line(tok_all))

    def tok_to_core():
        arrive("tok_x")
        coming[("tok_core",)] = [push(tok_all.at[:, core], tok_all.at[:, core], sibling)]

    def tok_turn():
        arrive("tok_core")
        tok_t[...] = tok_all[...].reshape(-1, tok_all.shape[3]).T

    def act_across():
        refs = enumerate((gate_ref, up_ref))
        coming[("act_y",)] = [push(ref, acts.at[k, yh, z], across) for k, ref in refs]

    def act_ring(ring, k, step):
        first = None
        if step > 1:
            arrive("act", ring, k, step - 1)
        elif ring == 1:
            first = (gate_ref, up_ref)[k]
        else:
            arrive("act_y")
        coming["act", ring, k, step] = ring_send(own_act if ring == 1 else other_act, k, step, first)

    def swap(h):
        arrive("sums", h, 4)
        total = part[h, z] + rs_recv[h, 0, 3].astype(F32) + rs_recv[h, 1, 3].astype(F32)
        part[h, z] = total
        swap_send[h] = total.astype(BF16)
        coming["swap", h] = [push(swap_send.at[h], swap_recv.at[h], across)]

    def grad_ring(h, step):
        if step == 1:
            arrive("swap", h)
            grad_h[h, z] = (part[h, z] + swap_recv[h].astype(F32)).astype(BF16)
        else:
            arrive("grad", h, step - 1)
        coming["grad", h, step] = ring_send(grad_block, h, step)

    def gradients(m):
        offsets = (m,) if m in (0, NZ // 2) else (m, NZ - m)
        places = [(z + o) % NZ for o in offsets]
        loaded(5, 6)
        for h in range(NH):
            if m > 0:
                arrive("grad", h, m)
        for at in places:
            for h in range(NH):

                @pl.loop(0, tb // ROWS)
                def _(i):
                    rows = pl.ds(pl.multiple_of(i * ROWS, ROWS), ROWS)
                    gh = grad_h[h, at, rows].astype(F32)
                    gate_grad[h, at, rows] = (gh * slope[h, at, rows]).astype(BF16)
                    up_grad[h, at, rows] = (gh * silu[h, at, rows]).astype(BF16)

        def tall(ref):
            return jnp.concatenate([ref[:, at].reshape(NH * tb, -1) for at in places], axis=0)

        sums = dot(tall(gate_grad), wg[...], 1, 1) + dot(tall(up_grad), wu[...], 1, 1)
        for n, o in enumerate(offsets):
            pair_sum[o] = sums[n * NH * tb : (n + 1) * NH * tb].reshape(pair_sum.shape[1:])
            core_send[o] = pair_sum[o, :, 1 - core]
            core_copy(o).start()

    def core_copy(o):
        return pltpu.make_async_remote_copy(
            src_ref=core_send.at[o], dst_ref=core_recv.at[o], send_sem=core_send_sem.at[o],
            recv_sem=core_recv_sem.at[o], device_id=sibling, device_id_type=MESH,
        )

    late = z % NY

    def is_late(o):
        return o in (0, NZ // 2)

    def x_copy(o, h, to_x, to_y):
        if is_late(o):
            src, dst = x_late_send.at[o // (NZ // 2), h], x_late_recv.at[x]
        else:
            src, dst = x_send.at[o, h], x_recv.at[x, to_y]
        return pltpu.make_async_remote_copy(
            src_ref=src, dst_ref=dst, send_sem=x_send_sem.at[o, h],
            recv_sem=x_recv_sem.at[to_y, x], device_id=at_row(to_x, yl, core), device_id_type=MESH,
        )

    def target(o, h):
        at = h * NZ + (z + o) % NZ
        return at // NY, at % NY

    def outward(m):
        for o in (m,) if is_late(m) else (m, NZ - m):
            core_copy(o).wait_recv()
            for h in range(NH):
                to_x, to_y = target(o, h)
                total = pair_sum[o, h, core] + core_recv[o, h]
                if is_late(o):
                    x_late_send[o // (NZ // 2), h] = total.astype(BF16)
                x_send[o, h] = total

                @pl.when(to_x == x)
                def _():
                    x_own[to_y] = x_send[o, h]

                @pl.when(to_x != x)
                def _():
                    x_copy(o, h, to_x, to_y).start()

    def line_sum(to_y, last):
        total = x_own[to_y]
        for d in range(1, NX):
            src = (x + d) % NX
            dst = x_late_recv.at[src] if last else x_recv.at[src, to_y]
            pltpu.make_async_remote_copy(
                src_ref=dst, dst_ref=dst, send_sem=x_send_sem.at[0, 0],
                recv_sem=x_recv_sem.at[to_y, src], device_id=sibling, device_id_type=MESH,
            ).wait_recv()
            total = total + dst[...].astype(F32)
        return total

    def y_copy(e, src, to_y):
        return pltpu.make_async_remote_copy(
            src_ref=y_late_send if e == 0 else y_send.at[e],
            dst_ref=y_late_recv.at[src] if e == 0 else y_recv.at[src], send_sem=y_send_sem.at[e],
            recv_sem=y_recv_sem.at[src], device_id=at_row(x, to_y, core), device_id_type=MESH,
        )

    def y_start(e):
        to_y = (late + e) % NY
        total = line_sum(to_y, e == 0)
        y_send[e] = total
        if e == 0:
            y_late_send[...] = total.astype(BF16)

        @pl.when(to_y != yl)
        def _():
            y_copy(e, yl, to_y).start()

    width = 256
    stores = []

    def keep(stage, out):
        stores.append(pltpu.make_async_copy(stage, out, here.at[7 + len(stores)]))
        stores[-1].start()

    def down_grads():
        go_flat = go_all[...].reshape(-1, go_all.shape[3])
        for n in range(hidden.shape[3] // width):
            cols = pl.ds(n * width, width)
            st_gd[cols] = dot(hidden[..., cols].reshape(-1, width), go_flat, 0, 0).astype(BF16)
        keep(st_gd, out_gd)

    ops = {
        "goy": go_along_y, "gox": go_along_x, "goc": go_to_core,
        "toky": tok_along_y, "tokx": tok_along_x, "tokc": tok_to_core, "T": tok_turn,
        "acty": act_across, "a": act_ring, "A": activate, "S": share, "r": reduce_step,
        "w": swap, "g": grad_ring, "G": gradients, "O": outward, "D": down_grads,
    }
    for op, *at in ORDER:
        ops[op](*at)

    for i, (grad, stage, out) in enumerate(((gate_grad, st_gg, out_gg), (up_grad, st_gu, out_gu))):
        for n in range(grad.shape[3] // width):
            cols = pl.ds(n * width, width)
            if i == 0 and n == 1:
                outward(4)
                for e in (2, 1, 3):
                    y_start(e)
            if i == 1 and n == 0:
                y_start(0)
            stage[:, cols] = dot(tok_t[...], grad[..., cols].reshape(-1, width), 1, 0).astype(BF16)
        keep(stage, out)

    others = [(yl + d) % NY for d in range(1, NY)]

    @pl.when(yl == late)
    def _():
        total = y_send[0]
        for src in others:
            y_copy(0, src, yl).wait_recv()
            total = total + y_late_recv[src].astype(F32)
        out_gt[...] = total.astype(BF16)

    @pl.when(yl != late)
    def _():
        total = y_send[(yl + NY - late) % NY]
        for src in others:
            y_copy(1, src, yl).wait_recv()
            total = total + y_recv[src]
        out_gt[...] = total.astype(BF16)

    for copy in sent:
        copy.wait_send()

    for o in range(NZ):
        core_copy(o).wait_send()
        for h in range(NH):
            to_x, to_y = target(o, h)

            @pl.when(to_x != x)
            def _():
                x_copy(o, h, to_x, to_y).wait_send()

    for e in range(NY):
        to_y = (late + e) % NY

        @pl.when(to_y != yl)
        def _():
            y_copy(e, yl, to_y).wait_send()

    for store in stores:
        store.wait()


def copy_kernel(*refs):
    sources, results, held, sems = refs[:4], refs[4:8], refs[8:12], refs[12]
    reads = [pltpu.make_async_copy(s, h, sems.at[0, i]) for i, (s, h) in enumerate(zip(sources, held))]
    writes = [pltpu.make_async_copy(h, r, sems.at[1, i]) for i, (h, r) in enumerate(zip(held, results))]
    for read in reads:
        read.start()
    for read, write in zip(reads, writes):
        read.wait()
        write.start()
    for write in writes:
        write.wait()


def on_device(tokens, grad_out, gate_pre, up_pre, w_gate, w_up, w_down):
    th, dd = tokens.shape
    tb, ff = gate_pre.shape
    nrow, ncol = NX * NY, NH * NZ
    anywhere = pl.BlockSpec(memory_space=pl.ANY)
    vmem = pltpu.VMEM
    dma = pltpu.SemaphoreType.DMA
    out = [
        jax.ShapeDtypeStruct(tokens.shape, BF16),
        jax.ShapeDtypeStruct(w_gate.shape, BF16),
        jax.ShapeDtypeStruct(w_up.shape, BF16),
        jax.ShapeDtypeStruct(w_down.shape, BF16),
    ]
    every = (NH, NZ, tb, ff)
    scratch = [
        vmem((nrow, NC, th, dd), BF16),
        vmem((nrow, NC, th, dd), BF16),
        vmem((2,) + every, BF16),
        vmem((dd, ff), BF16),
        vmem((dd, ff), BF16),
        vmem((ff, dd), BF16),
        vmem(every, F32),
        vmem((NH, 2, 4, tb, ff), BF16),
        vmem((NH, 2, 4, tb, ff), BF16),
        vmem((NH, tb, ff), BF16),
        vmem((NH, tb, ff), BF16),
        vmem(every, BF16),
        vmem(every, F32),
        vmem(every, F32),
        vmem(every, BF16),
        vmem(every, BF16),
        vmem(every, BF16),
        vmem((dd, ncol * tb), BF16),
        vmem((NZ, NH, NC, th, dd), F32),
        vmem((NZ, NH, th, dd), F32),
        vmem((NZ, NH, th, dd), F32),
        vmem((NZ, NH, th, dd), F32),
        vmem((NX, NY, th, dd), F32),
        vmem((2, NH, th, dd), BF16),
        vmem((NX, th, dd), BF16),
        vmem((NY, th, dd), F32),
        vmem((NY, th, dd), F32),
        vmem((NY, th, dd), F32),
        vmem((th, dd), BF16),
        vmem((NY, th, dd), BF16),
        vmem((dd, ff), BF16),
        vmem((dd, ff), BF16),
        vmem((ff, dd), BF16),
        dma((COPIES,)),
        dma((COPIES,)),
        dma((NZ,)),
        dma((NZ,)),
        dma((NZ, NH)),
        dma((NY, NX)),
        dma((NY,)),
        dma((NY,)),
        dma((10,)),
    ]
    results = (
        pl.pallas_call(
            kernel,
            out_shape=out,
            in_specs=[anywhere] * 7,
            out_specs=[pl.BlockSpec(memory_space=vmem)] + [anywhere] * 3,
            scratch_shapes=scratch,
            compiler_params=pltpu.CompilerParams(
                collective_id=0, has_side_effects=True, vmem_limit_bytes=56 * 2**20
            ),
            cost_estimate=pl.CostEstimate(
                flops=12 * nrow * NC * th * dd * ff, bytes_accessed=8 * dd * ff * 2, transcendentals=ncol * tb * ff
            ),
        )(tokens, grad_out, gate_pre, up_pre, w_gate, w_up, w_down)
    )
    return tuple(
        pl.pallas_call(
            copy_kernel,
            out_shape=out,
            in_specs=[anywhere] * 4,
            out_specs=[anywhere] * 4,
            scratch_shapes=[vmem(o.shape, o.dtype) for o in out] + [dma((2, 4))],
            compiler_params=pltpu.CompilerParams(vmem_limit_bytes=60 * 2**20),
        )(*results)
    )


def solution(mesh):
    return jax.shard_map(
        on_device,
        mesh=mesh,
        in_specs=(
            P("row", "col"),
            P("row", "col"),
            P("col", "row"),
            P("col", "row"),
            P("col", "row"),
            P("col", "row"),
            P("row", "col"),
        ),
        out_specs=(P("row", "col"), P("col", "row"), P("col", "row"), P("row", "col")),
        check_vma=False,
    )
```

```python
import functools

import jax
import jax.numpy as jnp
from jax import lax
from jax.experimental import pallas as pl
from jax.experimental.pallas import tpu as pltpu
from jax.sharding import PartitionSpec as P

MESH = pl.DeviceIdType.MESH
F32 = jnp.float32
BF16 = jnp.bfloat16
NX, NY, NC = 4, 4, 2
NH, NZ = 2, 8
ROWS = 32
COPIES = 82
ORDER = (
    ("goy",), ("a", 1, 1, 1), ("toky",), ("a", 1, 0, 1), ("gox",), ("a", 1, 1, 2), ("acty",), ("a", 1, 0, 2),
    ("a", 1, 1, 3), ("goc",), ("a", 1, 0, 3), ("a", 1, 1, 4), ("S", 4), ("r", 1, 1), ("a", 1, 0, 4),
    ("r", 0, 1), ("tokx",), ("S", 3), ("r", 1, 2), ("r", 0, 2), ("S", 2), ("r", 1, 3), ("S", 1), ("tokc",),
    ("r", 0, 3), ("r", 1, 4), ("A", 1, 4), ("r", 0, 4), ("S", 0), ("A", 2, 0), ("a", 2, 1, 1), ("w", 1),
    ("a", 2, 0, 1), ("w", 0), ("A", 1, 2), ("a", 2, 1, 2), ("a", 2, 0, 2), ("g", 1, 1), ("A", 2, 1),
    ("A", 1, 0), ("a", 2, 1, 3), ("A", 1, 1), ("T",), ("g", 0, 1), ("G", 0), ("g", 1, 2), ("A", 1, 3),
    ("A", 2, 2), ("g", 0, 2), ("a", 2, 0, 3), ("G", 1), ("g", 1, 3), ("O", 0), ("g", 0, 3), ("G", 2),
    ("a", 2, 0, 4), ("a", 2, 1, 4), ("O", 1), ("A", 2, 3), ("g", 1, 4), ("O", 2), ("G", 3), ("g", 0, 4),
    ("A", 2, 4), ("D",), ("O", 3), ("G", 4),
)


def dot(left, right, left_dim, right_dim):
    return lax.dot_general(
        left, right, (((left_dim,), (right_dim,)), ((), ())), preferred_element_type=F32
    )


def kernel(
    tok_ref, go_ref, gate_ref, up_ref, wg_ref, wu_ref, wd_ref,
    out_gt, out_gg, out_gu, out_gd,
    tok_all, go_all, acts, wg, wu, wd, part, rs_send, rs_recv, swap_send, swap_recv,
    grad_h, silu, slope, hidden, gate_grad, up_grad, tok_t, pair_sum, core_send, core_recv,
    x_send, x_recv, x_late_send, x_late_recv, x_own, y_send, y_recv, y_late_send, y_late_recv, st_gg, st_gu, st_gd,
    send, recv, core_send_sem, core_recv_sem, x_send_sem, x_recv_sem, y_send_sem, y_recv_sem, here,
):
    row, col = lax.axis_index("row"), lax.axis_index("col")
    x, yl, core = row // (NY * NC), (row // NC) % NY, row % NC
    yh, z = col // NZ, col % NZ
    tb, half = acts.shape[3], acts.shape[3] // 2

    def at_row(px, py, pc):
        return (px * (NY * NC) + py * NC + pc, col)

    def at_col(ph, pz):
        return (row, ph * NZ + pz)

    xs = [at_row((x + d) % NX, yl, core) for d in range(1, NX)]
    ys = [at_row(x, (yl + d) % NY, core) for d in range(1, NY)]
    sibling = at_row(x, yl, 1 - core)
    ahead, behind = at_col(yh, (z + 1) % NZ), at_col(yh, (z + NZ - 1) % NZ)
    across = at_col(1 - yh, z)

    sent = []
    coming = {}

    def push(src, dst, to):
        n = len(sent)
        copy = pltpu.make_async_remote_copy(
            src_ref=src, dst_ref=dst, send_sem=send.at[n], recv_sem=recv.at[n],
            device_id=to, device_id_type=MESH,
        )
        copy.start()
        sent.append(copy)
        return copy

    def arrive(*key):
        for copy in coming[key]:
            copy.wait_recv()
        coming[key] = ()

    def loaded(*which):
        for i in which:
            if loads[i] is not None:
                loads[i].wait()
                loads[i] = None

    mine = x * NY + yl
    loads = [
        (go_ref, go_all.at[mine, core]), (tok_ref, tok_all.at[mine, core]),
        (gate_ref, acts.at[0, yh, z]), (up_ref, acts.at[1, yh, z]),
        (wd_ref, wd), (wg_ref, wg), (wu_ref, wu),
    ]
    loads = [pltpu.make_async_copy(s, d, here.at[i]) for i, (s, d) in enumerate(loads)]
    for load in loads:
        load.start()

    barrier = pltpu.get_barrier_semaphore()
    partners = xs + ys + [sibling, ahead, behind, across]
    for to in partners:
        pl.semaphore_signal(barrier, inc=1, device_id=to, device_id_type=MESH)
    pl.semaphore_wait(barrier, len(partners))

    def ring_send(block, k, step, first=None):
        copies = []
        for way, to in ((1, ahead), (-1, behind)):
            at = (z + (NZ - way * (step - 1))) % NZ
            ref = block(k, at)
            if step == NZ // 2:
                ref = ref.at[pl.ds(0 if way == 1 else half, half)]
            copies.append(push(ref if first is None else first, ref, to))
        return copies

    def own_act(k, at):
        return acts.at[k, yh, at]

    def other_act(k, at):
        return acts.at[k, 1 - yh, at]

    def grad_block(k, at):
        return grad_h.at[k, at]

    def pair_loop(m, step):
        if m in (0, NZ // 2):
            step(m)
        else:
            pl.loop(0, 2)(lambda i: step(m + (NZ - 2 * m) * i))

    def activate(ring, m):
        h = yh if ring == 1 else 1 - yh
        if m == 0 and ring == 1:
            loaded(2, 3)
        elif m == 0:
            arrive("act_y")
        else:
            arrive("act", ring, 0, m)
            arrive("act", ring, 1, m)

        def step(o):
            at = (z + o) % NZ

            @pl.loop(0, tb // ROWS)
            def _(i):
                rows = pl.ds(pl.multiple_of(i * ROWS, ROWS), ROWS)
                g = acts[0, h, at, rows].astype(F32)
                u = acts[1, h, at, rows].astype(F32)
                s = jax.nn.sigmoid(g)
                gs = g * s
                silu[h, at, rows] = gs
                slope[h, at, rows] = u * s * (1.0 + g * (1.0 - s))
                hidden[h, at, rows] = (gs * u).astype(BF16)

        pair_loop(m, step)

    def share(m):
        arrive("go_core")
        loaded(4)

        def step(o):
            at = (z + o) % NZ
            rows = jnp.concatenate(
                [go_all[h * NZ + at].reshape(tb, -1) for h in range(NH)], axis=0
            )
            sums = dot(rows, wd[...], 1, 1)
            for h in range(NH):
                part[h, at] = sums[h * tb : (h + 1) * tb]

        pair_loop(m, step)

    def reduce_step(h, step):
        copies = []
        for w, (way, to) in enumerate(((1, ahead), (-1, behind))):
            at = (z + (NZ + way * (NZ // 2 + 1 - step))) % NZ
            out = rs_send.at[h, w, step - 1]
            rows = pl.ds(0 if way == 1 else half, half)
            if step == 1:
                out[rows] = part[h, at, rows].astype(BF16)
                copies.append(push(out.at[rows], rs_recv.at[h, w, 0, rows], to))
                continue
            coming["sums", h, step - 1][w].wait_recv()
            if step == 2:
                rest = pl.ds(half if way == 1 else 0, half)
                out[rows] = (part[h, at, rows] + rs_recv[h, w, 0, rows].astype(F32)).astype(BF16)
                out[rest] = part[h, at, rest].astype(BF16)
            else:
                out[...] = (part[h, at] + rs_recv[h, w, step - 2].astype(F32)).astype(BF16)
            copies.append(push(out, rs_recv.at[h, w, step - 1], to))
        coming["sums", h, step] = copies

    def spread(own, copies_of, source):
        return [push(source, own, to) for to in copies_of]

    def x_line(ref):
        return ref.at[pl.ds(x * NY, NY), core]

    def go_along_y():
        coming[("go_y",)] = spread(go_all.at[mine, core], ys, go_ref)

    def go_along_x():
        loaded(0)
        arrive("go_y")
        coming[("go_x",)] = spread(x_line(go_all), xs, x_line(go_all))

    def go_to_core():
        arrive("go_x")
        coming[("go_core",)] = [push(go_all.at[:, core], go_all.at[:, core], sibling)]

    def tok_along_y():
        coming[("tok_y",)] = spread(tok_all.at[mine, core], ys, tok_ref)

    def tok_along_x():
        loaded(1)
        arrive("tok_y")
        coming[("tok_x",)] = spread(x_line(tok_all), xs, x_line(tok_all))

    def tok_to_core():
        arrive("tok_x")
        coming[("tok_core",)] = [push(tok_all.at[:, core], tok_all.at[:, core], sibling)]

    def tok_turn():
        arrive("tok_core")
        tok_t[...] = tok_all[...].reshape(-1, tok_all.shape[3]).T

    def act_across():
        refs = enumerate((gate_ref, up_ref))
        coming[("act_y",)] = [push(ref, acts.at[k, yh, z], across) for k, ref in refs]

    def act_ring(ring, k, step):
        first = None
        if step > 1:
            arrive("act", ring, k, step - 1)
        elif ring == 1:
            first = (gate_ref, up_ref)[k]
        else:
            arrive("act_y")
        coming["act", ring, k, step] = ring_send(own_act if ring == 1 else other_act, k, step, first)

    def swap(h):
        arrive("sums", h, 4)
        total = part[h, z] + rs_recv[h, 0, 3].astype(F32) + rs_recv[h, 1, 3].astype(F32)
        part[h, z] = total
        swap_send[h] = total.astype(BF16)
        coming["swap", h] = [push(swap_send.at[h], swap_recv.at[h], across)]

    def grad_ring(h, step):
        if step == 1:
            arrive("swap", h)
            grad_h[h, z] = (part[h, z] + swap_recv[h].astype(F32)).astype(BF16)
        else:
            arrive("grad", h, step - 1)
        coming["grad", h, step] = ring_send(grad_block, h, step)

    def gradients(m):
        offsets = (m,) if m in (0, NZ // 2) else (m, NZ - m)
        places = [(z + o) % NZ for o in offsets]
        loaded(5, 6)
        for h in range(NH):
            if m > 0:
                arrive("grad", h, m)
        for at in places:
            for h in range(NH):

                @pl.loop(0, tb // ROWS)
                def _(i):
                    rows = pl.ds(pl.multiple_of(i * ROWS, ROWS), ROWS)
                    gh = grad_h[h, at, rows].astype(F32)
                    gate_grad[h, at, rows] = (gh * slope[h, at, rows]).astype(BF16)
                    up_grad[h, at, rows] = (gh * silu[h, at, rows]).astype(BF16)

        def tall(ref):
            return jnp.concatenate([ref[:, at].reshape(NH * tb, -1) for at in places], axis=0)

        sums = dot(tall(gate_grad), wg[...], 1, 1) + dot(tall(up_grad), wu[...], 1, 1)
        for n, o in enumerate(offsets):
            pair_sum[o] = sums[n * NH * tb : (n + 1) * NH * tb].reshape(pair_sum.shape[1:])
            core_send[o] = pair_sum[o, :, 1 - core]
            core_copy(o).start()

    def core_copy(o):
        return pltpu.make_async_remote_copy(
            src_ref=core_send.at[o], dst_ref=core_recv.at[o], send_sem=core_send_sem.at[o],
            recv_sem=core_recv_sem.at[o], device_id=sibling, device_id_type=MESH,
        )

    late = z % NY

    def is_late(o):
        return o in (0, NZ // 2)

    def x_copy(o, h, to_x, to_y):
        if is_late(o):
            src, dst = x_late_send.at[o // (NZ // 2), h], x_late_recv.at[x]
        else:
            src, dst = x_send.at[o, h], x_recv.at[x, to_y]
        return pltpu.make_async_remote_copy(
            src_ref=src, dst_ref=dst, send_sem=x_send_sem.at[o, h],
            recv_sem=x_recv_sem.at[to_y, x], device_id=at_row(to_x, yl, core), device_id_type=MESH,
        )

    def target(o, h):
        at = h * NZ + (z + o) % NZ
        return at // NY, at % NY

    def outward(m):
        for o in (m,) if is_late(m) else (m, NZ - m):
            core_copy(o).wait_recv()
            for h in range(NH):
                to_x, to_y = target(o, h)
                total = pair_sum[o, h, core] + core_recv[o, h]
                if is_late(o):
                    x_late_send[o // (NZ // 2), h] = total.astype(BF16)
                x_send[o, h] = total

                @pl.when(to_x == x)
                def _():
                    x_own[to_y] = x_send[o, h]

                @pl.when(to_x != x)
                def _():
                    x_copy(o, h, to_x, to_y).start()

    def line_sum(to_y, last):
        total = x_own[to_y]
        for d in range(1, NX):
            src = (x + d) % NX
            dst = x_late_recv.at[src] if last else x_recv.at[src, to_y]
            pltpu.make_async_remote_copy(
                src_ref=dst, dst_ref=dst, send_sem=x_send_sem.at[0, 0],
                recv_sem=x_recv_sem.at[to_y, src], device_id=sibling, device_id_type=MESH,
            ).wait_recv()
            total = total + dst[...].astype(F32)
        return total

    def y_copy(e, src, to_y):
        return pltpu.make_async_remote_copy(
            src_ref=y_late_send if e == 0 else y_send.at[e],
            dst_ref=y_late_recv.at[src] if e == 0 else y_recv.at[src], send_sem=y_send_sem.at[e],
            recv_sem=y_recv_sem.at[src], device_id=at_row(x, to_y, core), device_id_type=MESH,
        )

    def y_start(e):
        to_y = (late + e) % NY
        total = line_sum(to_y, e == 0)
        y_send[e] = total
        if e == 0:
            y_late_send[...] = total.astype(BF16)

        @pl.when(to_y != yl)
        def _():
            y_copy(e, yl, to_y).start()

    width = 256
    stores = []

    def keep(stage, out):
        stores.append(pltpu.make_async_copy(stage, out, here.at[7 + len(stores)]))
        stores[-1].start()

    def down_grads():
        go_flat = go_all[...].reshape(-1, go_all.shape[3])
        for n in range(hidden.shape[3] // width):
            cols = pl.ds(n * width, width)
            st_gd[cols] = dot(hidden[..., cols].reshape(-1, width), go_flat, 0, 0).astype(BF16)
        keep(st_gd, out_gd)

    ops = {
        "goy": go_along_y, "gox": go_along_x, "goc": go_to_core,
        "toky": tok_along_y, "tokx": tok_along_x, "tokc": tok_to_core, "T": tok_turn,
        "acty": act_across, "a": act_ring, "A": activate, "S": share, "r": reduce_step,
        "w": swap, "g": grad_ring, "G": gradients, "O": outward, "D": down_grads,
    }
    for op, *at in ORDER:
        ops[op](*at)

    for i, (grad, stage, out) in enumerate(((gate_grad, st_gg, out_gg), (up_grad, st_gu, out_gu))):
        for n in range(grad.shape[3] // width):
            cols = pl.ds(n * width, width)
            if i == 0 and n == 1:
                outward(4)
                for e in (2, 1, 3):
                    y_start(e)
            if i == 1 and n == 0:
                y_start(0)
            stage[:, cols] = dot(tok_t[...], grad[..., cols].reshape(-1, width), 1, 0).astype(BF16)
        keep(stage, out)

    others = [(yl + d) % NY for d in range(1, NY)]

    @pl.when(yl == late)
    def _():
        total = y_send[0]
        for src in others:
            y_copy(0, src, yl).wait_recv()
            total = total + y_late_recv[src].astype(F32)
        out_gt[...] = total.astype(BF16)

    @pl.when(yl != late)
    def _():
        total = y_send[(yl + NY - late) % NY]
        for src in others:
            y_copy(1, src, yl).wait_recv()
            total = total + y_recv[src]
        out_gt[...] = total.astype(BF16)

    for copy in sent:
        copy.wait_send()

    for o in range(NZ):
        core_copy(o).wait_send()
        for h in range(NH):
            to_x, to_y = target(o, h)

            @pl.when(to_x != x)
            def _():
                x_copy(o, h, to_x, to_y).wait_send()

    for e in range(NY):
        to_y = (late + e) % NY

        @pl.when(to_y != yl)
        def _():
            y_copy(e, yl, to_y).wait_send()

    for store in stores:
        store.wait()


def copy_kernel(*refs):
    sources, results, held, sems = refs[:4], refs[4:8], refs[8:12], refs[12]
    reads = [pltpu.make_async_copy(s, h, sems.at[0, i]) for i, (s, h) in enumerate(zip(sources, held))]
    writes = [pltpu.make_async_copy(h, r, sems.at[1, i]) for i, (h, r) in enumerate(zip(held, results))]
    for read in reads:
        read.start()
    for read, write in zip(reads, writes):
        read.wait()
        write.start()
    for write in writes:
        write.wait()


def on_device(tokens, grad_out, gate_pre, up_pre, w_gate, w_up, w_down):
    th, dd = tokens.shape
    tb, ff = gate_pre.shape
    nrow, ncol = NX * NY, NH * NZ
    anywhere = pl.BlockSpec(memory_space=pl.ANY)
    vmem = pltpu.VMEM
    dma = pltpu.SemaphoreType.DMA
    out = [
        jax.ShapeDtypeStruct(tokens.shape, BF16),
        jax.ShapeDtypeStruct(w_gate.shape, BF16),
        jax.ShapeDtypeStruct(w_up.shape, BF16),
        jax.ShapeDtypeStruct(w_down.shape, BF16),
    ]
    every = (NH, NZ, tb, ff)
    scratch = [
        vmem((nrow, NC, th, dd), BF16),
        vmem((nrow, NC, th, dd), BF16),
        vmem((2,) + every, BF16),
        vmem((dd, ff), BF16),
        vmem((dd, ff), BF16),
        vmem((ff, dd), BF16),
        vmem(every, F32),
        vmem((NH, 2, 4, tb, ff), BF16),
        vmem((NH, 2, 4, tb, ff), BF16),
        vmem((NH, tb, ff), BF16),
        vmem((NH, tb, ff), BF16),
        vmem(every, BF16),
        vmem(every, F32),
        vmem(every, F32),
        vmem(every, BF16),
        vmem(every, BF16),
        vmem(every, BF16),
        vmem((dd, ncol * tb), BF16),
        vmem((NZ, NH, NC, th, dd), F32),
        vmem((NZ, NH, th, dd), F32),
        vmem((NZ, NH, th, dd), F32),
        vmem((NZ, NH, th, dd), F32),
        vmem((NX, NY, th, dd), F32),
        vmem((2, NH, th, dd), BF16),
        vmem((NX, th, dd), BF16),
        vmem((NY, th, dd), F32),
        vmem((NY, th, dd), F32),
        vmem((NY, th, dd), F32),
        vmem((th, dd), BF16),
        vmem((NY, th, dd), BF16),
        vmem((dd, ff), BF16),
        vmem((dd, ff), BF16),
        vmem((ff, dd), BF16),
        dma((COPIES,)),
        dma((COPIES,)),
        dma((NZ,)),
        dma((NZ,)),
        dma((NZ, NH)),
        dma((NY, NX)),
        dma((NY,)),
        dma((NY,)),
        dma((10,)),
    ]
    results = (
        pl.pallas_call(
            kernel,
            out_shape=out,
            in_specs=[anywhere] * 7,
            out_specs=[pl.BlockSpec(memory_space=vmem)] + [anywhere] * 3,
            scratch_shapes=scratch,
            compiler_params=pltpu.CompilerParams(
                collective_id=0, has_side_effects=True, vmem_limit_bytes=56 * 2**20
            ),
            cost_estimate=pl.CostEstimate(
                flops=12 * nrow * NC * th * dd * ff, bytes_accessed=8 * dd * ff * 2, transcendentals=ncol * tb * ff
            ),
        )(tokens, grad_out, gate_pre, up_pre, w_gate, w_up, w_down)
    )
    return tuple(
        pl.pallas_call(
            copy_kernel,
            out_shape=out,
            in_specs=[anywhere] * 4,
            out_specs=[anywhere] * 4,
            scratch_shapes=[vmem(o.shape, o.dtype) for o in out] + [dma((2, 4))],
            compiler_params=pltpu.CompilerParams(vmem_limit_bytes=60 * 2**20),
        )(*results)
    )


def solution(mesh):
    return jax.shard_map(
        on_device,
        mesh=mesh,
        in_specs=(
            P("row", "col"),
            P("row", "col"),
            P("col", "row"),
            P("col", "row"),
            P("col", "row"),
            P("col", "row"),
            P("row", "col"),
        ),
        out_specs=(P("row", "col"), P("col", "row"), P("col", "row"), P("row", "col")),
        check_vma=False,
    )
```

```python
import functools

import jax
import jax.numpy as jnp
from jax import lax
from jax.experimental import pallas as pl
from jax.experimental.pallas import tpu as pltpu
from jax.sharding import PartitionSpec as P

MESH = pl.DeviceIdType.MESH
F32 = jnp.float32
BF16 = jnp.bfloat16
NX, NY, NC = 4, 4, 2
NH, NZ = 2, 8
PIECE = 192
ROWS = 32
COPIES = 111
ORDER = (
    ("goy",), ("a", 1, 1, 1), ("acty",), ("a", 1, 0, 1), ("gox",), ("a", 1, 1, 2), ("a", 1, 0, 2), ("goc", 0),
    ("a", 1, 1, 3), ("a", 1, 0, 3), ("goc", 1), ("a", 1, 1, 4), ("S", 4), ("r", 0, 0, 1), ("r", 0, 1, 1),
    ("r", 1, 0, 1), ("r", 1, 1, 1), ("S", 0), ("a", 1, 0, 4), ("S", 3), ("r", 0, 0, 2), ("r", 0, 1, 2),
    ("toky",), ("r", 1, 1, 2), ("S", 2), ("r", 0, 0, 3), ("r", 1, 0, 2), ("S", 1), ("r", 1, 1, 3),
    ("r", 0, 0, 4), ("tokx",), ("a", 2, 1, 1), ("r", 0, 1, 3), ("r", 1, 1, 4), ("r", 1, 0, 3), ("a", 2, 0, 1),
    ("w", 0, 0), ("r", 0, 1, 4), ("A", 2, 0), ("w", 1, 1), ("tokc",), ("A", 1, 4), ("g", 0, 0, 1),
    ("a", 2, 1, 2), ("A", 1, 3), ("r", 1, 0, 4), ("w", 0, 1), ("a", 2, 0, 2), ("A", 1, 1), ("g", 1, 1, 1),
    ("A", 1, 2), ("A", 1, 0), ("w", 1, 0), ("g", 0, 1, 1), ("a", 2, 1, 3), ("A", 2, 1), ("A", 2, 2),
    ("g", 0, 1, 2), ("g", 1, 0, 1), ("g", 1, 1, 2), ("G", 0), ("T",), ("g", 0, 0, 2), ("g", 1, 0, 2),
    ("a", 2, 0, 3), ("G", 1), ("g", 0, 0, 3), ("g", 0, 1, 3), ("g", 1, 1, 3), ("G", 2), ("g", 1, 0, 3),
    ("A", 2, 3), ("a", 2, 1, 4), ("a", 2, 0, 4), ("O", 1), ("g", 0, 0, 4), ("O", 2), ("g", 1, 1, 4),
    ("g", 0, 1, 4), ("O", 0), ("g", 1, 0, 4), ("G", 3), ("A", 2, 4), ("D",), ("O", 3), ("G", 4),
)


def dot(left, right, left_dim, right_dim):
    return lax.dot_general(
        left, right, (((left_dim,), (right_dim,)), ((), ())), preferred_element_type=F32
    )


def kernel(
    tok_ref, go_ref, gate_ref, up_ref, wg_ref, wu_ref, wd_ref,
    out_gt, out_gg, out_gu, out_gd,
    tok_all, go_all, acts, wg, wu, wd, part, rs_send, rs_recv, swap_send, swap_recv,
    grad_h, silu, slope, hidden, gate_grad, up_grad, tok_t, pair_sum, core_send, core_recv,
    x_send, x_recv, x_late_send, x_late_recv, x_own, y_send, y_recv, y_late_send, y_late_recv, st_gg, st_gu, st_gd,
    send, recv, core_send_sem, core_recv_sem, x_send_sem, x_recv_sem, y_send_sem, y_recv_sem, here,
):
    row, col = lax.axis_index("row"), lax.axis_index("col")
    x, yl, core = row // (NY * NC), (row // NC) % NY, row % NC
    yh, z = col // NZ, col % NZ
    tb, half = acts.shape[3], acts.shape[3] // 2

    def at_row(px, py, pc):
        return (px * (NY * NC) + py * NC + pc, col)

    def at_col(ph, pz):
        return (row, ph * NZ + pz)

    xs = [at_row((x + d) % NX, yl, core) for d in range(1, NX)]
    ys = [at_row(x, (yl + d) % NY, core) for d in range(1, NY)]
    sibling = at_row(x, yl, 1 - core)
    ahead, behind = at_col(yh, (z + 1) % NZ), at_col(yh, (z + NZ - 1) % NZ)
    across = at_col(1 - yh, z)

    sent = []
    coming = {}

    def push(src, dst, to):
        n = len(sent)
        copy = pltpu.make_async_remote_copy(
            src_ref=src, dst_ref=dst, send_sem=send.at[n], recv_sem=recv.at[n],
            device_id=to, device_id_type=MESH,
        )
        copy.start()
        sent.append(copy)
        return copy

    def arrive(*key):
        for copy in coming[key]:
            copy.wait_recv()
        coming[key] = ()

    def loaded(*which):
        for i in which:
            if loads[i] is not None:
                loads[i].wait()
                loads[i] = None

    mine = x * NY + yl
    loads = [
        (go_ref, go_all.at[mine, core]), (tok_ref, tok_all.at[mine, core]),
        (gate_ref, acts.at[0, yh, z]), (up_ref, acts.at[1, yh, z]),
        (wd_ref, wd), (wg_ref, wg), (wu_ref, wu),
    ]
    loads = [pltpu.make_async_copy(s, d, here.at[i]) for i, (s, d) in enumerate(loads)]
    for load in loads:
        load.start()

    barrier = pltpu.get_barrier_semaphore()
    partners = xs + ys + [sibling, ahead, behind, across]
    for to in partners:
        pl.semaphore_signal(barrier, inc=1, device_id=to, device_id_type=MESH)
    pl.semaphore_wait(barrier, len(partners))

    def ring_send(block, k, step, first=None):
        copies = []
        for way, to in ((1, ahead), (-1, behind)):
            at = (z + (NZ - way * (step - 1))) % NZ
            ref = block(k, at)
            if step == NZ // 2:
                ref = ref.at[pl.ds(0 if way == 1 else half, half)]
            copies.append(push(ref if first is None else first, ref, to))
        return copies

    def own_act(k, at):
        return acts.at[k, yh, at]

    def other_act(k, at):
        return acts.at[k, 1 - yh, at]

    def pair_loop(m, step):
        if m in (0, NZ // 2):
            step(m)
        else:
            pl.loop(0, 2)(lambda i: step(m + (NZ - 2 * m) * i))

    def activate(ring, m):
        h = yh if ring == 1 else 1 - yh
        if m == 0 and ring == 1:
            loaded(2, 3)
        elif m == 0:
            arrive("act_y")
        else:
            arrive("act", ring, 0, m)
            arrive("act", ring, 1, m)

        def step(o):
            at = (z + o) % NZ

            @pl.loop(0, tb // ROWS)
            def _(i):
                rows = pl.ds(pl.multiple_of(i * ROWS, ROWS), ROWS)
                g = acts[0, h, at, rows].astype(F32)
                u = acts[1, h, at, rows].astype(F32)
                s = jax.nn.sigmoid(g)
                gs = g * s
                silu[h, at, rows] = gs
                slope[h, at, rows] = u * s * (1.0 + g * (1.0 - s))
                hidden[h, at, rows] = (gs * u).astype(BF16)

        pair_loop(m, step)

    def share(m):
        arrive("go_core", 0)
        arrive("go_core", 1)
        loaded(4)

        def step(o):
            at = (z + o) % NZ
            rows = jnp.concatenate(
                [go_all[h * NZ + at].reshape(tb, -1) for h in range(NH)], axis=0
            )
            sums = dot(rows, wd[...], 1, 1)
            for h in range(NH):
                part[h, at] = sums[h * tb : (h + 1) * tb]

        pair_loop(m, step)

    ways = ((1, ahead), (-1, behind))

    def reduce_step(h, p, step):
        rows = pl.ds(p * half, half)
        for w, (way, to) in enumerate(ways):
            if step == 1 and w != p:
                continue
            at = (z + (NZ + way * (NZ // 2 + 1 - step))) % NZ
            out = rs_send.at[h, w, step - 1, rows]
            value = part[h, at, rows]
            if step > 2 or (step == 2 and w == p):
                arrive("sums", h, p, step - 1, w)
                value = value + rs_recv[h, w, step - 2, rows].astype(F32)
            out[...] = value.astype(BF16)
            coming["sums", h, p, step, w] = [push(out, rs_recv.at[h, w, step - 1, rows], to)]

    def spread(own, copies_of, source):
        return [push(source, own, to) for to in copies_of]

    def x_line(ref, away=0):
        return ref.at[pl.ds((x + away) % NX * NY, NY), core]

    def go_along_y():
        coming[("go_y",)] = spread(go_all.at[mine, core], ys, go_ref)

    def go_along_x():
        loaded(0)
        arrive("go_y")
        copies = spread(x_line(go_all), xs, x_line(go_all))
        coming["go_x", 0], coming["go_x", 1] = [copies[0], copies[2]], [copies[1]]

    def go_to_core(i):
        arrive("go_x", i)
        lines = [x_line(go_all, away) for away in ((0, 1, NX - 1), (NX // 2,))[i]]
        coming["go_core", i] = [push(line, line, sibling) for line in lines]

    def tok_along_y():
        coming[("tok_y",)] = spread(tok_all.at[mine, core], ys, tok_ref)

    def tok_along_x():
        loaded(1)
        arrive("tok_y")
        coming[("tok_x",)] = spread(x_line(tok_all), xs, x_line(tok_all))

    def tok_to_core():
        arrive("tok_x")
        coming[("tok_core",)] = [push(tok_all.at[:, core], tok_all.at[:, core], sibling)]

    def tok_turn():
        arrive("tok_core")
        tok_t[...] = tok_all[...].reshape(-1, tok_all.shape[3]).T

    def act_across():
        refs = enumerate((gate_ref, up_ref))
        coming[("act_y",)] = [push(ref, acts.at[k, yh, z], across) for k, ref in refs]

    def act_ring(ring, k, step):
        first = None
        if step > 1:
            arrive("act", ring, k, step - 1)
        elif ring == 1:
            first = (gate_ref, up_ref)[k]
        else:
            arrive("act_y")
        coming["act", ring, k, step] = ring_send(own_act if ring == 1 else other_act, k, step, first)

    def swap(h, p):
        rows = pl.ds(p * half, half)
        for w in range(2):
            arrive("sums", h, p, NZ // 2, w)
        total = part[h, z, rows] + rs_recv[h, 0, 3, rows].astype(F32) + rs_recv[h, 1, 3, rows].astype(F32)
        part[h, z, rows] = total
        swap_send[h, rows] = total.astype(BF16)
        coming["swap", h, p] = [push(swap_send.at[h, rows], swap_recv.at[h, rows], across)]

    def grad_ring(h, p, step):
        rows = pl.ds(p * half, half)
        if step == 1:
            arrive("swap", h, p)
            grad_h[h, z, rows] = (part[h, z, rows] + swap_recv[h, rows].astype(F32)).astype(BF16)
        for w, (way, to) in enumerate(ways):
            if step == NZ // 2 and w != p:
                continue
            if step > 1:
                arrive("grad", h, p, step - 1, w)
            ref = grad_h.at[h, (z + (NZ - way * (step - 1))) % NZ, rows]
            coming["grad", h, p, step, w] = [push(ref, ref, to)]

    def gradients(m):
        offsets = (m,) if m in (0, NZ // 2) else (m, NZ - m)
        places = [(z + o) % NZ for o in offsets]
        loaded(5, 6)
        for h in range(NH):
            for p, w in ((0, 0), (0, 1), (1, 0), (1, 1)):
                if m > 0 and not (m == NZ // 2 and w != p):
                    arrive("grad", h, p, m, w)
        for at in places:
            for h in range(NH):

                @pl.loop(0, tb // ROWS)
                def _(i):
                    rows = pl.ds(pl.multiple_of(i * ROWS, ROWS), ROWS)
                    gh = grad_h[h, at, rows].astype(F32)
                    gate_grad[h, at, rows] = (gh * slope[h, at, rows]).astype(BF16)
                    up_grad[h, at, rows] = (gh * silu[h, at, rows]).astype(BF16)

        def tall(ref):
            return jnp.concatenate([ref[:, at].reshape(NH * tb, -1) for at in places], axis=0)

        sums = dot(tall(gate_grad), wg[...], 1, 1) + dot(tall(up_grad), wu[...], 1, 1)
        for n, o in enumerate(offsets):
            pair_sum[o] = sums[n * NH * tb : (n + 1) * NH * tb].reshape(pair_sum.shape[1:])
            core_send[o] = pair_sum[o, :, 1 - core]
            core_copy(o).start()

    def core_copy(o):
        return pltpu.make_async_remote_copy(
            src_ref=core_send.at[o], dst_ref=core_recv.at[o], send_sem=core_send_sem.at[o],
            recv_sem=core_recv_sem.at[o], device_id=sibling, device_id_type=MESH,
        )

    late = z % NY

    def is_late(o):
        return o in (0, NZ // 2)

    def x_copy(o, h, to_x, to_y):
        if is_late(o):
            src, dst = x_late_send.at[o // (NZ // 2), h], x_late_recv.at[x]
        else:
            src, dst = x_send.at[o, h], x_recv.at[x, to_y]
        return pltpu.make_async_remote_copy(
            src_ref=src, dst_ref=dst, send_sem=x_send_sem.at[o, h],
            recv_sem=x_recv_sem.at[to_y, x], device_id=at_row(to_x, yl, core), device_id_type=MESH,
        )

    def target(o, h):
        at = h * NZ + (z + o) % NZ
        return at // NY, at % NY

    def outward(m):
        for o in (m,) if is_late(m) else (m, NZ - m):
            core_copy(o).wait_recv()
            for h in range(NH):
                to_x, to_y = target(o, h)
                total = pair_sum[o, h, core] + core_recv[o, h]
                if is_late(o):
                    x_late_send[o // (NZ // 2), h] = total.astype(BF16)
                x_send[o, h] = total

                @pl.when(to_x == x)
                def _():
                    x_own[to_y] = x_send[o, h]

                @pl.when(to_x != x)
                def _():
                    x_copy(o, h, to_x, to_y).start()

    def line_sum(to_y, last):
        total = x_own[to_y]
        for d in range(1, NX):
            src = (x + d) % NX
            dst = x_late_recv.at[src] if last else x_recv.at[src, to_y]
            pltpu.make_async_remote_copy(
                src_ref=dst, dst_ref=dst, send_sem=x_send_sem.at[0, 0],
                recv_sem=x_recv_sem.at[to_y, src], device_id=sibling, device_id_type=MESH,
            ).wait_recv()
            total = total + dst[...].astype(F32)
        return total

    def y_copy(e, src, to_y):
        return pltpu.make_async_remote_copy(
            src_ref=y_late_send if e == 0 else y_send.at[e],
            dst_ref=y_late_recv.at[src] if e == 0 else y_recv.at[src], send_sem=y_send_sem.at[e],
            recv_sem=y_recv_sem.at[src], device_id=at_row(x, to_y, core), device_id_type=MESH,
        )

    def y_start(e):
        to_y = (late + e) % NY
        total = line_sum(to_y, e == 0)
        y_send[e] = total
        if e == 0:
            y_late_send[...] = total.astype(BF16)

        @pl.when(to_y != yl)
        def _():
            y_copy(e, yl, to_y).start()

    width = 256
    stores = []

    def keep(stage, out):
        stores.append(pltpu.make_async_copy(stage, out, here.at[7 + len(stores)]))
        stores[-1].start()

    def down_grads():
        go_flat = go_all[...].reshape(-1, go_all.shape[3])
        for n in range(hidden.shape[3] // width):
            cols = pl.ds(n * width, width)
            st_gd[cols] = dot(hidden[..., cols].reshape(-1, width), go_flat, 0, 0).astype(BF16)
        keep(st_gd, out_gd)

    ops = {
        "goy": go_along_y, "gox": go_along_x, "goc": go_to_core,
        "toky": tok_along_y, "tokx": tok_along_x, "tokc": tok_to_core, "T": tok_turn,
        "acty": act_across, "a": act_ring, "A": activate, "S": share, "r": reduce_step,
        "w": swap, "g": grad_ring, "G": gradients, "O": outward, "D": down_grads,
    }
    for op, *at in ORDER:
        ops[op](*at)

    for i, (grad, stage, out) in enumerate(((gate_grad, st_gg, out_gg), (up_grad, st_gu, out_gu))):
        for n in range(grad.shape[3] // width):
            cols = pl.ds(n * width, width)
            if i == 0 and n == 1:
                outward(4)
                for e in (2, 1, 3):
                    y_start(e)
            if i == 1 and n == 0:
                y_start(0)
            stage[:, cols] = dot(tok_t[...], grad[..., cols].reshape(-1, width), 1, 0).astype(BF16)
        keep(stage, out)

    others = [(yl + d) % NY for d in range(1, NY)]

    @pl.when(yl == late)
    def _():
        total = y_send[0]
        for src in others:
            y_copy(0, src, yl).wait_recv()
            total = total + y_late_recv[src].astype(F32)
        out_gt[...] = total.astype(BF16)

    @pl.when(yl != late)
    def _():
        total = y_send[(yl + NY - late) % NY]
        for src in others:
            y_copy(1, src, yl).wait_recv()
            total = total + y_recv[src]
        out_gt[...] = total.astype(BF16)

    for copy in sent:
        copy.wait_send()

    for o in range(NZ):
        core_copy(o).wait_send()
        for h in range(NH):
            to_x, to_y = target(o, h)

            @pl.when(to_x != x)
            def _():
                x_copy(o, h, to_x, to_y).wait_send()

    for e in range(NY):
        to_y = (late + e) % NY

        @pl.when(to_y != yl)
        def _():
            y_copy(e, yl, to_y).wait_send()

    for store in stores:
        store.wait()


def copy_kernel(*refs):
    sources, results, held, sems = refs[:4], refs[4:8], refs[8:12], refs[12]
    reads, writes = [], []
    for source, result, hold in zip(sources, results, held):
        high = min(PIECE, source.shape[0])
        for at in range(0, source.shape[0], high):
            rows, n = pl.ds(at, high), len(reads)
            reads.append(pltpu.make_async_copy(source.at[rows], hold.at[rows], sems.at[0, n]))
            writes.append(pltpu.make_async_copy(hold.at[rows], result.at[rows], sems.at[1, n]))
            reads[-1].start()
    for read, write in zip(reads, writes):
        read.wait()
        write.start()
    for write in writes:
        write.wait()


def on_device(tokens, grad_out, gate_pre, up_pre, w_gate, w_up, w_down):
    th, dd = tokens.shape
    tb, ff = gate_pre.shape
    nrow, ncol = NX * NY, NH * NZ
    anywhere = pl.BlockSpec(memory_space=pl.ANY)
    vmem = pltpu.VMEM
    dma = pltpu.SemaphoreType.DMA
    out = [
        jax.ShapeDtypeStruct(tokens.shape, BF16),
        jax.ShapeDtypeStruct(w_gate.shape, BF16),
        jax.ShapeDtypeStruct(w_up.shape, BF16),
        jax.ShapeDtypeStruct(w_down.shape, BF16),
    ]
    every = (NH, NZ, tb, ff)
    scratch = [
        vmem((nrow, NC, th, dd), BF16),
        vmem((nrow, NC, th, dd), BF16),
        vmem((2,) + every, BF16),
        vmem((dd, ff), BF16),
        vmem((dd, ff), BF16),
        vmem((ff, dd), BF16),
        vmem(every, F32),
        vmem((NH, 2, 4, tb, ff), BF16),
        vmem((NH, 2, 4, tb, ff), BF16),
        vmem((NH, tb, ff), BF16),
        vmem((NH, tb, ff), BF16),
        vmem(every, BF16),
        vmem(every, F32),
        vmem(every, F32),
        vmem(every, BF16),
        vmem(every, BF16),
        vmem(every, BF16),
        vmem((dd, ncol * tb), BF16),
        vmem((NZ, NH, NC, th, dd), F32),
        vmem((NZ, NH, th, dd), F32),
        vmem((NZ, NH, th, dd), F32),
        vmem((NZ, NH, th, dd), F32),
        vmem((NX, NY, th, dd), F32),
        vmem((2, NH, th, dd), BF16),
        vmem((NX, th, dd), BF16),
        vmem((NY, th, dd), F32),
        vmem((NY, th, dd), F32),
        vmem((NY, th, dd), F32),
        vmem((th, dd), BF16),
        vmem((NY, th, dd), BF16),
        vmem((dd, ff), BF16),
        vmem((dd, ff), BF16),
        vmem((ff, dd), BF16),
        dma((COPIES,)),
        dma((COPIES,)),
        dma((NZ,)),
        dma((NZ,)),
        dma((NZ, NH)),
        dma((NY, NX)),
        dma((NY,)),
        dma((NY,)),
        dma((10,)),
    ]
    results = (
        pl.pallas_call(
            kernel,
            out_shape=out,
            in_specs=[anywhere] * 7,
            out_specs=[pl.BlockSpec(memory_space=vmem)] + [anywhere] * 3,
            scratch_shapes=scratch,
            compiler_params=pltpu.CompilerParams(
                collective_id=0, has_side_effects=True, vmem_limit_bytes=56 * 2**20
            ),
            cost_estimate=pl.CostEstimate(
                flops=12 * nrow * NC * th * dd * ff, bytes_accessed=8 * dd * ff * 2, transcendentals=ncol * tb * ff
            ),
        )(tokens, grad_out, gate_pre, up_pre, w_gate, w_up, w_down)
    )
    return tuple(
        pl.pallas_call(
            copy_kernel,
            out_shape=out,
            in_specs=[anywhere] * 4,
            out_specs=[anywhere] * 4,
            scratch_shapes=[vmem(o.shape, o.dtype) for o in out] + [dma((2, 16))],
            compiler_params=pltpu.CompilerParams(vmem_limit_bytes=60 * 2**20),
        )(*results)
    )


def solution(mesh):
    return jax.shard_map(
        on_device,
        mesh=mesh,
        in_specs=(
            P("row", "col"),
            P("row", "col"),
            P("col", "row"),
            P("col", "row"),
            P("col", "row"),
            P("col", "row"),
            P("row", "col"),
        ),
        out_specs=(P("row", "col"), P("col", "row"), P("col", "row"), P("row", "col")),
        check_vma=False,
    )
```

```python
import functools

import jax
import jax.numpy as jnp
from jax import lax
from jax.experimental import pallas as pl
from jax.experimental.pallas import tpu as pltpu
from jax.sharding import PartitionSpec as P

MESH = pl.DeviceIdType.MESH
F32 = jnp.float32
BF16 = jnp.bfloat16
NX, NY, NC = 4, 4, 2
NH, NZ = 2, 8
ROWS = 32
COPIES = 65
ORDER = (
    ("goy",), ("a", 1, 1), ("toky",), ("gox",), ("A", 1, 1), ("tokx",), ("a", 1, 2), ("goc",), ("acty",),
    ("A", 1, 0), ("S", 4), ("r", 1, 1), ("r", 0, 1), ("S", 3), ("r", 1, 2), ("S", 0), ("r", 0, 2), ("S", 2),
    ("r", 1, 3), ("r", 0, 3), ("S", 1), ("r", 1, 4), ("r", 0, 4), ("tokc",), ("a", 2, 1), ("w", 1),
    ("a", 1, 3), ("w", 0), ("T",), ("A", 2, 1), ("g", 1, 1), ("a", 2, 2), ("A", 2, 0), ("A", 1, 2),
    ("A", 1, 3), ("g", 0, 1), ("G", 0), ("a", 1, 4), ("g", 1, 2), ("A", 2, 2), ("O", 0), ("g", 0, 2),
    ("G", 1), ("a", 2, 3), ("g", 1, 3), ("A", 1, 4), ("O", 1), ("G", 2), ("g", 0, 3), ("a", 2, 4),
    ("A", 2, 3), ("O", 2), ("g", 1, 4), ("G", 3), ("g", 0, 4), ("A", 2, 4), ("D",), ("O", 3), ("G", 4),
)


def dot(left, right, left_dim, right_dim):
    return lax.dot_general(
        left, right, (((left_dim,), (right_dim,)), ((), ())), preferred_element_type=F32
    )


def kernel(
    tok_ref, go_ref, gate_ref, up_ref, wg_ref, wu_ref, wd_ref,
    out_gt, out_gg, out_gu, out_gd,
    tok_all, go_all, acts, wg, wu, wd, part, rs_send, rs_recv, swap_send, swap_recv,
    grad_h, silu, slope, hidden, gate_grad, up_grad, tok_t, pair_sum, core_send, core_recv,
    x_send, x_recv, x_late_send, x_late_recv, x_own, y_send, y_recv, y_late_send, y_late_recv, st_gg, st_gu, st_gd,
    send, recv, core_send_sem, core_recv_sem, x_send_sem, x_recv_sem, y_send_sem, y_recv_sem, here,
):
    row, col = lax.axis_index("row"), lax.axis_index("col")
    x, yl, core = row // (NY * NC), (row // NC) % NY, row % NC
    yh, z = col // NZ, col % NZ
    tb, half = acts.shape[3], acts.shape[3] // 2

    def at_row(px, py, pc):
        return (px * (NY * NC) + py * NC + pc, col)

    def at_col(ph, pz):
        return (row, ph * NZ + pz)

    xs = [at_row((x + d) % NX, yl, core) for d in range(1, NX)]
    ys = [at_row(x, (yl + d) % NY, core) for d in range(1, NY)]
    sibling = at_row(x, yl, 1 - core)
    ahead, behind = at_col(yh, (z + 1) % NZ), at_col(yh, (z + NZ - 1) % NZ)
    across = at_col(1 - yh, z)

    sent = []
    coming = {}

    def push(src, dst, to):
        n = len(sent)
        copy = pltpu.make_async_remote_copy(
            src_ref=src, dst_ref=dst, send_sem=send.at[n], recv_sem=recv.at[n],
            device_id=to, device_id_type=MESH,
        )
        copy.start()
        sent.append(copy)
        return copy

    def arrive(*key):
        for copy in coming[key]:
            copy.wait_recv()
        coming[key] = ()

    def loaded(*which):
        for i in which:
            if loads[i] is not None:
                loads[i].wait()
                loads[i] = None

    mine = x * NY + yl
    loads = [
        (go_ref, go_all.at[mine, core]), (tok_ref, tok_all.at[mine, core]),
        (gate_ref, acts.at[yh, z, 0]), (up_ref, acts.at[yh, z, 1]),
        (wd_ref, wd), (wg_ref, wg), (wu_ref, wu),
    ]
    loads = [pltpu.make_async_copy(s, d, here.at[i]) for i, (s, d) in enumerate(loads)]
    for load in loads:
        load.start()

    barrier = pltpu.get_barrier_semaphore()
    partners = xs + ys + [sibling, ahead, behind, across]
    for to in partners:
        pl.semaphore_signal(barrier, inc=1, device_id=to, device_id_type=MESH)
    pl.semaphore_wait(barrier, len(partners))

    def ring_send(block, step):
        copies = []
        for way, to in ((1, ahead), (-1, behind)):
            at = (z + (NZ - way * (step - 1))) % NZ
            ref = block(at)
            if step == NZ // 2:
                rows = pl.ds(0 if way == 1 else half, half)
                ref = ref.at[:, rows] if len(ref.shape) == 3 else ref.at[rows]
            copies.append(push(ref, ref, to))
        return copies

    def pair_loop(m, step):
        if m in (0, NZ // 2):
            step(m)
        else:
            pl.loop(0, 2)(lambda i: step(m + (NZ - 2 * m) * i))

    def activate(ring, m):
        h = yh if ring == 1 else 1 - yh
        if m == 0 and ring == 1:
            loaded(2, 3)
        elif m == 0:
            arrive("act_y")
        else:
            arrive("act", ring, m)

        def step(o):
            at = (z + o) % NZ

            @pl.loop(0, tb // ROWS)
            def _(i):
                rows = pl.ds(pl.multiple_of(i * ROWS, ROWS), ROWS)
                g = acts[h, at, 0, rows].astype(F32)
                u = acts[h, at, 1, rows].astype(F32)
                s = jax.nn.sigmoid(g)
                gs = g * s
                silu[h, at, rows] = gs
                slope[h, at, rows] = u * s * (1.0 + g * (1.0 - s))
                hidden[h, at, rows] = (gs * u).astype(BF16)

        pair_loop(m, step)

    def share(m):
        arrive("go_core")
        loaded(4)

        def step(o):
            at = (z + o) % NZ
            rows = jnp.concatenate(
                [go_all[h * NZ + at].reshape(tb, -1) for h in range(NH)], axis=0
            )
            sums = dot(rows, wd[...], 1, 1)
            for h in range(NH):
                part[h, at] = sums[h * tb : (h + 1) * tb]

        pair_loop(m, step)

    def reduce_step(h, step):
        copies = []
        for w, (way, to) in enumerate(((1, ahead), (-1, behind))):
            at = (z + (NZ + way * (NZ // 2 + 1 - step))) % NZ
            out = rs_send.at[h, w, step - 1]
            rows = pl.ds(0 if way == 1 else half, half)
            if step == 1:
                out[rows] = part[h, at, rows].astype(BF16)
                copies.append(push(out.at[rows], rs_recv.at[h, w, 0, rows], to))
                continue
            coming["sums", h, step - 1][w].wait_recv()
            if step == 2:
                rest = pl.ds(half if way == 1 else 0, half)
                out[rows] = (part[h, at, rows] + rs_recv[h, w, 0, rows].astype(F32)).astype(BF16)
                out[rest] = part[h, at, rest].astype(BF16)
            else:
                out[...] = (part[h, at] + rs_recv[h, w, step - 2].astype(F32)).astype(BF16)
            copies.append(push(out, rs_recv.at[h, w, step - 1], to))
        coming["sums", h, step] = copies

    def spread(own, copies_of, source):
        return [push(source, own, to) for to in copies_of]

    def x_line(ref):
        return ref.at[pl.ds(x * NY, NY), core]

    def go_along_y():
        coming[("go_y",)] = spread(go_all.at[mine, core], ys, go_ref)

    def go_along_x():
        loaded(0)
        arrive("go_y")
        coming[("go_x",)] = spread(x_line(go_all), xs, x_line(go_all))

    def go_to_core():
        arrive("go_x")
        coming[("go_core",)] = [push(go_all.at[:, core], go_all.at[:, core], sibling)]

    def tok_along_y():
        coming[("tok_y",)] = spread(tok_all.at[mine, core], ys, tok_ref)

    def tok_along_x():
        loaded(1)
        arrive("tok_y")
        coming[("tok_x",)] = spread(x_line(tok_all), xs, x_line(tok_all))

    def tok_to_core():
        arrive("tok_x")
        coming[("tok_core",)] = [push(tok_all.at[:, core], tok_all.at[:, core], sibling)]

    def tok_turn():
        arrive("tok_core")
        tok_t[...] = tok_all[...].reshape(-1, tok_all.shape[3]).T

    def act_across():
        loaded(2, 3)
        ref = acts.at[yh, z]
        coming[("act_y",)] = [push(ref, ref, across)]

    def act_ring(ring, step):
        if step > 1:
            arrive("act", ring, step - 1)
        elif ring == 1:
            loaded(2, 3)
        else:
            arrive("act_y")
        h = yh if ring == 1 else 1 - yh
        coming["act", ring, step] = ring_send(lambda at: acts.at[h, at], step)

    def swap(h):
        arrive("sums", h, 4)
        total = part[h, z] + rs_recv[h, 0, 3].astype(F32) + rs_recv[h, 1, 3].astype(F32)
        part[h, z] = total
        swap_send[h] = total.astype(BF16)
        coming["swap", h] = [push(swap_send.at[h], swap_recv.at[h], across)]

    def grad_ring(h, step):
        if step == 1:
            arrive("swap", h)
            grad_h[h, z] = (part[h, z] + swap_recv[h].astype(F32)).astype(BF16)
        else:
            arrive("grad", h, step - 1)
        coming["grad", h, step] = ring_send(lambda at: grad_h.at[h, at], step)

    def gradients(m):
        offsets = (m,) if m in (0, NZ // 2) else (m, NZ - m)
        places = [(z + o) % NZ for o in offsets]
        loaded(5, 6)
        for h in range(NH):
            if m > 0:
                arrive("grad", h, m)
        for at in places:
            for h in range(NH):

                @pl.loop(0, tb // ROWS)
                def _(i):
                    rows = pl.ds(pl.multiple_of(i * ROWS, ROWS), ROWS)
                    gh = grad_h[h, at, rows].astype(F32)
                    gate_grad[h, at, rows] = (gh * slope[h, at, rows]).astype(BF16)
                    up_grad[h, at, rows] = (gh * silu[h, at, rows]).astype(BF16)

        def tall(ref):
            return jnp.concatenate([ref[:, at].reshape(NH * tb, -1) for at in places], axis=0)

        sums = dot(tall(gate_grad), wg[...], 1, 1) + dot(tall(up_grad), wu[...], 1, 1)
        for n, o in enumerate(offsets):
            pair_sum[o] = sums[n * NH * tb : (n + 1) * NH * tb].reshape(pair_sum.shape[1:])
            core_send[m, n] = pair_sum[o, :, 1 - core]
        core_copy(m).start()

    def core_copy(m):
        src, dst = core_send.at[m], core_recv.at[m]
        if is_late(m):
            src, dst = src.at[0], dst.at[0]
        return pltpu.make_async_remote_copy(
            src_ref=src, dst_ref=dst, send_sem=core_send_sem.at[m],
            recv_sem=core_recv_sem.at[m], device_id=sibling, device_id_type=MESH,
        )

    late = z % NY

    def is_late(o):
        return o in (0, NZ // 2)

    def x_copy(o, h, to_x, to_y):
        if is_late(o):
            src, dst = x_late_send.at[o // (NZ // 2), h], x_late_recv.at[x]
        else:
            src, dst = x_send.at[o, h], x_recv.at[x, to_y]
        return pltpu.make_async_remote_copy(
            src_ref=src, dst_ref=dst, send_sem=x_send_sem.at[o, h],
            recv_sem=x_recv_sem.at[to_y, x], device_id=at_row(to_x, yl, core), device_id_type=MESH,
        )

    def target(o, h):
        at = h * NZ + (z + o) % NZ
        return at // NY, at % NY

    def outward(m):
        core_copy(m).wait_recv()
        for n, o in enumerate((m,) if is_late(m) else (m, NZ - m)):
            for h in range(NH):
                to_x, to_y = target(o, h)
                total = pair_sum[o, h, core] + core_recv[m, n, h]
                if is_late(o):
                    x_late_send[o // (NZ // 2), h] = total.astype(BF16)
                x_send[o, h] = total

                @pl.when(to_x == x)
                def _():
                    x_own[to_y] = x_send[o, h]

                @pl.when(to_x != x)
                def _():
                    x_copy(o, h, to_x, to_y).start()

    def line_sum(to_y, last):
        total = x_own[to_y]
        for d in range(1, NX):
            src = (x + d) % NX
            dst = x_late_recv.at[src] if last else x_recv.at[src, to_y]
            pltpu.make_async_remote_copy(
                src_ref=dst, dst_ref=dst, send_sem=x_send_sem.at[0, 0],
                recv_sem=x_recv_sem.at[to_y, src], device_id=sibling, device_id_type=MESH,
            ).wait_recv()
            total = total + dst[...].astype(F32)
        return total

    def y_copy(e, src, to_y):
        return pltpu.make_async_remote_copy(
            src_ref=y_late_send if e == 0 else y_send.at[e],
            dst_ref=y_late_recv.at[src] if e == 0 else y_recv.at[src], send_sem=y_send_sem.at[e],
            recv_sem=y_recv_sem.at[src], device_id=at_row(x, to_y, core), device_id_type=MESH,
        )

    def y_start(e):
        to_y = (late + e) % NY
        total = line_sum(to_y, e == 0)
        y_send[e] = total
        if e == 0:
            y_late_send[...] = total.astype(BF16)

        @pl.when(to_y != yl)
        def _():
            y_copy(e, yl, to_y).start()

    width = 256
    stores = []

    def keep(stage, out):
        stores.append(pltpu.make_async_copy(stage, out, here.at[7 + len(stores)]))
        stores[-1].start()

    def down_grads():
        go_flat = go_all[...].reshape(-1, go_all.shape[3])
        for n in range(hidden.shape[3] // width):
            cols = pl.ds(n * width, width)
            st_gd[cols] = dot(hidden[..., cols].reshape(-1, width), go_flat, 0, 0).astype(BF16)
        keep(st_gd, out_gd)

    ops = {
        "goy": go_along_y, "gox": go_along_x, "goc": go_to_core,
        "toky": tok_along_y, "tokx": tok_along_x, "tokc": tok_to_core, "T": tok_turn,
        "acty": act_across, "a": act_ring, "A": activate, "S": share, "r": reduce_step,
        "w": swap, "g": grad_ring, "G": gradients, "O": outward, "D": down_grads,
    }
    for op, *at in ORDER:
        ops[op](*at)

    for i, (grad, stage, out) in enumerate(((gate_grad, st_gg, out_gg), (up_grad, st_gu, out_gu))):
        for n in range(grad.shape[3] // width):
            cols = pl.ds(n * width, width)
            if i == 0 and n == 1:
                outward(4)
                for e in (2, 1, 3):
                    y_start(e)
            if i == 1 and n == 0:
                y_start(0)
            stage[:, cols] = dot(tok_t[...], grad[..., cols].reshape(-1, width), 1, 0).astype(BF16)
        keep(stage, out)

    others = [(yl + d) % NY for d in range(1, NY)]

    @pl.when(yl == late)
    def _():
        total = y_send[0]
        for src in others:
            y_copy(0, src, yl).wait_recv()
            total = total + y_late_recv[src].astype(F32)
        out_gt[...] = total.astype(BF16)

    @pl.when(yl != late)
    def _():
        total = y_send[(yl + NY - late) % NY]
        for src in others:
            y_copy(1, src, yl).wait_recv()
            total = total + y_recv[src]
        out_gt[...] = total.astype(BF16)

    for copy in sent:
        copy.wait_send()

    for m in range(NZ // 2 + 1):
        core_copy(m).wait_send()
    for o in range(NZ):
        for h in range(NH):
            to_x, to_y = target(o, h)

            @pl.when(to_x != x)
            def _():
                x_copy(o, h, to_x, to_y).wait_send()

    for e in range(NY):
        to_y = (late + e) % NY

        @pl.when(to_y != yl)
        def _():
            y_copy(e, yl, to_y).wait_send()

    for store in stores:
        store.wait()


def copy_kernel(*refs):
    sources, results, held, sems = refs[:4], refs[4:8], refs[8:12], refs[12]
    reads = [pltpu.make_async_copy(s, h, sems.at[0, i]) for i, (s, h) in enumerate(zip(sources, held))]
    writes = [pltpu.make_async_copy(h, r, sems.at[1, i]) for i, (h, r) in enumerate(zip(held, results))]
    for read in reads:
        read.start()
    for read, write in zip(reads, writes):
        read.wait()
        write.start()
    for write in writes:
        write.wait()


def on_device(tokens, grad_out, gate_pre, up_pre, w_gate, w_up, w_down):
    th, dd = tokens.shape
    tb, ff = gate_pre.shape
    nrow, ncol = NX * NY, NH * NZ
    anywhere = pl.BlockSpec(memory_space=pl.ANY)
    vmem = pltpu.VMEM
    dma = pltpu.SemaphoreType.DMA
    out = [
        jax.ShapeDtypeStruct(tokens.shape, BF16),
        jax.ShapeDtypeStruct(w_gate.shape, BF16),
        jax.ShapeDtypeStruct(w_up.shape, BF16),
        jax.ShapeDtypeStruct(w_down.shape, BF16),
    ]
    every = (NH, NZ, tb, ff)
    scratch = [
        vmem((nrow, NC, th, dd), BF16),
        vmem((nrow, NC, th, dd), BF16),
        vmem((NH, NZ, 2, tb, ff), BF16),
        vmem((dd, ff), BF16),
        vmem((dd, ff), BF16),
        vmem((ff, dd), BF16),
        vmem(every, F32),
        vmem((NH, 2, 4, tb, ff), BF16),
        vmem((NH, 2, 4, tb, ff), BF16),
        vmem((NH, tb, ff), BF16),
        vmem((NH, tb, ff), BF16),
        vmem(every, BF16),
        vmem(every, F32),
        vmem(every, F32),
        vmem(every, BF16),
        vmem(every, BF16),
        vmem(every, BF16),
        vmem((dd, ncol * tb), BF16),
        vmem((NZ, NH, NC, th, dd), F32),
        vmem((NZ // 2 + 1, 2, NH, th, dd), F32),
        vmem((NZ // 2 + 1, 2, NH, th, dd), F32),
        vmem((NZ, NH, th, dd), F32),
        vmem((NX, NY, th, dd), F32),
        vmem((2, NH, th, dd), BF16),
        vmem((NX, th, dd), BF16),
        vmem((NY, th, dd), F32),
        vmem((NY, th, dd), F32),
        vmem((NY, th, dd), F32),
        vmem((th, dd), BF16),
        vmem((NY, th, dd), BF16),
        vmem((dd, ff), BF16),
        vmem((dd, ff), BF16),
        vmem((ff, dd), BF16),
        dma((COPIES,)),
        dma((COPIES,)),
        dma((NZ,)),
        dma((NZ,)),
        dma((NZ, NH)),
        dma((NY, NX)),
        dma((NY,)),
        dma((NY,)),
        dma((10,)),
    ]
    results = (
        pl.pallas_call(
            kernel,
            out_shape=out,
            in_specs=[anywhere] * 7,
            out_specs=[pl.BlockSpec(memory_space=vmem)] + [anywhere] * 3,
            scratch_shapes=scratch,
            compiler_params=pltpu.CompilerParams(
                collective_id=0, has_side_effects=True, vmem_limit_bytes=56 * 2**20
            ),
            cost_estimate=pl.CostEstimate(
                flops=12 * nrow * NC * th * dd * ff, bytes_accessed=8 * dd * ff * 2, transcendentals=ncol * tb * ff
            ),
        )(tokens, grad_out, gate_pre, up_pre, w_gate, w_up, w_down)
    )
    return tuple(
        pl.pallas_call(
            copy_kernel,
            out_shape=out,
            in_specs=[anywhere] * 4,
            out_specs=[anywhere] * 4,
            scratch_shapes=[vmem(o.shape, o.dtype) for o in out] + [dma((2, 4))],
            compiler_params=pltpu.CompilerParams(vmem_limit_bytes=60 * 2**20),
        )(*results)
    )


def solution(mesh):
    return jax.shard_map(
        on_device,
        mesh=mesh,
        in_specs=(
            P("row", "col"),
            P("row", "col"),
            P("col", "row"),
            P("col", "row"),
            P("col", "row"),
            P("col", "row"),
            P("row", "col"),
        ),
        out_specs=(P("row", "col"), P("col", "row"), P("col", "row"), P("row", "col")),
        check_vma=False,
    )
```

```python
import functools

import jax
import jax.numpy as jnp
from jax import lax
from jax.experimental import pallas as pl
from jax.experimental.pallas import tpu as pltpu
from jax.sharding import PartitionSpec as P

MESH = pl.DeviceIdType.MESH
F32 = jnp.float32
BF16 = jnp.bfloat16
NX, NY, NC = 4, 4, 2
NH, NZ = 2, 8
ROWS = 32
COPIES = 82
ORDER = (
    ("goy",), ("a", 1, 0, 1), ("A", 1, 0), ("acty",), ("a", 1, 1, 1), ("gox",), ("a", 1, 0, 2),
    ("a", 1, 1, 2), ("a", 1, 0, 3), ("goc",), ("a", 1, 1, 3), ("A", 1, 1), ("a", 2, 1, 1), ("S", 4),
    ("r", 1, 1), ("toky",), ("r", 0, 1), ("a", 2, 0, 1), ("S", 2), ("S", 3), ("r", 1, 2), ("tokx",), ("S", 1),
    ("r", 0, 2), ("r", 1, 3), ("A", 1, 3), ("r", 0, 3), ("r", 1, 4), ("A", 2, 1), ("a", 1, 1, 4), ("r", 0, 4),
    ("S", 0), ("w", 1), ("a", 2, 1, 2), ("tokc",), ("A", 1, 2), ("a", 1, 0, 4), ("a", 2, 0, 2), ("w", 0),
    ("a", 2, 1, 3), ("A", 2, 0), ("g", 1, 1), ("T",), ("A", 2, 2), ("g", 0, 1), ("G", 0), ("a", 2, 0, 3),
    ("A", 1, 4), ("g", 1, 2), ("G", 1), ("g", 0, 2), ("A", 2, 3), ("g", 1, 3), ("O", 0), ("O", 1),
    ("g", 0, 3), ("G", 2), ("a", 2, 1, 4), ("a", 2, 0, 4), ("g", 1, 4), ("G", 3), ("O", 2), ("g", 0, 4),
    ("A", 2, 4), ("D",), ("O", 3), ("G", 4),
)


def dot(left, right, left_dim, right_dim):
    return lax.dot_general(
        left, right, (((left_dim,), (right_dim,)), ((), ())), preferred_element_type=F32
    )


def kernel(
    tok_ref, go_ref, gate_ref, up_ref, wg_ref, wu_ref, wd_ref,
    out_gt, out_gg, out_gu, out_gd,
    tok_all, go_all, acts, wg, wu, wd, part, rs_send, rs_recv, swap_send, swap_recv,
    grad_h, silu, slope, hidden, gate_grad, up_grad, tok_t, pair_sum, core_send, core_recv,
    x_send, x_recv, x_late_send, x_late_recv, x_own, y_send, y_recv, y_late_send, y_late_recv, st_gg, st_gu, st_gd,
    send, recv, core_send_sem, core_recv_sem, x_send_sem, x_recv_sem, y_send_sem, y_recv_sem, here,
):
    row, col = lax.axis_index("row"), lax.axis_index("col")
    x, yl, core = row // (NY * NC), (row // NC) % NY, row % NC
    yh, z = col // NZ, col % NZ
    tb, half = acts.shape[3], acts.shape[3] // 2

    def at_row(px, py, pc):
        return (px * (NY * NC) + py * NC + pc, col)

    def at_col(ph, pz):
        return (row, ph * NZ + pz)

    xs = [at_row((x + d) % NX, yl, core) for d in range(1, NX)]
    ys = [at_row(x, (yl + d) % NY, core) for d in range(1, NY)]
    sibling = at_row(x, yl, 1 - core)
    ahead, behind = at_col(yh, (z + 1) % NZ), at_col(yh, (z + NZ - 1) % NZ)
    across = at_col(1 - yh, z)

    sent = []
    coming = {}

    def push(src, dst, to):
        n = len(sent)
        copy = pltpu.make_async_remote_copy(
            src_ref=src, dst_ref=dst, send_sem=send.at[n], recv_sem=recv.at[n],
            device_id=to, device_id_type=MESH,
        )
        copy.start()
        sent.append(copy)
        return copy

    def arrive(*key):
        for copy in coming[key]:
            copy.wait_recv()
        coming[key] = ()

    def loaded(*which):
        for i in which:
            if loads[i] is not None:
                loads[i].wait()
                loads[i] = None

    mine = x * NY + yl
    loads = [
        (go_ref, go_all.at[mine, core]), (tok_ref, tok_all.at[mine, core]),
        (gate_ref, acts.at[0, yh, z]), (up_ref, acts.at[1, yh, z]),
        (wd_ref, wd), (wg_ref, wg), (wu_ref, wu),
    ]
    loads = [pltpu.make_async_copy(s, d, here.at[i]) for i, (s, d) in enumerate(loads)]
    for load in loads:
        load.start()

    barrier = pltpu.get_barrier_semaphore()
    partners = xs + ys + [sibling, ahead, behind, across]
    for to in partners:
        pl.semaphore_signal(barrier, inc=1, device_id=to, device_id_type=MESH)
    pl.semaphore_wait(barrier, len(partners))

    def ring_send(block, k, step, first=None):
        copies = []
        for way, to in ((1, ahead), (-1, behind)):
            at = (z + (NZ - way * (step - 1))) % NZ
            ref = block(k, at)
            if step == NZ // 2:
                ref = ref.at[pl.ds(0 if way == 1 else half, half)]
            copies.append(push(ref if first is None else first, ref, to))
        return copies

    def own_act(k, at):
        return acts.at[k, yh, at]

    def other_act(k, at):
        return acts.at[k, 1 - yh, at]

    def grad_block(k, at):
        return grad_h.at[k, at]

    def pair_loop(m, step):
        if m in (0, NZ // 2):
            step(m)
        else:
            pl.loop(0, 2)(lambda i: step(m + (NZ - 2 * m) * i))

    def activate(ring, m):
        h = yh if ring == 1 else 1 - yh
        if m == 0 and ring == 1:
            loaded(2, 3)
        elif m == 0:
            arrive("act_y")
        else:
            arrive("act", ring, 0, m)
            arrive("act", ring, 1, m)

        def step(o):
            at = (z + o) % NZ

            @pl.loop(0, tb // ROWS)
            def _(i):
                rows = pl.ds(pl.multiple_of(i * ROWS, ROWS), ROWS)
                g = acts[0, h, at, rows].astype(F32)
                u = acts[1, h, at, rows].astype(F32)
                s = jax.nn.sigmoid(g)
                gs = g * s
                silu[h, at, rows] = gs
                slope[h, at, rows] = u * s * (1.0 + g * (1.0 - s))
                hidden[h, at, rows] = (gs * u).astype(BF16)

        pair_loop(m, step)

    def share(m):
        arrive("go_core")
        loaded(4)

        def step(o):
            at = (z + o) % NZ
            rows = jnp.concatenate(
                [go_all[h * NZ + at].reshape(tb, -1) for h in range(NH)], axis=0
            )
            sums = dot(rows, wd[...], 1, 1)
            for h in range(NH):
                part[h, at] = sums[h * tb : (h + 1) * tb]

        pair_loop(m, step)

    def reduce_step(h, step):
        copies = []
        for w, (way, to) in enumerate(((1, ahead), (-1, behind))):
            at = (z + (NZ + way * (NZ // 2 + 1 - step))) % NZ
            out = rs_send.at[h, w, step - 1]
            rows = pl.ds(0 if way == 1 else half, half)
            if step == 1:
                out[rows] = part[h, at, rows].astype(BF16)
                copies.append(push(out.at[rows], rs_recv.at[h, w, 0, rows], to))
                continue
            coming["sums", h, step - 1][w].wait_recv()
            if step == 2:
                rest = pl.ds(half if way == 1 else 0, half)
                out[rows] = (part[h, at, rows] + rs_recv[h, w, 0, rows].astype(F32)).astype(BF16)
                out[rest] = part[h, at, rest].astype(BF16)
            else:
                out[...] = (part[h, at] + rs_recv[h, w, step - 2].astype(F32)).astype(BF16)
            copies.append(push(out, rs_recv.at[h, w, step - 1], to))
        coming["sums", h, step] = copies

    def spread(own, copies_of, source):
        return [push(source, own, to) for to in copies_of]

    def x_line(ref):
        return ref.at[pl.ds(x * NY, NY), core]

    def go_along_y():
        coming[("go_y",)] = spread(go_all.at[mine, core], ys, go_ref)

    def go_along_x():
        loaded(0)
        arrive("go_y")
        coming[("go_x",)] = spread(x_line(go_all), xs, x_line(go_all))

    def go_to_core():
        arrive("go_x")
        coming[("go_core",)] = [push(go_all.at[:, core], go_all.at[:, core], sibling)]

    def tok_along_y():
        coming[("tok_y",)] = spread(tok_all.at[mine, core], ys, tok_ref)

    def tok_along_x():
        loaded(1)
        arrive("tok_y")
        coming[("tok_x",)] = spread(x_line(tok_all), xs, x_line(tok_all))

    def tok_to_core():
        arrive("tok_x")
        coming[("tok_core",)] = [push(tok_all.at[:, core], tok_all.at[:, core], sibling)]

    def tok_turn():
        arrive("tok_core")
        tok_t[...] = tok_all[...].reshape(-1, tok_all.shape[3]).T

    def act_across():
        refs = enumerate((gate_ref, up_ref))
        coming[("act_y",)] = [push(ref, acts.at[k, yh, z], across) for k, ref in refs]

    def act_ring(ring, k, step):
        first = None
        if step > 1:
            arrive("act", ring, k, step - 1)
        elif ring == 1:
            first = (gate_ref, up_ref)[k]
        else:
            arrive("act_y")
        coming["act", ring, k, step] = ring_send(own_act if ring == 1 else other_act, k, step, first)

    def swap(h):
        arrive("sums", h, 4)
        total = part[h, z] + rs_recv[h, 0, 3].astype(F32) + rs_recv[h, 1, 3].astype(F32)
        part[h, z] = total
        swap_send[h] = total.astype(BF16)
        coming["swap", h] = [push(swap_send.at[h], swap_recv.at[h], across)]

    def grad_ring(h, step):
        if step == 1:
            arrive("swap", h)
            grad_h[h, z] = (part[h, z] + swap_recv[h].astype(F32)).astype(BF16)
        else:
            arrive("grad", h, step - 1)
        coming["grad", h, step] = ring_send(grad_block, h, step)

    def gradients(m):
        offsets = (m,) if m in (0, NZ // 2) else (m, NZ - m)
        places = [(z + o) % NZ for o in offsets]
        loaded(5, 6)
        for h in range(NH):
            if m > 0:
                arrive("grad", h, m)
        for at in places:
            for h in range(NH):

                @pl.loop(0, tb // ROWS)
                def _(i):
                    rows = pl.ds(pl.multiple_of(i * ROWS, ROWS), ROWS)
                    gh = grad_h[h, at, rows].astype(F32)
                    gate_grad[h, at, rows] = (gh * slope[h, at, rows]).astype(BF16)
                    up_grad[h, at, rows] = (gh * silu[h, at, rows]).astype(BF16)

        def tall(ref):
            return jnp.concatenate([ref[:, at].reshape(NH * tb, -1) for at in places], axis=0)

        sums = dot(tall(gate_grad), wg[...], 1, 1) + dot(tall(up_grad), wu[...], 1, 1)
        for n, o in enumerate(offsets):
            pair_sum[o] = sums[n * NH * tb : (n + 1) * NH * tb].reshape(pair_sum.shape[1:])
            core_send[m, n] = pair_sum[o, :, 1 - core]
        core_copy(m).start()

    def core_copy(m):
        src, dst = core_send.at[m], core_recv.at[m]
        if is_late(m):
            src, dst = src.at[0], dst.at[0]
        return pltpu.make_async_remote_copy(
            src_ref=src, dst_ref=dst, send_sem=core_send_sem.at[m],
            recv_sem=core_recv_sem.at[m], device_id=sibling, device_id_type=MESH,
        )

    late = z % NY

    def is_late(o):
        return o in (0, NZ // 2)

    def x_copy(o, h, to_x, to_y):
        if is_late(o):
            src, dst = x_late_send.at[o // (NZ // 2), h], x_late_recv.at[x]
        else:
            src, dst = x_send.at[o, h], x_recv.at[x, to_y]
        return pltpu.make_async_remote_copy(
            src_ref=src, dst_ref=dst, send_sem=x_send_sem.at[o, h],
            recv_sem=x_recv_sem.at[to_y, x], device_id=at_row(to_x, yl, core), device_id_type=MESH,
        )

    def target(o, h):
        at = h * NZ + (z + o) % NZ
        return at // NY, at % NY

    def outward(m):
        core_copy(m).wait_recv()
        for n, o in enumerate((m,) if is_late(m) else (m, NZ - m)):
            for h in range(NH):
                to_x, to_y = target(o, h)
                total = pair_sum[o, h, core] + core_recv[m, n, h]
                if is_late(o):
                    x_late_send[o // (NZ // 2), h] = total.astype(BF16)
                x_send[o, h] = total

                @pl.when(to_x == x)
                def _():
                    x_own[to_y] = x_send[o, h]

                @pl.when(to_x != x)
                def _():
                    x_copy(o, h, to_x, to_y).start()

    def line_sum(to_y, last):
        total = x_own[to_y]
        for d in range(1, NX):
            src = (x + d) % NX
            dst = x_late_recv.at[src] if last else x_recv.at[src, to_y]
            pltpu.make_async_remote_copy(
                src_ref=dst, dst_ref=dst, send_sem=x_send_sem.at[0, 0],
                recv_sem=x_recv_sem.at[to_y, src], device_id=sibling, device_id_type=MESH,
            ).wait_recv()
            total = total + dst[...].astype(F32)
        return total

    def y_copy(e, src, to_y):
        return pltpu.make_async_remote_copy(
            src_ref=y_late_send if e == 0 else y_send.at[e],
            dst_ref=y_late_recv.at[src] if e == 0 else y_recv.at[src], send_sem=y_send_sem.at[e],
            recv_sem=y_recv_sem.at[src], device_id=at_row(x, to_y, core), device_id_type=MESH,
        )

    def y_start(e):
        to_y = (late + e) % NY
        total = line_sum(to_y, e == 0)
        y_send[e] = total
        if e == 0:
            y_late_send[...] = total.astype(BF16)

        @pl.when(to_y != yl)
        def _():
            y_copy(e, yl, to_y).start()

    width = 256
    stores = []

    def keep(stage, out):
        stores.append(pltpu.make_async_copy(stage, out, here.at[7 + len(stores)]))
        stores[-1].start()

    def down_grads():
        go_flat = go_all[...].reshape(-1, go_all.shape[3])
        for n in range(hidden.shape[3] // width):
            cols = pl.ds(n * width, width)
            st_gd[cols] = dot(hidden[..., cols].reshape(-1, width), go_flat, 0, 0).astype(BF16)
        keep(st_gd, out_gd)

    ops = {
        "goy": go_along_y, "gox": go_along_x, "goc": go_to_core,
        "toky": tok_along_y, "tokx": tok_along_x, "tokc": tok_to_core, "T": tok_turn,
        "acty": act_across, "a": act_ring, "A": activate, "S": share, "r": reduce_step,
        "w": swap, "g": grad_ring, "G": gradients, "O": outward, "D": down_grads,
    }
    for op, *at in ORDER:
        ops[op](*at)

    for i, (grad, stage, out) in enumerate(((gate_grad, st_gg, out_gg), (up_grad, st_gu, out_gu))):
        for n in range(grad.shape[3] // width):
            cols = pl.ds(n * width, width)
            if i == 0 and n == 1:
                outward(4)
                for e in (2, 1, 3):
                    y_start(e)
            if i == 1 and n == 0:
                y_start(0)
            stage[:, cols] = dot(tok_t[...], grad[..., cols].reshape(-1, width), 1, 0).astype(BF16)
        keep(stage, out)

    others = [(yl + d) % NY for d in range(1, NY)]

    @pl.when(yl == late)
    def _():
        total = y_send[0]
        for src in others:
            y_copy(0, src, yl).wait_recv()
            total = total + y_late_recv[src].astype(F32)
        out_gt[...] = total.astype(BF16)

    @pl.when(yl != late)
    def _():
        total = y_send[(yl + NY - late) % NY]
        for src in others:
            y_copy(1, src, yl).wait_recv()
            total = total + y_recv[src]
        out_gt[...] = total.astype(BF16)

    for copy in sent:
        copy.wait_send()

    for m in range(NZ // 2 + 1):
        core_copy(m).wait_send()
    for o in range(NZ):
        for h in range(NH):
            to_x, to_y = target(o, h)

            @pl.when(to_x != x)
            def _():
                x_copy(o, h, to_x, to_y).wait_send()

    for e in range(NY):
        to_y = (late + e) % NY

        @pl.when(to_y != yl)
        def _():
            y_copy(e, yl, to_y).wait_send()

    for store in stores:
        store.wait()


def copy_kernel(*refs):
    sources, results, held, sems = refs[:4], refs[4:8], refs[8:12], refs[12]
    reads = [pltpu.make_async_copy(s, h, sems.at[0, i]) for i, (s, h) in enumerate(zip(sources, held))]
    writes = [pltpu.make_async_copy(h, r, sems.at[1, i]) for i, (h, r) in enumerate(zip(held, results))]
    for read in reads:
        read.start()
    for read, write in zip(reads, writes):
        read.wait()
        write.start()
    for write in writes:
        write.wait()


def on_device(tokens, grad_out, gate_pre, up_pre, w_gate, w_up, w_down):
    th, dd = tokens.shape
    tb, ff = gate_pre.shape
    nrow, ncol = NX * NY, NH * NZ
    anywhere = pl.BlockSpec(memory_space=pl.ANY)
    vmem = pltpu.VMEM
    dma = pltpu.SemaphoreType.DMA
    out = [
        jax.ShapeDtypeStruct(tokens.shape, BF16),
        jax.ShapeDtypeStruct(w_gate.shape, BF16),
        jax.ShapeDtypeStruct(w_up.shape, BF16),
        jax.ShapeDtypeStruct(w_down.shape, BF16),
    ]
    every = (NH, NZ, tb, ff)
    scratch = [
        vmem((nrow, NC, th, dd), BF16),
        vmem((nrow, NC, th, dd), BF16),
        vmem((2,) + every, BF16),
        vmem((dd, ff), BF16),
        vmem((dd, ff), BF16),
        vmem((ff, dd), BF16),
        vmem(every, F32),
        vmem((NH, 2, 4, tb, ff), BF16),
        vmem((NH, 2, 4, tb, ff), BF16),
        vmem((NH, tb, ff), BF16),
        vmem((NH, tb, ff), BF16),
        vmem(every, BF16),
        vmem(every, F32),
        vmem(every, F32),
        vmem(every, BF16),
        vmem(every, BF16),
        vmem(every, BF16),
        vmem((dd, ncol * tb), BF16),
        vmem((NZ, NH, NC, th, dd), F32),
        vmem((NZ // 2 + 1, 2, NH, th, dd), F32),
        vmem((NZ // 2 + 1, 2, NH, th, dd), F32),
        vmem((NZ, NH, th, dd), F32),
        vmem((NX, NY, th, dd), F32),
        vmem((2, NH, th, dd), BF16),
        vmem((NX, th, dd), BF16),
        vmem((NY, th, dd), F32),
        vmem((NY, th, dd), F32),
        vmem((NY, th, dd), F32),
        vmem((th, dd), BF16),
        vmem((NY, th, dd), BF16),
        vmem((dd, ff), BF16),
        vmem((dd, ff), BF16),
        vmem((ff, dd), BF16),
        dma((COPIES,)),
        dma((COPIES,)),
        dma((NZ,)),
        dma((NZ,)),
        dma((NZ, NH)),
        dma((NY, NX)),
        dma((NY,)),
        dma((NY,)),
        dma((10,)),
    ]
    results = (
        pl.pallas_call(
            kernel,
            out_shape=out,
            in_specs=[anywhere] * 7,
            out_specs=[pl.BlockSpec(memory_space=vmem)] + [anywhere] * 3,
            scratch_shapes=scratch,
            compiler_params=pltpu.CompilerParams(
                collective_id=0, has_side_effects=True, vmem_limit_bytes=56 * 2**20
            ),
            cost_estimate=pl.CostEstimate(
                flops=12 * nrow * NC * th * dd * ff, bytes_accessed=8 * dd * ff * 2, transcendentals=ncol * tb * ff
            ),
        )(tokens, grad_out, gate_pre, up_pre, w_gate, w_up, w_down)
    )
    return tuple(
        pl.pallas_call(
            copy_kernel,
            out_shape=out,
            in_specs=[anywhere] * 4,
            out_specs=[anywhere] * 4,
            scratch_shapes=[vmem(o.shape, o.dtype) for o in out] + [dma((2, 4))],
            compiler_params=pltpu.CompilerParams(vmem_limit_bytes=60 * 2**20),
        )(*results)
    )


def solution(mesh):
    return jax.shard_map(
        on_device,
        mesh=mesh,
        in_specs=(
            P("row", "col"),
            P("row", "col"),
            P("col", "row"),
            P("col", "row"),
            P("col", "row"),
            P("col", "row"),
            P("row", "col"),
        ),
        out_specs=(P("row", "col"), P("col", "row"), P("col", "row"), P("row", "col")),
        check_vma=False,
    )
```

```python
import functools

import jax
import jax.numpy as jnp
from jax import lax
from jax.experimental import pallas as pl
from jax.experimental.pallas import tpu as pltpu
from jax.sharding import PartitionSpec as P

MESH = pl.DeviceIdType.MESH
F32 = jnp.float32
BF16 = jnp.bfloat16
NX, NY, NC = 4, 4, 2
NH, NZ = 2, 8
ROWS = 32
COPIES = 82
ORDER = (
    ("goy",), ("a", 1, 1, 1), ("toky",), ("a", 1, 0, 1), ("gox",), ("a", 1, 1, 2), ("a", 1, 0, 2),
    ("a", 1, 1, 3), ("goc",), ("acty",), ("a", 1, 0, 3), ("a", 1, 1, 4), ("S", 4), ("r", 1, 1),
    ("a", 1, 0, 4), ("r", 0, 1), ("tokx",), ("S", 3), ("r", 1, 2), ("r", 0, 2), ("S", 2), ("r", 1, 3),
    ("S", 1), ("tokc",), ("r", 0, 3), ("r", 1, 4), ("A", 1, 4), ("r", 0, 4), ("S", 0), ("A", 2, 0),
    ("a", 2, 1, 1), ("w", 1), ("a", 2, 0, 1), ("w", 0), ("A", 1, 2), ("a", 2, 1, 2), ("a", 2, 0, 2),
    ("g", 1, 1), ("A", 2, 1), ("A", 1, 0), ("a", 2, 1, 3), ("A", 1, 1), ("T",), ("g", 0, 1), ("G", 0),
    ("g", 1, 2), ("A", 1, 3), ("A", 2, 2), ("g", 0, 2), ("a", 2, 0, 3), ("G", 1), ("g", 1, 3), ("O", 0),
    ("g", 0, 3), ("G", 2), ("a", 2, 0, 4), ("a", 2, 1, 4), ("O", 1), ("A", 2, 3), ("g", 1, 4), ("O", 2),
    ("G", 3), ("g", 0, 4), ("A", 2, 4), ("D",), ("O", 3), ("G", 4),
)


def dot(left, right, left_dim, right_dim):
    return lax.dot_general(
        left, right, (((left_dim,), (right_dim,)), ((), ())), preferred_element_type=F32
    )


def kernel(
    tok_ref, go_ref, gate_ref, up_ref, wg_ref, wu_ref, wd_ref,
    out_gt, out_gg, out_gu, out_gd,
    tok_all, go_all, acts, wg, wu, wd, part, rs_send, rs_recv, swap_send, swap_recv,
    grad_h, silu, slope, hidden, gate_grad, up_grad, tok_t, pair_sum, core_send, core_recv,
    x_send, x_recv, x_late_send, x_late_recv, x_own, y_send, y_recv, y_late_send, y_late_recv, st_gg, st_gu, st_gd,
    send, recv, core_send_sem, core_recv_sem, x_send_sem, x_recv_sem, y_send_sem, y_recv_sem, here,
):
    row, col = lax.axis_index("row"), lax.axis_index("col")
    x, yl, core = row // (NY * NC), (row // NC) % NY, row % NC
    yh, z = col // NZ, col % NZ
    tb, half = acts.shape[3], acts.shape[3] // 2

    def at_row(px, py, pc):
        return (px * (NY * NC) + py * NC + pc, col)

    def at_col(ph, pz):
        return (row, ph * NZ + pz)

    xs = [at_row((x + d) % NX, yl, core) for d in range(1, NX)]
    ys = [at_row(x, (yl + d) % NY, core) for d in range(1, NY)]
    sibling = at_row(x, yl, 1 - core)
    ahead, behind = at_col(yh, (z + 1) % NZ), at_col(yh, (z + NZ - 1) % NZ)
    across = at_col(1 - yh, z)

    sent = []
    coming = {}

    def push(src, dst, to):
        n = len(sent)
        copy = pltpu.make_async_remote_copy(
            src_ref=src, dst_ref=dst, send_sem=send.at[n], recv_sem=recv.at[n],
            device_id=to, device_id_type=MESH,
        )
        copy.start()
        sent.append(copy)
        return copy

    def arrive(*key):
        for copy in coming[key]:
            copy.wait_recv()
        coming[key] = ()

    def loaded(*which):
        for i in which:
            if loads[i] is not None:
                loads[i].wait()
                loads[i] = None

    mine = x * NY + yl
    loads = [
        (go_ref, go_all.at[mine, core]), (tok_ref, tok_all.at[mine, core]),
        (gate_ref, acts.at[0, yh, z]), (up_ref, acts.at[1, yh, z]),
        (wd_ref, wd), (wg_ref, wg), (wu_ref, wu),
    ]
    loads = [pltpu.make_async_copy(s, d, here.at[i]) for i, (s, d) in enumerate(loads)]
    for load in loads:
        load.start()

    barrier = pltpu.get_barrier_semaphore()
    partners = xs + ys + [sibling, ahead, behind, across]
    for to in partners:
        pl.semaphore_signal(barrier, inc=1, device_id=to, device_id_type=MESH)
    pl.semaphore_wait(barrier, len(partners))

    def ring_send(block, k, step, first=None):
        copies = []
        for way, to in ((1, ahead), (-1, behind)):
            at = (z + (NZ - way * (step - 1))) % NZ
            ref = block(k, at)
            if step == NZ // 2:
                ref = ref.at[pl.ds(0 if way == 1 else half, half)]
            copies.append(push(ref if first is None else first, ref, to))
        return copies

    def own_act(k, at):
        return acts.at[k, yh, at]

    def other_act(k, at):
        return acts.at[k, 1 - yh, at]

    def grad_block(k, at):
        return grad_h.at[k, at]

    def pair_loop(m, step):
        if m in (0, NZ // 2):
            step(m)
        else:
            pl.loop(0, 2)(lambda i: step(m + (NZ - 2 * m) * i))

    def activate(ring, m):
        h = yh if ring == 1 else 1 - yh
        if m == 0 and ring == 1:
            loaded(2, 3)
        elif m == 0:
            arrive("act_y")
        else:
            arrive("act", ring, 0, m)
            arrive("act", ring, 1, m)

        def step(o):
            at = (z + o) % NZ

            @pl.loop(0, tb // ROWS)
            def _(i):
                rows = pl.ds(pl.multiple_of(i * ROWS, ROWS), ROWS)
                g = acts[0, h, at, rows].astype(F32)
                u = acts[1, h, at, rows].astype(F32)
                s = jax.nn.sigmoid(g)
                gs = g * s
                silu[h, at, rows] = gs
                slope[h, at, rows] = u * s * (1.0 + g * (1.0 - s))
                hidden[h, at, rows] = (gs * u).astype(BF16)

        pair_loop(m, step)

    def share(m):
        arrive("go_core")
        loaded(4)

        def step(o):
            at = (z + o) % NZ
            rows = jnp.concatenate(
                [go_all[h * NZ + at].reshape(tb, -1) for h in range(NH)], axis=0
            )
            sums = dot(rows, wd[...], 1, 1)
            for h in range(NH):
                part[h, at] = sums[h * tb : (h + 1) * tb]

        pair_loop(m, step)

    def reduce_step(h, step):
        copies = []
        for w, (way, to) in enumerate(((1, ahead), (-1, behind))):
            at = (z + (NZ + way * (NZ // 2 + 1 - step))) % NZ
            out = rs_send.at[h, w, step - 1]
            rows = pl.ds(0 if way == 1 else half, half)
            if step == 1:
                out[rows] = part[h, at, rows].astype(BF16)
                copies.append(push(out.at[rows], rs_recv.at[h, w, 0, rows], to))
                continue
            coming["sums", h, step - 1][w].wait_recv()
            if step == 2:
                rest = pl.ds(half if way == 1 else 0, half)
                out[rows] = (part[h, at, rows] + rs_recv[h, w, 0, rows].astype(F32)).astype(BF16)
                out[rest] = part[h, at, rest].astype(BF16)
            else:
                out[...] = (part[h, at] + rs_recv[h, w, step - 2].astype(F32)).astype(BF16)
            copies.append(push(out, rs_recv.at[h, w, step - 1], to))
        coming["sums", h, step] = copies

    def spread(own, copies_of, source):
        return [push(source, own, to) for to in copies_of]

    def x_line(ref):
        return ref.at[pl.ds(x * NY, NY), core]

    def go_along_y():
        coming[("go_y",)] = spread(go_all.at[mine, core], ys, go_ref)

    def go_along_x():
        loaded(0)
        arrive("go_y")
        coming[("go_x",)] = spread(x_line(go_all), xs, x_line(go_all))

    def go_to_core():
        arrive("go_x")
        coming[("go_core",)] = [push(go_all.at[:, core], go_all.at[:, core], sibling)]

    def tok_along_y():
        coming[("tok_y",)] = spread(tok_all.at[mine, core], ys, tok_ref)

    def tok_along_x():
        loaded(1)
        arrive("tok_y")
        coming[("tok_x",)] = spread(x_line(tok_all), xs, x_line(tok_all))

    def tok_to_core():
        arrive("tok_x")
        coming[("tok_core",)] = [push(tok_all.at[:, core], tok_all.at[:, core], sibling)]

    def tok_turn():
        arrive("tok_core")
        tok_t[...] = tok_all[...].reshape(-1, tok_all.shape[3]).T

    def act_across():
        refs = enumerate((gate_ref, up_ref))
        coming[("act_y",)] = [push(ref, acts.at[k, yh, z], across) for k, ref in refs]

    def act_ring(ring, k, step):
        first = None
        if step > 1:
            arrive("act", ring, k, step - 1)
        elif ring == 1:
            first = (gate_ref, up_ref)[k]
        else:
            arrive("act_y")
        coming["act", ring, k, step] = ring_send(own_act if ring == 1 else other_act, k, step, first)

    def swap(h):
        arrive("sums", h, 4)
        total = part[h, z] + rs_recv[h, 0, 3].astype(F32) + rs_recv[h, 1, 3].astype(F32)
        part[h, z] = total
        swap_send[h] = total.astype(BF16)
        coming["swap", h] = [push(swap_send.at[h], swap_recv.at[h], across)]

    def grad_ring(h, step):
        if step == 1:
            arrive("swap", h)
            grad_h[h, z] = (part[h, z] + swap_recv[h].astype(F32)).astype(BF16)
        else:
            arrive("grad", h, step - 1)
        coming["grad", h, step] = ring_send(grad_block, h, step)

    def gradients(m):
        offsets = (m,) if m in (0, NZ // 2) else (m, NZ - m)
        places = [(z + o) % NZ for o in offsets]
        loaded(5, 6)
        for h in range(NH):
            if m > 0:
                arrive("grad", h, m)
        for at in places:
            for h in range(NH):

                @pl.loop(0, tb // ROWS)
                def _(i):
                    rows = pl.ds(pl.multiple_of(i * ROWS, ROWS), ROWS)
                    gh = grad_h[h, at, rows].astype(F32)
                    gate_grad[h, at, rows] = (gh * slope[h, at, rows]).astype(BF16)
                    up_grad[h, at, rows] = (gh * silu[h, at, rows]).astype(BF16)

        def tall(ref):
            return jnp.concatenate([ref[:, at].reshape(NH * tb, -1) for at in places], axis=0)

        sums = dot(tall(gate_grad), wg[...], 1, 1) + dot(tall(up_grad), wu[...], 1, 1)
        for n, o in enumerate(offsets):
            pair_sum[o] = sums[n * NH * tb : (n + 1) * NH * tb].reshape(pair_sum.shape[1:])
            core_send[m, n] = pair_sum[o, :, 1 - core]
        core_copy(m).start()

    def core_copy(m):
        src, dst = core_send.at[m], core_recv.at[m]
        if is_late(m):
            src, dst = src.at[0], dst.at[0]
        return pltpu.make_async_remote_copy(
            src_ref=src, dst_ref=dst, send_sem=core_send_sem.at[m],
            recv_sem=core_recv_sem.at[m], device_id=sibling, device_id_type=MESH,
        )

    late = z % NY

    def is_late(o):
        return o in (0, NZ // 2)

    def x_copy(o, h, to_x, to_y):
        if is_late(o):
            src, dst = x_late_send.at[o // (NZ // 2), h], x_late_recv.at[x]
        else:
            src, dst = x_send.at[o, h], x_recv.at[x, to_y]
        return pltpu.make_async_remote_copy(
            src_ref=src, dst_ref=dst, send_sem=x_send_sem.at[o, h],
            recv_sem=x_recv_sem.at[to_y, x], device_id=at_row(to_x, yl, core), device_id_type=MESH,
        )

    def target(o, h):
        at = h * NZ + (z + o) % NZ
        return at // NY, at % NY

    def outward(m):
        core_copy(m).wait_recv()
        for n, o in enumerate((m,) if is_late(m) else (m, NZ - m)):
            for h in range(NH):
                to_x, to_y = target(o, h)
                total = pair_sum[o, h, core] + core_recv[m, n, h]
                if is_late(o):
                    x_late_send[o // (NZ // 2), h] = total.astype(BF16)
                x_send[o, h] = total

                @pl.when(to_x == x)
                def _():
                    x_own[to_y] = x_send[o, h]

                @pl.when(to_x != x)
                def _():
                    x_copy(o, h, to_x, to_y).start()

    def line_sum(to_y, last):
        total = x_own[to_y]
        for d in range(1, NX):
            src = (x + d) % NX
            dst = x_late_recv.at[src] if last else x_recv.at[src, to_y]
            pltpu.make_async_remote_copy(
                src_ref=dst, dst_ref=dst, send_sem=x_send_sem.at[0, 0],
                recv_sem=x_recv_sem.at[to_y, src], device_id=sibling, device_id_type=MESH,
            ).wait_recv()
            total = total + dst[...].astype(F32)
        return total

    def y_copy(e, src, to_y):
        return pltpu.make_async_remote_copy(
            src_ref=y_late_send if e == 0 else y_send.at[e],
            dst_ref=y_late_recv.at[src] if e == 0 else y_recv.at[src], send_sem=y_send_sem.at[e],
            recv_sem=y_recv_sem.at[src], device_id=at_row(x, to_y, core), device_id_type=MESH,
        )

    def y_start(e):
        to_y = (late + e) % NY
        total = line_sum(to_y, e == 0)
        y_send[e] = total
        if e == 0:
            y_late_send[...] = total.astype(BF16)

        @pl.when(to_y != yl)
        def _():
            y_copy(e, yl, to_y).start()

    width = 256
    stores = []

    def keep(stage, out):
        stores.append(pltpu.make_async_copy(stage, out, here.at[7 + len(stores)]))
        stores[-1].start()

    def down_grads():
        go_flat = go_all[...].reshape(-1, go_all.shape[3])
        for n in range(hidden.shape[3] // width):
            cols = pl.ds(n * width, width)
            st_gd[cols] = dot(hidden[..., cols].reshape(-1, width), go_flat, 0, 0).astype(BF16)
        keep(st_gd, out_gd)

    ops = {
        "goy": go_along_y, "gox": go_along_x, "goc": go_to_core,
        "toky": tok_along_y, "tokx": tok_along_x, "tokc": tok_to_core, "T": tok_turn,
        "acty": act_across, "a": act_ring, "A": activate, "S": share, "r": reduce_step,
        "w": swap, "g": grad_ring, "G": gradients, "O": outward, "D": down_grads,
    }
    for op, *at in ORDER:
        ops[op](*at)

    for i, (grad, stage, out) in enumerate(((gate_grad, st_gg, out_gg), (up_grad, st_gu, out_gu))):
        for n in range(grad.shape[3] // width):
            cols = pl.ds(n * width, width)
            if i == 0 and n == 1:
                outward(4)
                for e in (2, 1, 3):
                    y_start(e)
            if i == 1 and n == 0:
                y_start(0)
            stage[:, cols] = dot(tok_t[...], grad[..., cols].reshape(-1, width), 1, 0).astype(BF16)
        keep(stage, out)

    others = [(yl + d) % NY for d in range(1, NY)]

    @pl.when(yl == late)
    def _():
        total = y_send[0]
        for src in others:
            y_copy(0, src, yl).wait_recv()
            total = total + y_late_recv[src].astype(F32)
        out_gt[...] = total.astype(BF16)

    @pl.when(yl != late)
    def _():
        total = y_send[(yl + NY - late) % NY]
        for src in others:
            y_copy(1, src, yl).wait_recv()
            total = total + y_recv[src]
        out_gt[...] = total.astype(BF16)

    for copy in sent:
        copy.wait_send()

    for m in range(NZ // 2 + 1):
        core_copy(m).wait_send()
    for o in range(NZ):
        for h in range(NH):
            to_x, to_y = target(o, h)

            @pl.when(to_x != x)
            def _():
                x_copy(o, h, to_x, to_y).wait_send()

    for e in range(NY):
        to_y = (late + e) % NY

        @pl.when(to_y != yl)
        def _():
            y_copy(e, yl, to_y).wait_send()

    for store in stores:
        store.wait()


def copy_kernel(*refs):
    sources, results, held, sems = refs[:4], refs[4:8], refs[8:12], refs[12]
    reads = [pltpu.make_async_copy(s, h, sems.at[0, i]) for i, (s, h) in enumerate(zip(sources, held))]
    writes = [pltpu.make_async_copy(h, r, sems.at[1, i]) for i, (h, r) in enumerate(zip(held, results))]
    for read in reads:
        read.start()
    for read, write in zip(reads, writes):
        read.wait()
        write.start()
    for write in writes:
        write.wait()


def on_device(tokens, grad_out, gate_pre, up_pre, w_gate, w_up, w_down):
    th, dd = tokens.shape
    tb, ff = gate_pre.shape
    nrow, ncol = NX * NY, NH * NZ
    anywhere = pl.BlockSpec(memory_space=pl.ANY)
    vmem = pltpu.VMEM
    dma = pltpu.SemaphoreType.DMA
    out = [
        jax.ShapeDtypeStruct(tokens.shape, BF16),
        jax.ShapeDtypeStruct(w_gate.shape, BF16),
        jax.ShapeDtypeStruct(w_up.shape, BF16),
        jax.ShapeDtypeStruct(w_down.shape, BF16),
    ]
    every = (NH, NZ, tb, ff)
    scratch = [
        vmem((nrow, NC, th, dd), BF16),
        vmem((nrow, NC, th, dd), BF16),
        vmem((2,) + every, BF16),
        vmem((dd, ff), BF16),
        vmem((dd, ff), BF16),
        vmem((ff, dd), BF16),
        vmem(every, F32),
        vmem((NH, 2, 4, tb, ff), BF16),
        vmem((NH, 2, 4, tb, ff), BF16),
        vmem((NH, tb, ff), BF16),
        vmem((NH, tb, ff), BF16),
        vmem(every, BF16),
        vmem(every, F32),
        vmem(every, F32),
        vmem(every, BF16),
        vmem(every, BF16),
        vmem(every, BF16),
        vmem((dd, ncol * tb), BF16),
        vmem((NZ, NH, NC, th, dd), F32),
        vmem((NZ // 2 + 1, 2, NH, th, dd), F32),
        vmem((NZ // 2 + 1, 2, NH, th, dd), F32),
        vmem((NZ, NH, th, dd), F32),
        vmem((NX, NY, th, dd), F32),
        vmem((2, NH, th, dd), BF16),
        vmem((NX, th, dd), BF16),
        vmem((NY, th, dd), F32),
        vmem((NY, th, dd), F32),
        vmem((NY, th, dd), F32),
        vmem((th, dd), BF16),
        vmem((NY, th, dd), BF16),
        vmem((dd, ff), BF16),
        vmem((dd, ff), BF16),
        vmem((ff, dd), BF16),
        dma((COPIES,)),
        dma((COPIES,)),
        dma((NZ,)),
        dma((NZ,)),
        dma((NZ, NH)),
        dma((NY, NX)),
        dma((NY,)),
        dma((NY,)),
        dma((10,)),
    ]
    results = (
        pl.pallas_call(
            kernel,
            out_shape=out,
            in_specs=[anywhere] * 7,
            out_specs=[pl.BlockSpec(memory_space=vmem)] + [anywhere] * 3,
            scratch_shapes=scratch,
            compiler_params=pltpu.CompilerParams(
                collective_id=0, has_side_effects=True, vmem_limit_bytes=56 * 2**20
            ),
            cost_estimate=pl.CostEstimate(
                flops=12 * nrow * NC * th * dd * ff, bytes_accessed=8 * dd * ff * 2, transcendentals=ncol * tb * ff
            ),
        )(tokens, grad_out, gate_pre, up_pre, w_gate, w_up, w_down)
    )
    return tuple(
        pl.pallas_call(
            copy_kernel,
            out_shape=out,
            in_specs=[anywhere] * 4,
            out_specs=[anywhere] * 4,
            scratch_shapes=[vmem(o.shape, o.dtype) for o in out] + [dma((2, 4))],
            compiler_params=pltpu.CompilerParams(vmem_limit_bytes=60 * 2**20),
        )(*results)
    )


def solution(mesh):
    return jax.shard_map(
        on_device,
        mesh=mesh,
        in_specs=(
            P("row", "col"),
            P("row", "col"),
            P("col", "row"),
            P("col", "row"),
            P("col", "row"),
            P("col", "row"),
            P("row", "col"),
        ),
        out_specs=(P("row", "col"), P("col", "row"), P("col", "row"), P("row", "col")),
        check_vma=False,
    )
```
